32 devices in a mesh: dp: 8 (over z, y), seq: 4 (over x, core).
Axes of the slice: x: 2, y: 2, z: 4, core: 2. Of those that a mesh axis runs over, the one named last changes fastest.
Arguments:
- tokens_in: bfloat16 [32, 512, 768], P('dp', 'seq'), may hold values from -6 to 6
- segment_ids: int32 [32, 512], P('dp'), may hold values from 0 to 3, as said below
- pad_mask: int32 [32, 512], P('dp'), may hold values from 0 to 1, as said below
- out_grad: bfloat16 [32, 512, 768], P('dp', 'seq'), may hold values from -6 to 6
- w_query: float32 [768, 768], P(('dp', 'seq')), may hold values from -0.21875 to 0.21875
- w_key: float32 [768, 768], P(('dp', 'seq')), may hold values from -0.21875 to 0.21875
- w_value: float32 [768, 768], P(('dp', 'seq')), may hold values from -0.21875 to 0.21875
- w_out: float32 [768, 768], P(('dp', 'seq')), may hold values from -0.875 to 0.875
- w_up: float32 [768, 3072], P(('dp', 'seq')), may hold values from -0.21875 to 0.21875
- w_down: float32 [3072, 768], P(('dp', 'seq')), may hold values from -0.109375 to 0.109375
- norm_params: float32 [4, 768], P(None, ('dp', 'seq')), may hold values from -0.5 to 3.2, as said below
- first_query: float32 [768, 768], P(('dp', 'seq')), may hold values from -0.0048828125 to 0.0048828125
- first_key: float32 [768, 768], P(('dp', 'seq')), may hold values from -0.0048828125 to 0.0048828125
- first_value: float32 [768, 768], P(('dp', 'seq')), may hold values from -0.001953125 to 0.001953125
- first_out: float32 [768, 768], P(('dp', 'seq')), may hold values from -0.00048828125 to 0.00048828125
- first_up: float32 [768, 3072], P(('dp', 'seq')), may hold values from -0.00048828125 to 0.00048828125
- first_down: float32 [3072, 768], P(('dp', 'seq')), may hold values from -0.0012207031 to 0.0012207031
- first_norm: float32 [4, 768], P(None, ('dp', 'seq')), may hold values from -0.0024414062 to 0.0024414062
- second_query: float32 [768, 768], P(('dp', 'seq')), may hold values from 5.6073225e-07 to 2.2360907e-06
- second_key: float32 [768, 768], P(('dp', 'seq')), may hold values from 5.6073225e-07 to 2.2360907e-06
- second_value: float32 [768, 768], P(('dp', 'seq')), may hold values from 8.77013e-08 to 3.4973567e-07
- second_out: float32 [768, 768], P(('dp', 'seq')), may hold values from 6.673177e-09 to 2.6611328e-08
- second_up: float32 [768, 3072], P(('dp', 'seq')), may hold values from 6.673177e-09 to 2.6611328e-08
- second_down: float32 [3072, 768], P(('dp', 'seq')), may hold values from 3.6378083e-08 to 1.450687e-07
- second_norm: float32 [4, 768], P(None, ('dp', 'seq')), may hold values from 1.15853766e-07 to 4.6200222e-07
Outputs:
- output: bfloat16 [32, 512, 768], P('dp', 'seq')
- input_grad: bfloat16 [32, 512, 768], P('dp', 'seq')
- grad_norm: float32 [], replicated
- w_query_next: float32 [768, 768], P(('dp', 'seq'))
- w_key_next: float32 [768, 768], P(('dp', 'seq'))
- w_value_next: float32 [768, 768], P(('dp', 'seq'))
- w_out_next: float32 [768, 768], P(('dp', 'seq'))
- w_up_next: float32 [768, 3072], P(('dp', 'seq'))
- w_down_next: float32 [3072, 768], P(('dp', 'seq'))
- norm_params_next: float32 [4, 768], P(None, ('dp', 'seq'))
- first_query_next: float32 [768, 768], P(('dp', 'seq'))
- first_key_next: float32 [768, 768], P(('dp', 'seq'))
- first_value_next: float32 [768, 768], P(('dp', 'seq'))
- first_out_next: float32 [768, 768], P(('dp', 'seq'))
- first_up_next: float32 [768, 3072], P(('dp', 'seq'))
- first_down_next: float32 [3072, 768], P(('dp', 'seq'))
- first_norm_next: float32 [4, 768], P(None, ('dp', 'seq'))
- second_query_next: float32 [768, 768], P(('dp', 'seq'))
- second_key_next: float32 [768, 768], P(('dp', 'seq'))
- second_value_next: float32 [768, 768], P(('dp', 'seq'))
- second_out_next: float32 [768, 768], P(('dp', 'seq'))
- second_up_next: float32 [768, 3072], P(('dp', 'seq'))
- second_down_next: float32 [3072, 768], P(('dp', 'seq'))
- second_norm_next: float32 [4, 768], P(None, ('dp', 'seq'))
The draws below stay inside these ranges and needn't reach their ends.
Inputs may be any that keep to these rules, and one draw needn't show every extreme that they name: `segment_ids`: ids never fall along a row; equal ids form one document. `pad_mask`: in each row the padded positions, at most half of 128 of them, are its last ones. `norm_params`: rows 0 and 2 are gains, rows 1 and 3 shifts.
All inputs are finite; a program needn't handle non-finite values.
Results may differ from the reference program's by a relative error of at most 0.014.
The reference program's roundings to bfloat16 on the way count: a program that leaves them out, or rounds other values in their place, can miss the bound.
Values may be sent and summed in bfloat16 or wider, within the bound.
No kernel may reach another device: no remote copies, remote signals or barrier semaphores. Data moves between devices by JAX's collectives and lax.ppermute only.
A program may use at most 128 MiB of HBM per device.

```python
import math
import jax
import jax.numpy as jnp
from jax import lax

D = 768
H = 12
HD = 64
FF = 3072
LEN = 512
STEP = 7
R_DEV = 4
PIECE = 128
ROWS = 32


def draw_segment_ids(key, part):
    key = jax.random.fold_in(key, 11)
    subkeys = jax.random.split(key, 3)
    opening = jax.random.randint(subkeys[0], (ROWS, 1), 0, PIECE)
    closing = jax.random.randint(subkeys[1], (ROWS, 1), LEN - PIECE + 1, LEN)
    extra_cut = jax.random.randint(subkeys[2], (ROWS, 1), 0, PIECE)
    positions = jnp.arange(LEN)[None, :]
    return (positions >= opening).astype(jnp.int32) + (positions >= closing).astype(jnp.int32) + (positions >= extra_cut).astype(jnp.int32)


def draw_pad_mask(key, part):
    key = jax.random.fold_in(key, 12)
    padded = jax.random.randint(key, (ROWS, 1), 0, PIECE // 2 + 1)
    positions = jnp.arange(LEN)[None, :]
    return (positions < LEN - padded).astype(jnp.int32)


def draw_norm_params(key, part):
    key = jax.random.fold_in(key, 13)
    subkeys = jax.random.split(key, 2)
    ramp_low, ramp_top = (0.6, 1.8)
    across = jnp.arange(D, dtype=jnp.float32) / (D - 1)
    ramp = ramp_low + (ramp_top - ramp_low) * across
    factor = jax.random.uniform(subkeys[0], (4, D), jnp.float32, 0.8, 1.25)
    shifts = jax.random.uniform(subkeys[1], (4, D), jnp.float32, -0.5, 0.5)
    is_gain = (jnp.arange(4) % 2 == 0)[:, None]
    return jnp.where(is_gain, ramp[None, :] * factor, shifts).astype(jnp.float32)


def shard_levels(key, dims, shards, least, top_value):
    level, own = 1.0, jax.random.fold_in(key, 6)
    for dim, parts in shards:
        steps = jnp.exp(jax.random.uniform(jax.random.fold_in(own, dim), (parts,), jnp.float32, least / len(shards), top_value / len(shards)))
        level = level * jnp.repeat(steps, dims[dim] // parts).reshape([-1 if axis == dim else 1 for axis in range(len(dims))])
    return level


def noise(key, dims, deviation, bound, cuts=(), kind=jnp.bfloat16):
    loudness = shard_levels(key, dims, cuts, -0.22, 0.18) if cuts else 1.0
    values = jax.random.normal(key, dims, jnp.float32) * deviation * loudness
    return jnp.minimum(jnp.maximum(values, -bound), bound).astype(kind)


def setup_inputs(seed: int = 0) -> dict:
    key_of = jax.random.split(jax.random.key(seed), 26)
    tokens_in = noise(key_of[0], (ROWS, LEN, D), 1.0, 6.0, ((0, 8), (1, 4)))
    segment_ids = draw_segment_ids(jax.random.fold_in(key_of[25], 71), 0)
    pad_mask = draw_pad_mask(jax.random.fold_in(key_of[25], 71), 0)
    out_grad = noise(key_of[3], (ROWS, LEN, D), 1.0, 6.0, ((0, 8), (1, 4)))
    w_query = noise(key_of[4], (D, D), D ** -0.5, 0.21875, ((0, 32),), jnp.float32)
    w_key = noise(key_of[5], (D, D), D ** -0.5, 0.21875, ((0, 32),), jnp.float32)
    w_value = noise(key_of[6], (D, D), D ** -0.5, 0.21875, ((0, 32),), jnp.float32)
    w_out = noise(key_of[7], (D, D), (D // 16) ** -0.5, 0.875, ((0, 32),), jnp.float32)
    w_up = noise(key_of[8], (D, FF), D ** -0.5, 0.21875, ((0, 32),), jnp.float32)
    w_down = noise(key_of[9], (FF, D), FF ** -0.5, 0.109375, ((0, 32),), jnp.float32)
    norm_params = draw_norm_params(jax.random.fold_in(key_of[25], 71), 0)
    first_query = noise(key_of[11], (D, D), (2.2 / (D * (4 * D + 2 * FF)) ** 0.5), 0.0048828125, ((0, 32),), jnp.float32)
    first_key = noise(key_of[12], (D, D), (2.2 / (D * (4 * D + 2 * FF)) ** 0.5), 0.0048828125, ((0, 32),), jnp.float32)
    first_value = noise(key_of[13], (D, D), (0.87 / (D * (4 * D + 2 * FF)) ** 0.5), 0.001953125, ((0, 32),), jnp.float32)
    first_out = noise(key_of[14], (D, D), (0.24 / (D * (4 * D + 2 * FF)) ** 0.5), 0.00048828125, ((0, 32),), jnp.float32)
    first_up = noise(key_of[15], (D, FF), (0.24 / (D * (4 * D + 2 * FF)) ** 0.5), 0.00048828125, ((0, 32),), jnp.float32)
    first_down = noise(key_of[16], (FF, D), (0.56 / (D * (4 * D + 2 * FF)) ** 0.5), 0.0012207031, ((0, 32),), jnp.float32)
    first_norm = noise(key_of[17], (4, D), (1.0 / (D * (4 * D + 2 * FF)) ** 0.5), 0.0024414062, ((1, 32),), jnp.float32)
    second_query = jnp.clip(jnp.exp(math.log(2.23609072236286e-06) - 1.3832409 * jax.random.uniform(key_of[18], (D, D), jnp.float32) ** shard_levels(key_of[18], (D, D), ((0, 32),), -0.2, 0.2)), 5.607322464129538e-07, 2.23609072236286e-06)
    second_key = jnp.clip(jnp.exp(math.log(2.23609072236286e-06) - 1.3832409 * jax.random.uniform(key_of[19], (D, D), jnp.float32) ** shard_levels(key_of[19], (D, D), ((0, 32),), -0.2, 0.2)), 5.607322464129538e-07, 2.23609072236286e-06)
    second_value = jnp.clip(jnp.exp(math.log(3.497356715342903e-07) - 1.3832409 * jax.random.uniform(key_of[20], (D, D), jnp.float32) ** shard_levels(key_of[20], (D, D), ((0, 32),), -0.2, 0.2)), 8.770130222046646e-08, 3.497356715342903e-07)
    second_out = jnp.clip(jnp.exp(math.log(2.6611328252101885e-08) - 1.3832409 * jax.random.uniform(key_of[21], (D, D), jnp.float32) ** shard_levels(key_of[21], (D, D), ((0, 32),), -0.2, 0.2)), 6.673177121996332e-09, 2.6611328252101885e-08)
    second_up = jnp.clip(jnp.exp(math.log(2.6611328252101885e-08) - 1.3832409 * jax.random.uniform(key_of[22], (D, FF), jnp.float32) ** shard_levels(key_of[22], (D, FF), ((0, 32),), -0.2, 0.2)), 6.673177121996332e-09, 2.6611328252101885e-08)
    second_down = jnp.clip(jnp.exp(math.log(1.4506869661090604e-07) - 1.3832409 * jax.random.uniform(key_of[23], (FF, D), jnp.float32) ** shard_levels(key_of[23], (FF, D), ((0, 32),), -0.2, 0.2)), 3.6378082768351305e-08, 1.4506869661090604e-07)
    second_norm = jnp.clip(jnp.exp(math.log(4.620022195922502e-07) - 1.3832409 * jax.random.uniform(key_of[24], (4, D), jnp.float32) ** shard_levels(key_of[24], (4, D), ((1, 32),), -0.2, 0.2)), 1.1585376569200889e-07, 4.620022195922502e-07)
    return {"tokens_in": tokens_in, "segment_ids": segment_ids, "pad_mask": pad_mask, "out_grad": out_grad, "w_query": w_query, "w_key": w_key, "w_value": w_value, "w_out": w_out, "w_up": w_up, "w_down": w_down, "norm_params": norm_params, "first_query": first_query, "first_key": first_key, "first_value": first_value, "first_out": first_out, "first_up": first_up, "first_down": first_down, "first_norm": first_norm, "second_query": second_query, "second_key": second_key, "second_value": second_value, "second_out": second_out, "second_up": second_up, "second_down": second_down, "second_norm": second_norm}


precise = lax.Precision.HIGHEST
clip_limit = 1.0

@jax.custom_vjp
def low(v):
    return lax.optimization_barrier(v.astype(jnp.bfloat16)).astype(jnp.float32)

@jax.custom_vjp
def low_back(v):
    return v

def low_keep(v):
    return (low(v), None)

def low_pass(kept, grad):
    return (grad,)

def back_keep(v):
    return (v, None)

def back_low(kept, grad):
    return (low(grad),)
low.defvjp(low_keep, low_pass)
low_back.defvjp(back_keep, back_low)

def layer_norm(values, gain, shift):
    center = values - lax.optimization_barrier(jnp.mean(values, axis=-1, keepdims=True))
    variance = lax.optimization_barrier(jnp.mean(center * center, axis=-1, keepdims=True))
    return center * lax.rsqrt(variance + 1e-05) * gain + shift

def project(acts, matrix):
    return jnp.einsum('rtd,de->rte', acts, matrix, precision=precise)

def block_forward(tokens, w_query, w_key, w_value, w_out, w_up, w_down, norm_params, segment_ids, pad_mask):
    gains = low(norm_params)
    row_count = tokens.shape[0]
    attn_input = low(layer_norm(tokens, gains[0], gains[1]))

    def heads_of(matrix):
        return low(low_back(project(attn_input, low(matrix)))).reshape(row_count, LEN, H, HD)
    queries = heads_of(w_query)
    key_heads = heads_of(w_key)
    value_heads = heads_of(w_value)
    same_doc = segment_ids[:, :, None] == segment_ids[:, None, :]
    on_diag = jnp.eye(LEN, dtype=bool)[None]
    permit = same_doc & ((pad_mask[:, None, :] == 1) | on_diag)
    raw = jnp.einsum('rqhd,rkhd->rhqk', queries, key_heads, precision=precise) * 0.125
    scores = jnp.where(permit[:, None], low_back(raw), -1e+30)
    soft = jax.nn.softmax(scores, axis=-1)
    mixed_heads = jnp.einsum('rhqk,rkhd->rqhd', low(soft), value_heads, precision=precise)
    attended = low(low_back(mixed_heads.reshape(row_count, LEN, D)))
    mid_stream = tokens + low_back(project(attended, low(w_out)))
    mlp_input = low(layer_norm(mid_stream, gains[2], gains[3]))
    up_proj = low_back(project(mlp_input, low(w_up)))
    hidden = low(jax.nn.gelu(up_proj, approximate=False))
    return mid_stream + low_back(project(hidden, low(w_down)))

def adam_update(weight, gradient, moment_one, moment_two, step_rate, decay_rate):
    one_next = 0.5 * moment_one + 0.5 * gradient
    two_next = 0.55 * moment_two + 0.45 * gradient * gradient
    corrected = one_next / (1.0 - 0.5 ** STEP)
    root_term = jnp.sqrt(two_next / (1.0 - 0.55 ** STEP)) + 1e-08
    return (weight - step_rate * (corrected / root_term + decay_rate * weight), one_next, two_next)

def reference(tokens_in, segment_ids, pad_mask, out_grad, w_query, w_key, w_value, w_out, w_up, w_down, norm_params, first_query, first_key, first_value, first_out, first_up, first_down, first_norm, second_query, second_key, second_value, second_out, second_up, second_down, second_norm):
    weights = (w_query, w_key, w_value, w_out, w_up, w_down, norm_params)
    block_rows = R_DEV
    block_count = ROWS // block_rows

    def in_blocks(array):
        return array.reshape((block_count, block_rows) + array.shape[1:])
    tokens = in_blocks(tokens_in.astype(jnp.float32))
    cotangent = in_blocks(out_grad.astype(jnp.float32))

    def one_block(carry, pieces):
        tok_block, cot_block, seg_block, pad_block = pieces

        def forward_fn(tok, *params):
            return block_forward(tok, *params, seg_block, pad_block)
        result, pull = jax.vjp(forward_fn, tok_block, *weights)
        grads = pull(cot_block)
        carry_next = tuple((acc + piece_grad for acc, piece_grad in zip(carry, grads[1:])))
        return (carry_next, (result.astype(jnp.bfloat16), grads[0].astype(jnp.bfloat16)))
    zeros = tuple((jnp.zeros_like(weight) for weight in weights))
    sums, (out_blocks, grad_blocks) = lax.scan(one_block, zeros, (tokens, cotangent, in_blocks(segment_ids), in_blocks(pad_mask)))
    output = out_blocks.reshape(ROWS, LEN, D)
    input_grad = grad_blocks.reshape(ROWS, LEN, D)
    total_sq = sum((jnp.sum(piece_grad * piece_grad) for piece_grad in sums))
    grad_norm = jnp.sqrt(total_sq)
    factor = jnp.minimum(1.0, clip_limit / (grad_norm + 1e-06))
    rates = (D ** (-0.5), D ** (-0.5), D ** (-0.5), 4.0 * D ** (-0.5), D ** (-0.5), FF ** (-0.5), 0.2)
    decays = (0.01, 0.01, 0.01, 0.01, 0.01, 0.01, 0.0)
    firsts = (first_query, first_key, first_value, first_out, first_up, first_down, first_norm)
    seconds = (second_query, second_key, second_value, second_out, second_up, second_down, second_norm)
    updated = [adam_update(weights[index], factor * sums[index], firsts[index], seconds[index], rates[index], decays[index]) for index in range(7)]
    return (output, input_grad, grad_norm, updated[0][0], updated[1][0], updated[2][0], updated[3][0], updated[4][0], updated[5][0], updated[6][0], updated[0][1], updated[1][1], updated[2][1], updated[3][1], updated[4][1], updated[5][1], updated[6][1], updated[0][2], updated[1][2], updated[2][2], updated[3][2], updated[4][2], updated[5][2], updated[6][2])
```

```python
from functools import partial

import jax
import jax.numpy as jnp
from jax import lax
from jax.experimental import pallas as pl
from jax.experimental.pallas import tpu as pltpu
from jax.sharding import PartitionSpec as P

D = 768
H = 12
HD = 64
FF = 3072
STEP = 7
HALF = D // 2
PAIRS = H // 2
BLOCKS = 4
BF = jnp.bfloat16
F32 = jnp.float32
AXES = ("dp", "seq")
clip_limit = 1.0
MIB = 2**20

VM = pl.BlockSpec(memory_space=pltpu.VMEM)
ANY = pl.BlockSpec(memory_space=pl.ANY)


def dot(left, right, left_dim, right_dim):
    return lax.dot_general(
        left, right, (((left_dim,), (right_dim,)), ((), ())), preferred_element_type=F32
    )


def shape(dims, kind):
    return jax.ShapeDtypeStruct(dims, kind)


class Plan:
    def __init__(self, mesh, rows_each):
        self.dp = mesh.shape["dp"]
        self.seq = mesh.shape["seq"]
        self.count = self.dp * self.seq
        self.fast = (
            self.seq == 4
            and self.dp % 2 == 0
            and BLOCKS * 8 == self.count
            and (2 * D // self.count) % 16 == 0
        )
        self.nz = self.dp // 2
        self.rows = D // self.count
        self.far = FF // self.count
        both = range(self.count)
        self.core = [(d, d ^ 1) for d in both]
        self.first = [(d, d ^ (2 if d % 2 == 0 else 4)) for d in both]
        self.second = [(d, d ^ (4 if d % 2 == 0 else 2)) for d in both]
        self.groups = [list(range(low, self.dp, 2)) for low in range(2)]

    def wide(self, rows, columns):
        if self.fast:
            return (2, self.nz, 4, 2 * rows // self.count, columns)
        return (2, BLOCKS, 1, rows // BLOCKS, columns)

    def parts(self):
        return 8 if self.fast else 1

    def grads(self, rows, columns):
        if self.fast:
            half = shape((4 * self.nz, rows // self.count, columns), BF)
            return [half, half]
        return [shape((rows, columns), BF)]


def place():
    seq = lax.axis_index("seq")
    return seq & 1, seq >> 1, lax.axis_index("dp") & 1


def start_parts(plan, parts, whole, sems, pieces):
    if not plan.fast:
        for index, (first, size) in enumerate(pieces):
            columns = pl.ds(first, size)
            pltpu.make_async_copy(
                parts[0].at[..., columns], whole.at[..., columns], sems.at[index]
            ).start()
        return
    core, mine_x, mine_y = place()
    for index, (first, size) in enumerate(pieces):
        columns = pl.ds(first, size)
        for number, part in enumerate(parts):
            owner = core if number < 4 else 1 - core
            one, two = (number >> 1) & 1, number & 1
            off_x = jnp.where(owner == 0, one, two)
            off_y = jnp.where(owner == 0, two, one)
            spot = (mine_y ^ off_y) * 2 + (mine_x ^ off_x)
            pltpu.make_async_copy(
                part.at[:, :, columns], whole.at[owner, :, spot, :, columns], sems.at[index]
            ).start()


def wait_part(whole, sems, index, piece):
    columns = pl.ds(*piece)
    view = whole.at[..., columns]
    pltpu.make_async_copy(view, view, sems.at[index]).wait()


def flat(value):
    return value.reshape(-1, value.shape[-1])


def store_grad(plan, tile, outs, rows, first_row, columns):
    if not plan.fast:
        outs[0][pl.ds(first_row, tile.shape[0]), columns] = tile.astype(BF)
        return
    keep, send = outs
    core, mine_x, mine_y = place()
    step = rows // plan.count

    def spot(pair, owner):
        off_x = (pair & 1) ^ mine_x
        off_y = ((pair >> 1) & 1) ^ mine_y
        one = jnp.where(owner == 0, off_x, off_y)
        return (one * 2 + (off_x + off_y - one)) * plan.nz + (pair >> 2)

    for local in range(tile.shape[0] // (2 * step)):
        pair = first_row // (2 * step) + local
        low = tile[2 * step * local : 2 * step * local + step]
        high = tile[2 * step * local + step : 2 * step * (local + 1)]
        keep[spot(pair, core), :, columns] = jnp.where(core == 0, low, high).astype(BF)
        send[spot(pair, 1 - core), :, columns] = jnp.where(core == 0, high, low).astype(BF)


def call(body, name, ins, outs, scratch, limit, flops, args):
    moved = sum(a.size * a.dtype.itemsize for a in args) + sum(
        o.size * o.dtype.itemsize for o in outs
    )
    return pl.pallas_call(
        body,
        out_shape=outs,
        in_specs=ins,
        out_specs=[VM] * len(outs),
        scratch_shapes=scratch,
        compiler_params=pltpu.CompilerParams(vmem_limit_bytes=limit * MIB),
        cost_estimate=pl.CostEstimate(flops=flops, bytes_accessed=moved, transcendentals=0),
        name=name,
    )(*args)


def norm_of(values):
    center = values - jnp.mean(values, axis=-1, keepdims=True)
    inverse = lax.rsqrt(jnp.mean(center * center, axis=-1, keepdims=True) + 1e-05)
    return center * inverse, inverse


def norm_back(upstream, normed, inverse, gain):
    scaled = upstream * gain
    return inverse * (
        scaled
        - jnp.mean(scaled, axis=-1, keepdims=True)
        - normed * jnp.mean(scaled * normed, axis=-1, keepdims=True)
    )


def fill_bias(bias, seg, pad):
    length = bias.shape[0]
    code = (2 * seg + pad).astype(F32)
    wanted = (2 * seg + 1).astype(F32)
    coded = jnp.broadcast_to(code, (length, length)).T
    rows = lax.broadcasted_iota(jnp.int32, (length, length), 0)
    cols = lax.broadcasted_iota(jnp.int32, (length, length), 1)
    bias[...] = jnp.where((coded == wanted) | (rows == cols), 0.0, -1e30)


def halves_of(values):
    lane = lax.broadcasted_iota(jnp.int32, values.shape, 1)
    zero = jnp.zeros_like(values)
    return jnp.where(lane < HD, values, zero), jnp.where(lane < HD, zero, values)


def attend(plan, tokens, seg, pad, norms, parts):
    length = tokens.shape[0]
    pieces = [(m * HALF, HALF) for m in range(3)]

    def body(x_ref, seg_ref, pad_ref, n_ref, *rest):
        part_refs, rest = rest[: plan.parts()], rest[plan.parts() :]
        h_ref, q_ref, k_ref, v_ref, at_ref, a_ref, l_ref, whole, bias, sems = rest
        start_parts(plan, part_refs, whole, sems, pieces)

        @pl.loop(0, length // 128)
        def _(i):
            rows = pl.ds(pl.multiple_of(i * 128, 128), 128)
            normed, _ = norm_of(x_ref[rows, :].astype(F32))
            h_ref[rows, :] = (normed * n_ref[0:1, :] + n_ref[1:2, :]).astype(BF)

        fill_bias(bias, seg_ref[...], pad_ref[...])
        for m, (out, scale) in enumerate(((q_ref, 0.125), (k_ref, 1.0), (v_ref, 1.0))):
            wait_part(whole, sems, m, pieces[m])
            for h in range(2):
                weight = flat(whole[h, :, :, :, m * HALF : (m + 1) * HALF])
                out[:, h * HALF : (h + 1) * HALF] = (dot(h_ref[...], weight, 1, 0) * scale).astype(BF)

        @pl.loop(0, PAIRS)
        def _(p):
            cols = pl.ds(pl.multiple_of(p * 128, 128), 128)
            keys = k_ref[:, cols]
            turned = v_ref[:, cols].T
            for half, query in enumerate(halves_of(q_ref[:, cols])):
                scores = dot(keys, query, 1, 1) + bias[...]
                top = jnp.max(scores, axis=0, keepdims=True)
                lifted = jnp.exp(scores - top)
                total = jnp.sum(lifted, axis=0, keepdims=True)
                soft = (lifted * (1.0 / total)).astype(BF)
                mixed = dot(turned[half * HD : (half + 1) * HD], soft, 1, 0)
                at_ref[pl.ds(pl.multiple_of(p * 128 + half * HD, HD), HD), :] = mixed.astype(BF)
                l_ref[pl.ds(2 * p + half, 1), :] = top + jnp.log(total)
            a_ref[:, cols] = at_ref[pl.ds(pl.multiple_of(p * 128, 128), 128), :].T

    act = shape((length, D), BF)
    return call(
        body, "attend", [VM] * 4 + [ANY] * plan.parts(),
        [act, act, act, act, shape((D, length), BF), act, shape((H, length), F32)],
        [pltpu.VMEM(plan.wide(D, 3 * HALF), BF), pltpu.VMEM((length, length), F32), pltpu.SemaphoreType.DMA((3,))],
        40, 2 * length * (3 * D * D + 2 * length * D), [tokens, seg, pad, norms, *parts],
    )


def widen(plan, tokens, mixed, cot, norms, parts):
    length = tokens.shape[0]
    pieces = [(0, HALF), (HALF, D), (HALF + D, D)]

    def body(x_ref, a_ref, g_ref, n_ref, *rest):
        part_refs, rest = rest[: plan.parts()], rest[plan.parts() :]
        m_ref, h_ref, z_ref, s_ref, *rest = rest
        grads, (whole, sems) = rest[:-2], rest[-2:]
        start_parts(plan, part_refs, whole, sems, pieces)
        wait_part(whole, sems, 0, pieces[0])
        for h in range(2):
            cols = slice(h * HALF, (h + 1) * HALF)
            weight = flat(whole[h, :, :, :, 0:HALF])
            m_ref[:, cols] = x_ref[:, cols].astype(F32) + dot(a_ref[...], weight, 1, 0)

        @pl.loop(0, length // 128)
        def _(i):
            rows = pl.ds(pl.multiple_of(i * 128, 128), 128)
            normed, _ = norm_of(m_ref[rows, :])
            h_ref[rows, :] = (normed * n_ref[2:3, :] + n_ref[3:4, :]).astype(BF)

        for part in range(2):
            wait_part(whole, sems, 1 + part, pieces[1 + part])
            for h in range(2):
                block = h * 2 + part
                cols = slice(block * D, (block + 1) * D)
                weight = flat(whole[h, :, :, :, HALF + part * D : HALF + (part + 1) * D])
                up = dot(h_ref[...], weight, 1, 0)
                bell = 0.5 + 0.5 * lax.erf(up * 0.7071067811865476)
                z_ref[:, cols] = (up * bell).astype(BF)
                s_ref[:, cols] = bell + up * (jnp.exp(-0.5 * up * up) * 0.3989422804014327)
                tile = dot(z_ref[:, cols], g_ref[...], 0, 0)
                store_grad(plan, tile, grads, FF, block * D, slice(None))

    act = shape((length, D), BF)
    return call(
        body, "widen", [VM] * 4 + [ANY] * plan.parts(),
        [shape((length, D), F32), act, shape((length, FF), BF), shape((length, FF), F32), *plan.grads(FF, D)],
        [pltpu.VMEM(plan.wide(D, 5 * HALF), BF), pltpu.SemaphoreType.DMA((3,))],
        56, 2 * length * (D * D + 2 * D * FF), [tokens, mixed, cot, norms, *parts],
    )


def narrow(plan, mid, low, hidden, slope, cot, parts_up, parts_down):
    length = mid.shape[0]
    up_pieces = [(HALF, 2 * D)]
    down_pieces = [(0, HALF)]

    def body(m_ref, h_ref, z_ref, s_ref, g_ref, *rest):
        n = plan.parts()
        ups, downs, rest = rest[:n], rest[n : 2 * n], rest[2 * n :]
        o_ref, b_ref, *rest = rest
        grads, (acc, whole_up, whole_down, sems) = rest[:-4], rest[-4:]
        start_parts(plan, downs, whole_down, sems.at[pl.ds(0, 1)], down_pieces)
        start_parts(plan, ups, whole_up, sems.at[pl.ds(1, 1)], up_pieces)
        wait_part(whole_down, sems, 0, down_pieces[0])
        wait_part(whole_up, sems, 1, up_pieces[0])
        for block in range(BLOCKS):
            cols = slice(block * D, (block + 1) * D)
            z = z_ref[:, cols]
            for h in range(2):
                half = slice(h * HALF, (h + 1) * HALF)
                gain = dot(z, flat(whole_down[h, block]), 1, 0)
                acc[:, half] = gain + (m_ref[:, half] if block == 0 else acc[:, half])
            back = dot(g_ref[:, 0:HALF], flat(whole_down[0, block]), 1, 1)
            back += dot(g_ref[:, HALF:D], flat(whole_down[1, block]), 1, 1)
            du = (back * s_ref[:, cols]).astype(BF)
            first = HALF + (block % 2) * D
            lower = dot(du, flat(whole_up[block // 2, :, :, :, first : first + D]), 1, 1)
            b_ref[...] = lower if block == 0 else b_ref[...] + lower
            tile = dot(h_ref[...], du, 0, 0)
            store_grad(plan, tile, grads, D, 0, cols)
        o_ref[...] = acc[...].astype(BF)

    return call(
        body, "narrow", [VM] * 5 + [ANY] * (2 * plan.parts()),
        [shape((length, D), BF), shape((length, D), F32), *plan.grads(D, FF)],
        [
            pltpu.VMEM((length, D), F32),
            pltpu.VMEM(plan.wide(D, 5 * HALF), BF),
            pltpu.VMEM(plan.wide(FF, HALF), BF),
            pltpu.SemaphoreType.DMA((2,)),
        ],
        58, 2 * length * 4 * D * FF, [mid, low, hidden, slope, cot, *parts_up, *parts_down],
    )


def turn(plan, mid, back, cot, norms, mixed_t, parts):
    length = mid.shape[0]
    pieces = [(0, HALF)]

    def body(m_ref, b_ref, g_ref, n_ref, at_ref, *rest):
        part_refs, rest = rest[: plan.parts()], rest[plan.parts() :]
        x_ref, d_ref, s_ref, *rest = rest
        grads, (low, whole, sems) = rest[:-3], rest[-3:]
        start_parts(plan, part_refs, whole, sems, pieces)
        s_ref[...] = jnp.zeros_like(s_ref)

        @pl.loop(0, length // 128)
        def _(i):
            rows = pl.ds(pl.multiple_of(i * 128, 128), 128)
            normed, inverse = norm_of(m_ref[rows, :])
            upstream = b_ref[rows, :]
            total = g_ref[rows, :].astype(F32) + norm_back(upstream, normed, inverse, n_ref[2:3, :])
            x_ref[rows, :] = total
            low[rows, :] = total.astype(BF)
            s_ref[0:1, :] += jnp.sum(upstream * normed, axis=0, keepdims=True)
            s_ref[1:2, :] += jnp.sum(upstream, axis=0, keepdims=True)

        wait_part(whole, sems, 0, pieces[0])
        back_a = dot(low[:, 0:HALF], flat(whole[0, :, :, :, 0:HALF]), 1, 1)
        back_a += dot(low[:, HALF:D], flat(whole[1, :, :, :, 0:HALF]), 1, 1)
        d_ref[...] = back_a.astype(BF)
        store_grad(plan, dot(at_ref[...], low[...], 1, 0), grads, D, 0, slice(None))

    return call(
        body, "turn", [VM] * 5 + [ANY] * plan.parts(),
        [shape((length, D), F32), shape((length, D), BF), shape((2, D), F32), *plan.grads(D, D)],
        [pltpu.VMEM((length, D), BF), pltpu.VMEM(plan.wide(D, 5 * HALF), BF), pltpu.SemaphoreType.DMA((1,))],
        40, 2 * length * 2 * D * D, [mid, back, cot, norms, mixed_t, *parts],
    )


def attend_back(plan, low, query, key, value, lse, cot, seg, pad):
    length = low.shape[0]

    def body(h_ref, q_ref, k_ref, v_ref, l_ref, c_ref, seg_ref, pad_ref, d_ref, *rest):
        grads, (bias,) = rest[:-1], rest[-1:]
        fill_bias(bias, seg_ref[...], pad_ref[...])

        @pl.loop(0, PAIRS)
        def _(p):
            first = pl.multiple_of(p * 128, 128)
            cols = pl.ds(first, 128)
            keys, values = k_ref[:, cols], v_ref[:, cols]
            turned = keys.T
            queries, cots = halves_of(q_ref[:, cols]), halves_of(c_ref[:, cols])
            dv = dk = None
            dqs = []
            for half in range(2):
                scores = dot(keys, queries[half], 1, 1) + bias[...]
                soft = jnp.exp(scores - l_ref[pl.ds(2 * p + half, 1), :])
                gain = dot(soft.astype(BF), cots[half], 1, 0)
                dv = gain if dv is None else dv + gain
                dp = dot(values, cots[half], 1, 1)
                share = jnp.sum(soft * dp, axis=0, keepdims=True)
                ds = (soft * (dp - share)).astype(BF)
                gain = dot(ds, queries[half], 1, 0)
                dk = gain if dk is None else dk + gain
                dqs.append(dot(turned[half * HD : (half + 1) * HD], ds, 1, 0) * 0.125)
            d_ref[:, cols] = jnp.concatenate(dqs, axis=0).T.astype(BF)
            d_ref[:, pl.ds(first + D, 128)] = dk.astype(BF)
            d_ref[:, pl.ds(first + 2 * D, 128)] = dv.astype(BF)

        for m in range(3):
            cols = slice(m * D, (m + 1) * D)
            store_grad(plan, dot(h_ref[...], d_ref[:, cols], 0, 0), grads, D, 0, cols)

    return call(
        body, "attend_back", [VM] * 8,
        [shape((length, 3 * D), BF), *plan.grads(D, 3 * D)],
        [pltpu.VMEM((length, length), F32)],
        40, 2 * length * (3 * D * D + 5 * length * D), [low, query, key, value, lse, cot, seg, pad],
    )


def finish_tokens(plan, tokens, spread, mid_cot, norms, parts):
    length = tokens.shape[0]
    pieces = [(0, 3 * HALF)]

    def body(x_ref, d_ref, c_ref, n_ref, *rest):
        part_refs, rest = rest[: plan.parts()], rest[plan.parts() :]
        o_ref, s_ref, back, whole, sems = rest
        start_parts(plan, part_refs, whole, sems, pieces)
        s_ref[...] = jnp.zeros_like(s_ref)
        wait_part(whole, sems, 0, pieces[0])
        total = None
        for m in range(3):
            for h in range(2):
                first = m * D + h * HALF
                weight = flat(whole[h, :, :, :, m * HALF : (m + 1) * HALF])
                gain = dot(d_ref[:, first : first + HALF], weight, 1, 1)
                total = gain if total is None else total + gain
        back[...] = total

        @pl.loop(0, length // 128)
        def _(i):
            rows = pl.ds(pl.multiple_of(i * 128, 128), 128)
            normed, inverse = norm_of(x_ref[rows, :].astype(F32))
            upstream = back[rows, :]
            o_ref[rows, :] = (
                c_ref[rows, :] + norm_back(upstream, normed, inverse, n_ref[0:1, :])
            ).astype(BF)
            s_ref[0:1, :] += jnp.sum(upstream * normed, axis=0, keepdims=True)
            s_ref[1:2, :] += jnp.sum(upstream, axis=0, keepdims=True)

    return call(
        body, "finish_tokens", [VM] * 4 + [ANY] * plan.parts(),
        [shape((length, D), BF), shape((2, D), F32)],
        [pltpu.VMEM((length, D), F32), pltpu.VMEM(plan.wide(D, 3 * HALF), BF), pltpu.SemaphoreType.DMA((1,))],
        40, 2 * length * 3 * D * D, [tokens, spread, mid_cot, norms, *parts],
    )


def update(grads, squares, masters, firsts, seconds):
    rates = [D**-0.5] * 3 + [4.0 * D**-0.5, D**-0.5, FF**-0.5, 0.2]
    decays = [0.01] * 6 + [0.0]
    count = len(masters)

    def body(*refs):
        grad_refs, sq_ref = refs[:5], refs[5]
        w_refs, m_refs, s_refs = (refs[6 + count * i : 6 + count * (i + 1)] for i in range(3))
        outs = refs[6 + 3 * count :]
        norm = jnp.sqrt(jnp.sum(sq_ref[...], axis=0, keepdims=True))
        outs[0][...] = norm
        factor = jnp.minimum(1.0, clip_limit / (norm + 1e-06))[:, 0:1]
        for i in range(count):
            if i < 3:
                grad = grad_refs[0][:, i * D : (i + 1) * D]
            else:
                grad = grad_refs[i - 2][...]
            clipped = factor * grad
            one = 0.5 * m_refs[i][...] + 0.5 * clipped
            two = 0.55 * s_refs[i][...] + 0.45 * clipped * clipped
            root = jnp.sqrt(two * (1.0 / (1.0 - 0.55**STEP))) + 1e-08
            weight = w_refs[i][...]
            step = (one * (1.0 / (1.0 - 0.5**STEP))) / root + decays[i] * weight
            outs[1 + i][...] = weight - rates[i] * step
            outs[1 + count + i][...] = one
            outs[1 + 2 * count + i][...] = two

    args = [*grads, squares, *masters, *firsts, *seconds]
    like = [shape(w.shape, F32) for w in masters]
    return call(
        body, "update", [VM] * len(args), [shape((1, squares.shape[1]), F32), *like * 3], [], 40, 10**7, args
    )


def side_by_side(matrices):
    split = [w.reshape(w.shape[0], 2, -1) for w in matrices]
    return jnp.concatenate(split, axis=2).transpose(1, 0, 2).astype(BF)


def gather(plan, matrices):
    halves = side_by_side(matrices)
    if not plan.fast:
        full = lax.all_gather(halves, AXES, axis=1, tiled=True)
        return [full.reshape(2, BLOCKS, 1, -1, full.shape[-1])]
    core = lax.axis_index("seq") & 1
    mine = lax.dynamic_index_in_dim(halves, core, 0, keepdims=False)
    other = lax.dynamic_index_in_dim(halves, 1 - core, 0, keepdims=False)
    got = lax.ppermute(other, AXES, plan.core)
    block = jnp.where(core == 0, jnp.concatenate([mine, got]), jnp.concatenate([got, mine]))
    spread = jnp.broadcast_to(block[None], (plan.nz, *block.shape))
    near = lax.all_to_all(spread, "dp", 0, 0, axis_index_groups=plan.groups, tiled=True)
    beside = lax.ppermute(near, AXES, plan.second)
    across = [near, beside, lax.ppermute(near, AXES, plan.first), lax.ppermute(beside, AXES, plan.first)]
    return across + [lax.ppermute(part, AXES, plan.core) for part in across]


def add(one, two):
    return one.astype(F32) + two.astype(F32)


def reduce(plan, outs):
    if not plan.fast:
        return lax.psum_scatter(outs[0].astype(F32), AXES, scatter_dimension=0, tiled=True)
    keep, send = outs
    nz = plan.nz
    got = lax.ppermute(send, AXES, plan.core)
    for perm, size in ((plan.first, 2 * nz), (plan.second, nz)):
        send = add(keep[size:], got[size:]).astype(BF)
        keep = add(keep[:size], got[:size]).astype(BF)
        got = lax.ppermute(send, AXES, perm)
    block = add(keep, got).astype(BF)
    blocks = lax.all_to_all(block, "dp", 0, 0, axis_index_groups=plan.groups, tiled=True)
    return jnp.sum(blocks.astype(F32), axis=0)


def everywhere(plan, values):
    spread = jnp.broadcast_to(values[None], (plan.count, *values.shape))
    return lax.all_to_all(spread, AXES, 0, 0, tiled=True)


def on_device(plan, *args):
    tokens_in, segment_ids, pad_mask, out_grad = args[:4]
    masters, firsts, seconds = args[4:11], args[11:18], args[18:25]
    w_query, w_key, w_value, w_out, w_up, w_down, norm_params = masters
    each, piece, _ = tokens_in.shape
    length = each // plan.seq * plan.seq * piece

    def to_rows(values):
        return lax.all_to_all(values, "seq", 0, 0, tiled=True).reshape(length, D)

    def to_pieces(values):
        return lax.all_to_all(values.reshape(each, piece, D), "seq", 0, 0, tiled=True)

    tokens = to_rows(tokens_in)
    parts_qkv = gather(plan, [w_query, w_key, w_value])
    small = everywhere(plan, norm_params.astype(BF))
    norms = small.transpose(1, 0, 2).reshape(4, D).astype(F32)
    parts_up = gather(plan, [w_out, w_up])
    cot = to_rows(out_grad)
    parts_down = gather(plan, [w_down])
    row = lax.axis_index("seq")
    seg = lax.dynamic_slice_in_dim(segment_ids, row, 1, 0)
    pad = lax.dynamic_slice_in_dim(pad_mask, row, 1, 0)

    low_one, query, key, value, mixed_t, mixed, lse = attend(plan, tokens, seg, pad, norms, parts_qkv)
    mid, low_two, hidden, slope, *grads_down = widen(plan, tokens, mixed, cot, norms, parts_up)
    grad_down = reduce(plan, grads_down)
    result, back, *grads_up = narrow(plan, mid, low_two, hidden, slope, cot, parts_up, parts_down)
    output = to_pieces(result)
    grad_up = reduce(plan, grads_up)
    mid_cot, mixed_cot, sums_two, *grads_out = turn(plan, mid, back, cot, norms, mixed_t, parts_up)
    grad_out = reduce(plan, grads_out)
    spread, *grads_qkv = attend_back(plan, low_one, query, key, value, lse, mixed_cot, seg, pad)
    grad_qkv = reduce(plan, grads_qkv)
    stream, sums_one = finish_tokens(plan, tokens, spread, mid_cot, norms, parts_qkv)
    input_grad = to_pieces(stream)
    sums = jnp.concatenate([sums_one, sums_two], axis=0)
    slices = sums.reshape(4, plan.count, -1).transpose(1, 0, 2)
    grad_norms = jnp.sum(lax.all_to_all(slices, AXES, 0, 0, tiled=True), axis=0)

    grads = [grad_qkv, grad_out, grad_up, grad_down, grad_norms]
    local = sum(jnp.sum(g * g) for g in grads)
    squares = everywhere(plan, jnp.broadcast_to(local, (1, 128))).reshape(plan.count, 128)
    norm, *updated = update(grads, squares, masters, firsts, seconds)
    return (output, input_grad, norm[0, 0], *updated)


def solution(mesh):
    plan = Plan(mesh, None)
    rows = P(AXES, None)
    weights = (*[rows] * 6, P(None, AXES))
    tokens = P("dp", "seq", None)
    return jax.shard_map(
        partial(on_device, plan),
        mesh=mesh,
        in_specs=(tokens, P("dp", None), P("dp", None), tokens, *weights * 3),
        out_specs=(tokens, tokens, P(), *weights * 3),
        check_vma=False,
    )
```

```python
from functools import partial

import jax
import jax.numpy as jnp
from jax import lax
from jax.experimental import pallas as pl
from jax.experimental.pallas import tpu as pltpu
from jax.sharding import PartitionSpec as P

D = 768
H = 12
HD = 64
FF = 3072
STEP = 7
HALF = D // 2
PAIRS = H // 2
BLOCKS = 4
BF = jnp.bfloat16
F32 = jnp.float32
AXES = ("dp", "seq")
clip_limit = 1.0
MIB = 2**20

VM = pl.BlockSpec(memory_space=pltpu.VMEM)
ANY = pl.BlockSpec(memory_space=pl.ANY)
FAR = pl.BlockSpec(memory_space=pltpu.HBM)


def dot(left, right, left_dim, right_dim):
    return lax.dot_general(
        left, right, (((left_dim,), (right_dim,)), ((), ())), preferred_element_type=F32
    )


def shape(dims, kind):
    return jax.ShapeDtypeStruct(dims, kind)


class Plan:
    def __init__(self, mesh, rows_each):
        self.dp = mesh.shape["dp"]
        self.seq = mesh.shape["seq"]
        self.count = self.dp * self.seq
        self.fast = (
            self.seq == 4
            and self.dp % 2 == 0
            and BLOCKS * 8 == self.count
            and (2 * D // self.count) % 16 == 0
        )
        self.nz = self.dp // 2
        self.rows = D // self.count
        self.far = FF // self.count
        both = range(self.count)
        self.core = [(d, d ^ 1) for d in both]
        self.first = [(d, d ^ (2 if d % 2 == 0 else 4)) for d in both]
        self.second = [(d, d ^ (4 if d % 2 == 0 else 2)) for d in both]
        self.groups = [list(range(low, self.dp, 2)) for low in range(2)]

    def wide(self, rows, columns):
        if self.fast:
            return (2, self.nz, 4, 2 * rows // self.count, columns)
        return (2, BLOCKS, 1, rows // BLOCKS, columns)

    def parts(self):
        return 8 if self.fast else 1

    def grads(self, rows, columns):
        if self.fast:
            half = shape((4 * self.nz, rows // self.count, columns), BF)
            return [half, half]
        return [shape((rows, columns), BF)]

    def outs(self):
        return 2 if self.fast else 1

    def bands(self):
        return self.seq if self.fast else 1

    def band_shapes(self, length):
        return [shape((length // self.bands(), D), BF)] * self.bands()


def place():
    seq = lax.axis_index("seq")
    return seq & 1, seq >> 1, lax.axis_index("dp") & 1


def start_parts(plan, parts, whole, sems, pieces, blocks=None):
    blocks = slice(None) if blocks is None else pl.ds(blocks[0], len(blocks))
    if len(parts) == 1:
        for index, (first, size) in enumerate(pieces):
            columns = pl.ds(first, size)
            pltpu.make_async_copy(
                parts[0].at[:, blocks, :, :, columns], whole.at[..., columns], sems.at[index]
            ).start()
        return
    core, mine_x, mine_y = place()
    for index, (first, size) in enumerate(pieces):
        columns = pl.ds(first, size)
        for number, part in enumerate(parts):
            owner = core if number < 4 else 1 - core
            one, two = (number >> 1) & 1, number & 1
            off_x = jnp.where(owner == 0, one, two)
            off_y = jnp.where(owner == 0, two, one)
            spot = (mine_y ^ off_y) * 2 + (mine_x ^ off_x)
            pltpu.make_async_copy(
                part.at[blocks, :, columns], whole.at[owner, :, spot, :, columns], sems.at[index]
            ).start()


def wait_part(whole, sems, index, piece):
    columns = pl.ds(*piece)
    view = whole.at[..., columns]
    pltpu.make_async_copy(view, view, sems.at[index]).wait()


def band(plan, number, length):
    if plan.bands() == 1:
        return pl.ds(0, length)
    size = length // plan.bands()
    return pl.ds(pl.multiple_of((lax.axis_index("seq") ^ number) * size, size), size)


def load_bands(plan, refs, whole, sems):
    copies = []
    for number, ref in enumerate(refs):
        source = ref.at[lax.axis_index("seq")] if number == 0 and plan.bands() > 1 else ref
        target = whole.at[band(plan, number, whole.shape[0]), :]
        copies.append(pltpu.make_async_copy(source, target, sems.at[number]))
    for copy in copies:
        copy.start()
    return copies


def flat(value):
    return value.reshape(-1, value.shape[-1])


def store_grad(plan, tile, outs, rows, first_row, columns):
    if not plan.fast:
        outs[0][pl.ds(first_row, tile.shape[0]), columns] = tile.astype(BF)
        return
    keep, send = outs
    core, mine_x, mine_y = place()
    step = rows // plan.count

    def spot(pair, owner):
        off_x = (pair & 1) ^ mine_x
        off_y = ((pair >> 1) & 1) ^ mine_y
        one = jnp.where(owner == 0, off_x, off_y)
        return (one * 2 + (off_x + off_y - one)) * plan.nz + (pair >> 2)

    for local in range(tile.shape[0] // (2 * step)):
        pair = first_row // (2 * step) + local
        low = tile[2 * step * local : 2 * step * local + step]
        high = tile[2 * step * local + step : 2 * step * (local + 1)]
        keep[spot(pair, core), :, columns] = jnp.where(core == 0, low, high).astype(BF)
        send[spot(pair, 1 - core), :, columns] = jnp.where(core == 0, high, low).astype(BF)


class Io:
    def __init__(self, ins, outs, held_in, held_out, in_sems, out_sems):
        self.loads = {}
        for number, (index, ref, cut) in enumerate(ins):
            source = ref if cut is None else ref.at[:, pl.ds(*cut)]
            self.loads[index] = pltpu.make_async_copy(source, held_in[number], in_sems.at[number])
            self.loads[index].start()
        self.outs = {
            index: (held_out[number], ref, out_sems.at[number]) for number, (index, ref) in enumerate(outs)
        }
        self.shipped = []

    def need(self, *indices):
        for index in indices:
            self.loads.pop(index).wait()

    def ship(self, index, columns=None):
        held, ref, sem = self.outs[index]
        if columns is None:
            pltpu.make_async_copy(held, ref, sem).start()
        else:
            pltpu.make_async_copy(held.at[..., columns], ref.at[..., columns], sem).start()
        if index not in self.shipped:
            self.shipped.append(index)

    def finish(self):
        self.need(*list(self.loads))
        for index in self.outs:
            if index not in self.shipped:
                self.ship(index)
        for held, ref, sem in self.outs.values():
            pltpu.make_async_copy(held, ref, sem).wait()


def call(name, body, ins, outs, scratch, limit, flops, aliases=None):
    staged_in = [i for i, item in enumerate(ins) if item[1] == "far"]
    staged_out = [i for i, item in enumerate(outs) if item[1] == "far"]
    cuts = {i: (ins[i][2] if len(ins[i]) > 2 else None) for i in staged_in}

    def held_shape(i):
        array = ins[i][0]
        dims = array.shape if cuts[i] is None else (array.shape[0], cuts[i][1])
        return pltpu.VMEM(dims, array.dtype)

    specs = {"near": VM, "far": FAR, "raw": FAR, "any": ANY}
    n_in, n_out, n_scratch = len(ins), len(outs), len(scratch)

    def kernel(*refs):
        in_refs, refs = list(refs[:n_in]), refs[n_in:]
        out_refs, refs = list(refs[:n_out]), refs[n_out:]
        own, refs = refs[:n_scratch], refs[n_scratch:]
        held_in, refs = refs[: len(staged_in)], refs[len(staged_in) :]
        held_out, refs = refs[: len(staged_out)], refs[len(staged_out) :]
        in_sems, out_sems = refs
        io = Io(
            [(i, in_refs[i], cuts[i]) for i in staged_in],
            [(i, out_refs[i]) for i in staged_out],
            held_in, held_out, in_sems, out_sems,
        )
        for number, i in enumerate(staged_in):
            in_refs[i] = held_in[number]
        for number, i in enumerate(staged_out):
            out_refs[i] = held_out[number]
        body(io, in_refs, out_refs, *own)
        io.finish()

    args = [
        pltpu.with_memory_space_constraint(item[0], pltpu.HBM) if item[1] in ("far", "raw") else item[0]
        for item in ins
    ]
    moved = sum(item[0].size * item[0].dtype.itemsize for item in (*ins, *outs))
    return pl.pallas_call(
        kernel,
        out_shape=[pltpu.HBM(o.shape, o.dtype) if kind in ("far", "raw") else o for o, kind in outs],
        in_specs=[specs[item[1]] for item in ins],
        out_specs=[specs[kind] for _, kind in outs],
        scratch_shapes=[
            *scratch,
            *[held_shape(i) for i in staged_in],
            *[pltpu.VMEM(outs[i][0].shape, outs[i][0].dtype) for i in staged_out],
            pltpu.SemaphoreType.DMA((max(1, len(staged_in)),)),
            pltpu.SemaphoreType.DMA((max(1, len(staged_out)),)),
        ],
        input_output_aliases=aliases or {},
        compiler_params=pltpu.CompilerParams(vmem_limit_bytes=limit * MIB),
        cost_estimate=pl.CostEstimate(flops=flops, bytes_accessed=moved, transcendentals=0),
        name=name,
    )(*args)


def far(*arrays):
    return [(array, "far") for array in arrays]


def norm_of(values):
    center = values - jnp.mean(values, axis=-1, keepdims=True)
    inverse = lax.rsqrt(jnp.mean(center * center, axis=-1, keepdims=True) + 1e-05)
    return center * inverse, inverse


def norm_back(upstream, normed, inverse, gain):
    scaled = upstream * gain
    return inverse * (
        scaled
        - jnp.mean(scaled, axis=-1, keepdims=True)
        - normed * jnp.mean(scaled * normed, axis=-1, keepdims=True)
    )


def fill_bias(bias, seg, pad):
    length = bias.shape[0]
    code = (2 * seg + pad).astype(F32)
    wanted = (2 * seg + 1).astype(F32)
    coded = jnp.broadcast_to(code, (length, length)).T
    rows = lax.broadcasted_iota(jnp.int32, (length, length), 0)
    cols = lax.broadcasted_iota(jnp.int32, (length, length), 1)
    bias[...] = jnp.where((coded == wanted) | (rows == cols), 0.0, -1e30)


def halves_of(values):
    lane = lax.broadcasted_iota(jnp.int32, values.shape, 1)
    zero = jnp.zeros_like(values)
    return jnp.where(lane < HD, values, zero), jnp.where(lane < HD, zero, values)


def prepare(plan, matrices, norm_params):
    side = jnp.pad(norm_params.T, ((0, 0), (0, 128 - norm_params.shape[0])))
    matrices = [*matrices[0:3], jnp.concatenate([side, side], axis=1), *matrices[3:]]
    groups = [matrices[0:4], matrices[4:6], matrices[6:7]]

    def body(io, ins, outs):
        core = lax.axis_index("seq") & 1
        first = 0
        for number, group in enumerate(groups):
            at = 0
            for index in range(first, first + len(group)):
                io.need(index)
                size = ins[index].shape[1] // 2
                left, right = ins[index][:, :size], ins[index][:, size:]
                mine = jnp.where(core == 0, left, right).astype(BF)
                other = jnp.where(core == 0, right, left).astype(BF)
                outs[2 * number][:, at : at + size] = mine
                outs[2 * number + 1][:, at : at + size] = other
                at += size
            first += len(group)

    outs = []
    for group in groups:
        outs += [(shape((group[0].shape[0], sum(w.shape[1] for w in group) // 2), BF), "near")] * 2
    flat_outs = call("prepare", body, far(*matrices), outs, [], 8, 10**6)
    return [flat_outs[0:2], flat_outs[2:4], flat_outs[4:6]]


def row_blocks(length):
    for i in range(length // 128):
        yield slice(i * 128, (i + 1) * 128)


def project(plan, tokens, parts):
    length = tokens[0].size // D if len(tokens) == 1 else tokens[1].shape[0] * len(tokens)
    width = 3 * HALF + 128
    pieces = [(0, width)]

    def body(io, ins, outs, whole, rows_in, sems, put_sems):
        h_ref, q_ref, k_ref, v_ref, n_ref, w_ref, x_ref = outs
        start_parts(plan, ins[len(tokens) :], whole, sems, pieces)
        loads = load_bands(plan, ins[: len(tokens)], rows_in, sems.at[pl.ds(1, len(tokens))])
        wait_part(whole, sems, 0, pieces[0])
        puts = [pltpu.make_async_copy(whole, w_ref, put_sems.at[0])]
        puts[0].start()
        norms = flat(whole[0, :, :, :, 3 * HALF :]).astype(F32).T[0:8]
        n_ref[...] = norms
        for load in loads:
            load.wait()
        puts.append(pltpu.make_async_copy(rows_in, x_ref, put_sems.at[1]))
        puts[1].start()
        for rows in row_blocks(length):
            normed, _ = norm_of(rows_in[rows, :].astype(F32))
            h_ref[rows, :] = (normed * norms[0:1, :] + norms[1:2, :]).astype(BF)
        io.ship(0)
        for m, (out, scale) in enumerate(((q_ref, 0.125), (k_ref, 1.0), (v_ref, 1.0))):
            for h in range(2):
                weight = flat(whole[h, :, :, :, m * HALF : (m + 1) * HALF])
                out[:, h * HALF : (h + 1) * HALF] = (dot(h_ref[...], weight, 1, 0) * scale).astype(BF)
            io.ship(1 + m)
        for put in puts:
            put.wait()

    act = shape((length, D), BF)
    wide = plan.wide(D, width)
    return call(
        "project", body, [*[(t, "any") for t in tokens], *[(p, "any") for p in parts]],
        [*[(act, "far")] * 4, (shape((8, D), F32), "near"), (shape(wide, BF), "raw"), (act, "raw")],
        [
            pltpu.VMEM(wide, BF), pltpu.VMEM((length, D), BF),
            pltpu.SemaphoreType.DMA((1 + len(tokens),)), pltpu.SemaphoreType.DMA((2,)),
        ],
        20, 2 * length * 3 * D * D,
    )


def mix(plan, query, key, value, seg, pad):
    length = query.shape[0]

    def body(io, ins, outs, bias):
        q_ref, k_ref, v_ref, seg_ref, pad_ref = ins
        at_ref, a_ref, l_ref = outs
        fill_bias(bias, seg_ref[...], pad_ref[...])
        io.need(0, 1, 2)

        @pl.loop(0, PAIRS)
        def _(p):
            cols = pl.ds(pl.multiple_of(p * 128, 128), 128)
            keys = k_ref[:, cols]
            turned = v_ref[:, cols].T
            for half, query in enumerate(halves_of(q_ref[:, cols])):
                scores = dot(keys, query, 1, 1) + bias[...]
                top = jnp.max(scores, axis=0, keepdims=True)
                lifted = jnp.exp(scores - top)
                total = jnp.sum(lifted, axis=0, keepdims=True)
                soft = (lifted * (1.0 / total)).astype(BF)
                mixed = dot(turned[half * HD : (half + 1) * HD], soft, 1, 0)
                at_ref[pl.ds(pl.multiple_of(p * 128 + half * HD, HD), HD), :] = mixed.astype(BF)
                l_ref[pl.ds(2 * p + half, 1), :] = top + jnp.log(total)
            a_ref[:, cols] = at_ref[pl.ds(pl.multiple_of(p * 128, 128), 128), :].T

    return call(
        "mix", body, [*far(query, key, value), (seg, "near"), (pad, "near")],
        [(shape((D, length), BF), "far"), (shape((length, D), BF), "far"), (shape((H, length), F32), "far")],
        [pltpu.VMEM((length, length), F32)],
        14, 2 * length * (2 * length * D),
    )


def widen(plan, tokens, mixed, cot, norms, parts):
    length = tokens.shape[0]
    pieces = [(0, HALF), (HALF, D), (HALF + D, D)]

    def body(io, ins, outs, whole, g_in, sems, put_sems):
        x_ref, a_ref, n_ref, *rest = ins
        m_ref, h_ref, z_ref, s_ref, *grads = outs[:-2]
        w_ref, g_out = outs[-2:]
        start_parts(plan, rest[len(cot) :], whole, sems, pieces)
        loads = load_bands(plan, rest[: len(cot)], g_in, sems.at[pl.ds(3, len(cot))])
        io.need(0, 1)
        wait_part(whole, sems, 0, pieces[0])
        for h in range(2):
            cols = slice(h * HALF, (h + 1) * HALF)
            weight = flat(whole[h, :, :, :, 0:HALF])
            m_ref[:, cols] = x_ref[:, cols].astype(F32) + dot(a_ref[...], weight, 1, 0)
        io.ship(0)
        for rows in row_blocks(length):
            normed, _ = norm_of(m_ref[rows, :])
            h_ref[rows, :] = (normed * n_ref[2:3, :] + n_ref[3:4, :]).astype(BF)
        io.ship(1)
        wait_part(whole, sems, 1, pieces[1])
        wait_part(whole, sems, 2, pieces[2])
        puts = [pltpu.make_async_copy(whole, w_ref, put_sems.at[0]), pltpu.make_async_copy(g_in, g_out, put_sems.at[1])]
        puts[0].start()
        for load in loads:
            load.wait()
        puts[1].start()
        for part in range(2):
            for h in range(2):
                block = h * 2 + part
                cols = slice(block * D, (block + 1) * D)
                weight = flat(whole[h, :, :, :, HALF + part * D : HALF + (part + 1) * D])
                up = dot(h_ref[...], weight, 1, 0)
                bell = 0.5 + 0.5 * lax.erf(up * 0.7071067811865476)
                z_ref[:, cols] = (up * bell).astype(BF)
                s_ref[:, cols] = (bell + up * (jnp.exp(-0.5 * up * up) * 0.3989422804014327)).astype(BF)
                io.ship(2, pl.ds(block * D, D))
                io.ship(3, pl.ds(block * D, D))
                tile = dot(z_ref[:, cols], g_in[...], 0, 0)
                store_grad(plan, tile, grads, FF, block * D, slice(None))
        for index in range(len(grads)):
            io.ship(4 + index)
        for put in puts:
            put.wait()

    act = shape((length, D), BF)
    wide = plan.wide(D, 5 * HALF)
    outs = [shape((length, D), F32), act, shape((length, FF), BF), shape((length, FF), BF), *plan.grads(FF, D)]
    return call(
        "widen", body,
        [*far(tokens, mixed), (norms, "near"), *[(c, "any") for c in cot], *[(p, "any") for p in parts]],
        [*[(o, "far") for o in outs], (shape(wide, BF), "raw"), (act, "raw")],
        [
            pltpu.VMEM(wide, BF), pltpu.VMEM((length, D), BF),
            pltpu.SemaphoreType.DMA((3 + len(cot),)), pltpu.SemaphoreType.DMA((2,)),
        ],
        40, 2 * length * (D * D + 2 * D * FF),
    )


def narrow(plan, blocks, mid, below, grads, low, hidden, slope, cot, whole_ou, parts_down):
    length = mid.shape[0]
    up_pieces = [(HALF + (block % 2) * D, D) for block in blocks]
    side = blocks[0] // 2
    start, final = blocks[0] == 0, blocks[-1] == BLOCKS - 1
    cut = (blocks[0] * D, len(blocks) * D)
    n_out = plan.outs()

    def body(io, ins, outs, *scratch):
        m_ref, h_ref, z_ref, s_ref, g_ref, up_ref, *rest = ins
        downs = rest[: len(parts_down)]
        b_ref, *grad_refs = outs[: 1 + n_out]
        o_refs = outs[1 + n_out :]
        held, (acc, whole_up, whole_down, sems, put_sems) = scratch[:-5], scratch[-5:]
        copies = []
        start_parts(plan, downs, whole_down, sems.at[pl.ds(0, 1)], [(0, HALF)], blocks)
        ups = []
        for number, (first, size) in enumerate(up_pieces):
            up = pltpu.make_async_copy(
                up_ref.at[side, :, :, :, pl.ds(first, size)], whole_up.at[number], sems.at[1 + number]
            )
            up.start()
            ups.append(up)
        wait_part(whole_down, sems, 0, (0, HALF))
        io.need(4, 3, 1, 2)
        for number, block in enumerate(blocks):
            local = slice(number * D, (number + 1) * D)
            back = dot(g_ref[:, 0:HALF], flat(whole_down[0, number]), 1, 1)
            back += dot(g_ref[:, HALF:D], flat(whole_down[1, number]), 1, 1)
            du = (back * s_ref[:, local]).astype(BF)
            tile = dot(h_ref[...], du, 0, 0)
            store_grad(plan, tile, held, D, 0, local)
            for i in range(n_out):
                copy = pltpu.make_async_copy(
                    held[i].at[..., pl.ds(number * D, D)], grad_refs[i].at[..., pl.ds(block * D, D)], put_sems.at[number, i]
                )
                copy.start()
                copies.append(copy)
            ups[number].wait()
            lower = dot(du, flat(whole_up[number]), 1, 1)
            if number == 0:
                if start:
                    b_ref[...] = lower
                else:
                    io.need(6 + len(parts_down))
                    b_ref[...] = rest[len(parts_down)][...] + lower
                io.need(0)
            else:
                b_ref[...] += lower
            z = z_ref[:, local]
            for h in range(2):
                half = slice(h * HALF, (h + 1) * HALF)
                gain = dot(z, flat(whole_down[h, number]), 1, 0)
                acc[:, half] = gain + (m_ref[:, half] if number == 0 else acc[:, half])
        if final:
            for number, o_ref in enumerate(o_refs):
                o_ref[...] = acc[band(plan, number, length), :].astype(BF)
        else:
            o_refs[0][...] = acc[...]
        for copy in copies:
            copy.wait()

    wide = plan.wide(D, D)
    deep = plan.wide(FF, HALF)
    ins = [
        *far(mid, low), (hidden, "far", cut), (slope, "far", cut), *far(cot), (whole_ou, "raw"),
        *[(p, "any") for p in parts_down],
    ]
    aliases = {}
    if not start:
        ins += far(below)
        aliases = {len(ins) + i: 1 + i for i in range(n_out)}
        ins += [(g, "raw") for g in grads]
    return call(
        "narrow" + str(blocks[0]), body, ins,
        [
            (shape((length, D), F32), "far"), *[(g, "raw") for g in plan.grads(D, FF + D)],
            *[(o, "far") for o in (plan.band_shapes(length) if final else [shape((length, D), F32)])],
        ],
        [pltpu.VMEM(o.shape, BF) for o in plan.grads(D, len(blocks) * D)]
        + [
            pltpu.VMEM((length, D), F32),
            pltpu.VMEM((len(blocks), *wide[1:]), BF),
            pltpu.VMEM((2, len(blocks), *deep[2:]), BF),
            pltpu.SemaphoreType.DMA((1 + len(blocks),)),
            pltpu.SemaphoreType.DMA((len(blocks), n_out)),
        ],
        40, 2 * length * len(blocks) * D * D * 4, aliases,
    )


def turn(plan, mid, back, cot, norms, mixed_t, whole_ou, grads):
    length = mid.shape[0]
    n_out = plan.outs()

    def body(io, ins, outs, *scratch):
        m_ref, b_ref, g_ref, n_ref, at_ref, w_ref, *_ = ins
        x_ref, d_ref, s_ref, *grad_refs = outs
        held, (low, whole, sems, put_sems) = scratch[:-4], scratch[-4:]
        load = pltpu.make_async_copy(w_ref.at[..., pl.ds(0, HALF)], whole, sems.at[0])
        load.start()
        s_ref[...] = jnp.zeros_like(s_ref)
        io.need(0, 1, 2)
        for rows in row_blocks(length):
            normed, inverse = norm_of(m_ref[rows, :])
            upstream = b_ref[rows, :]
            total = g_ref[rows, :].astype(F32) + norm_back(upstream, normed, inverse, n_ref[2:3, :])
            x_ref[rows, :] = total
            low[rows, :] = total.astype(BF)
            s_ref[0:1, :] += jnp.sum(upstream * normed, axis=0, keepdims=True)
            s_ref[1:2, :] += jnp.sum(upstream, axis=0, keepdims=True)
        io.ship(0)
        io.need(4)
        store_grad(plan, dot(at_ref[...], low[...], 1, 0), held, D, 0, slice(None))
        copies = [
            pltpu.make_async_copy(held[i], grad_refs[i].at[..., pl.ds(FF, D)], put_sems.at[i]) for i in range(n_out)
        ]
        for copy in copies:
            copy.start()
        load.wait()
        back_a = dot(low[:, 0:HALF], flat(whole[0]), 1, 1)
        back_a += dot(low[:, HALF:D], flat(whole[1]), 1, 1)
        d_ref[...] = back_a.astype(BF)
        io.ship(1)
        for copy in copies:
            copy.wait()

    ins = [*far(mid, back, cot), (norms, "near"), *far(mixed_t), (whole_ou, "raw"), *[(g, "raw") for g in grads]]
    return call(
        "turn", body, ins,
        [
            (shape((length, D), F32), "far"), (shape((length, D), BF), "far"), (shape((2, D), F32), "near"),
            *[(g, "raw") for g in plan.grads(D, FF + D)],
        ],
        [pltpu.VMEM(o.shape, BF) for o in plan.grads(D, D)]
        + [
            pltpu.VMEM((length, D), BF), pltpu.VMEM(plan.wide(D, HALF), BF),
            pltpu.SemaphoreType.DMA((1,)), pltpu.SemaphoreType.DMA((n_out,)),
        ],
        24, 2 * length * 2 * D * D, {6 + i: 3 + i for i in range(n_out)},
    )


def attend_back(plan, side, low, query, key, value, lse, cot, seg, pad):
    length = low.shape[0]
    cut = (side * HALF, HALF)

    def body(io, ins, outs, bias):
        h_ref, q_ref, k_ref, v_ref, c_ref, l_ref, seg_ref, pad_ref = ins
        d_ref, *grads = outs
        fill_bias(bias, seg_ref[...], pad_ref[...])
        io.need(1, 2, 3, 4, 5)

        @pl.loop(0, PAIRS // 2)
        def _(local):
            p = local + side * (PAIRS // 2)
            first = pl.multiple_of(local * 128, 128)
            cols = pl.ds(first, 128)
            keys, values = k_ref[:, cols], v_ref[:, cols]
            turned = keys.T
            queries, cots = halves_of(q_ref[:, cols]), halves_of(c_ref[:, cols])
            dv = dk = None
            dqs = []
            for half in range(2):
                scores = dot(keys, queries[half], 1, 1) + bias[...]
                soft = jnp.exp(scores - l_ref[pl.ds(2 * p + half, 1), :])
                gain = dot(soft.astype(BF), cots[half], 1, 0)
                dv = gain if dv is None else dv + gain
                dp = dot(values, cots[half], 1, 1)
                share = jnp.sum(soft * dp, axis=0, keepdims=True)
                ds = (soft * (dp - share)).astype(BF)
                gain = dot(ds, queries[half], 1, 0)
                dk = gain if dk is None else dk + gain
                dqs.append(dot(turned[half * HD : (half + 1) * HD], ds, 1, 0) * 0.125)
            d_ref[:, cols] = jnp.concatenate(dqs, axis=0).T.astype(BF)
            d_ref[:, pl.ds(first + HALF, 128)] = dk.astype(BF)
            d_ref[:, pl.ds(first + 2 * HALF, 128)] = dv.astype(BF)

        io.ship(0)
        io.need(0)
        for m in range(3):
            cols = slice(m * HALF, (m + 1) * HALF)
            store_grad(plan, dot(h_ref[...], d_ref[:, cols], 0, 0), grads, D, 0, cols)
            for index in range(len(grads)):
                io.ship(1 + index, pl.ds(m * HALF, HALF))

    return call(
        "attend_back" + str(side), body,
        [
            *far(low), *[(a, "far", cut) for a in (query, key, value, cot)], *far(lse),
            (seg, "near"), (pad, "near"),
        ],
        [(shape((length, 3 * HALF), BF), "far"), *[(g, "far") for g in plan.grads(D, 3 * HALF)]],
        [pltpu.VMEM((length, length), F32)],
        20, length * (3 * D * D + 5 * length * D),
    )


def finish_tokens(plan, tokens, spreads, mid_cot, norms, whole_qkv):
    length = tokens.shape[0]
    pieces = [(0, 3 * HALF)]

    def body(io, ins, outs, back, whole, sems):
        x_ref, d0_ref, d1_ref, c_ref, n_ref, w_ref = ins
        *o_refs, s_ref = outs
        start_parts(plan, [w_ref], whole, sems, pieces)
        s_ref[...] = jnp.zeros_like(s_ref)
        wait_part(whole, sems, 0, pieces[0])
        total = None
        io.need(1, 2)
        for m in range(3):
            for h in range(2):
                cols = slice(m * HALF, (m + 1) * HALF)
                gain = dot((d0_ref, d1_ref)[h][:, cols], flat(whole[h, :, :, :, cols]), 1, 1)
                total = gain if total is None else total + gain
        back[...] = total
        io.need(0, 3)
        for rows in row_blocks(length):
            normed, inverse = norm_of(x_ref[rows, :].astype(F32))
            upstream = back[rows, :]
            c_ref[rows, :] += norm_back(upstream, normed, inverse, n_ref[0:1, :])
            s_ref[0:1, :] += jnp.sum(upstream * normed, axis=0, keepdims=True)
            s_ref[1:2, :] += jnp.sum(upstream, axis=0, keepdims=True)
        for number, o_ref in enumerate(o_refs):
            o_ref[...] = c_ref[band(plan, number, length), :].astype(BF)

    return call(
        "finish_tokens", body, [*far(tokens, *spreads, mid_cot), (norms, "near"), (whole_qkv, "raw")],
        [*[(o, "far") for o in plan.band_shapes(length)], (shape((2, D), F32), "near")],
        [pltpu.VMEM((length, D), F32), pltpu.VMEM(plan.wide(D, 3 * HALF), BF), pltpu.SemaphoreType.DMA((1,))],
        20, 2 * length * 3 * D * D,
    )


def update(plan, grads, squares, masters, firsts, seconds, passed):
    rates = [D**-0.5] * 3 + [4.0 * D**-0.5, D**-0.5, FF**-0.5, 0.2]
    decays = [0.01] * 6 + [0.0]
    count = len(masters)
    given = len(grads)

    def body(io, ins, outs, sems):
        grad_refs, sq_ref = ins[:given], ins[given]
        first = given + 1
        norm = jnp.sqrt(jnp.sum(sq_ref[...], axis=0, keepdims=True))
        outs[0][...] = norm
        factor = jnp.minimum(1.0, clip_limit / (norm + 1e-06))[:, 0:1]
        for i in reversed(range(count)):
            w_ref, m_ref, s_ref = (ins[first + k * count + i] for k in range(3))
            io.need(*(first + k * count + i for k in range(3)))
            if i < 3:
                cols = [
                    (slice(h * HALF, (h + 1) * HALF), grad_refs[0][:, (3 * h + i) * HALF : (3 * h + i + 1) * HALF])
                    for h in range(2)
                ]
            elif i == 3:
                cols = [(slice(None), grad_refs[1][:, FF:])]
            elif i == 4:
                cols = [(slice(None), grad_refs[1][:, :FF])]
            else:
                cols = [(slice(None), grad_refs[i - 3][...])]
            for where, grad in cols:
                clipped = factor * grad
                one = 0.5 * m_ref[:, where] + 0.5 * clipped
                two = 0.55 * s_ref[:, where] + 0.45 * clipped * clipped
                root = jnp.sqrt(two * (1.0 / (1.0 - 0.55**STEP))) + 1e-08
                weight = w_ref[:, where]
                step = (one * (1.0 / (1.0 - 0.5**STEP))) / root + decays[i] * weight
                outs[1 + i][:, where] = weight - rates[i] * step
                outs[1 + count + i][:, where] = one
                outs[1 + 2 * count + i][:, where] = two
            for k in range(3):
                io.ship(1 + k * count + i)
        last = first + 3 * count
        copies = []
        for number in range(len(passed)):
            which, place_in = number // plan.bands(), number % plan.bands()
            io.need(last + number)
            target = outs[1 + 3 * count + which]
            if plan.bands() > 1:
                target = target.at[lax.axis_index("seq") ^ place_in]
            copies.append(pltpu.make_async_copy(ins[last + number], target, sems.at[number]))
            copies[-1].start()
        for copy in copies:
            copy.wait()

    like = [(shape(w.shape, F32), "far") for w in masters] * 3
    pieces = [shape((plan.bands(), *p.shape), BF) if plan.bands() > 1 else p for p in passed[:: plan.bands()]]
    return call(
        "update", body, [*[(g, "near") for g in grads], (squares, "near"), *far(*masters, *firsts, *seconds, *passed)],
        [(shape((1, squares.shape[1]), F32), "near"), *like, *[(o, "raw") for o in pieces]],
        [pltpu.SemaphoreType.DMA((len(passed),))], 20, 10**7,
    )


def after(values, *others):
    return lax.optimization_barrier((values, others))[0]


def send(plan, values, perm):
    return lax.ppermute(values, AXES, perm)


def blocks_of(plan, mine, other):
    core = lax.axis_index("seq") & 1
    got = send(plan, other, plan.core)
    block = jnp.where(core == 0, jnp.concatenate([mine, got]), jnp.concatenate([got, mine]))
    return jnp.broadcast_to(block[None], (plan.nz, *block.shape))


def along_z(plan, values):
    return lax.all_to_all(values, "dp", 0, 0, axis_index_groups=plan.groups, tiled=True)


def gather_whole(matrices):
    split = [w.reshape(w.shape[0], 2, -1) for w in matrices]
    halves = jnp.concatenate(split, axis=2).transpose(1, 0, 2).astype(BF)
    full = lax.all_gather(halves, AXES, axis=1, tiled=True)
    return [full.reshape(2, BLOCKS, 1, -1, full.shape[-1])]


def add(one, two):
    return one.astype(F32) + two.astype(F32)


def fold(keep, got):
    size = keep.shape[0] // 2
    return add(keep[size:], got[size:]).astype(BF), add(keep[:size], got[:size]).astype(BF)


def total(blocks):
    return jnp.sum(blocks.astype(F32), axis=0)


def everywhere(plan, values):
    spread = jnp.broadcast_to(values[None], (plan.count, *values.shape))
    return lax.all_to_all(spread, AXES, 0, 0, tiled=True)


def norm_slices(plan, sums_one, sums_two):
    sums = jnp.concatenate([sums_one, sums_two], axis=0)
    slices = sums.reshape(4, plan.count, -1).transpose(1, 0, 2)
    return jnp.sum(lax.all_to_all(slices, AXES, 0, 0, tiled=True), axis=0)


def finish(plan, grads, masters, firsts, seconds, *passed):
    local = sum(jnp.sum(g * g) for g in grads)
    squares = everywhere(plan, jnp.broadcast_to(local, (1, 128))).reshape(plan.count, 128)
    norm, *updated, output, input_grad = update(plan, grads, squares, masters, firsts, seconds, passed)
    return (output, input_grad, norm[0, 0], *updated)


def on_device(plan, *args):
    tokens_in, segment_ids, pad_mask, out_grad = args[:4]
    masters, firsts, seconds = args[4:11], args[11:18], args[18:25]
    each, piece, _ = tokens_in.shape
    length = each // plan.seq * plan.seq * piece

    plan.fast = plan.fast and each == plan.seq

    def swap(values, number):
        return lax.ppermute(values, "seq", [(i, i ^ number) for i in range(plan.seq)])

    def to_rows(values):
        if not plan.fast:
            return [lax.all_to_all(values, "seq", 0, 0, tiled=True).reshape(length, D)]
        others = [lax.dynamic_index_in_dim(values, row ^ n, 0, keepdims=False) for n in range(1, plan.seq)]
        return [values, *[swap(other, 1 + n) for n, other in enumerate(others)]]

    def to_pieces(bands):
        if not plan.fast:
            return [lax.all_to_all(bands[0].reshape(each, piece, D), "seq", 0, 0, tiled=True)]
        return [bands[0], *[swap(other, 1 + n) for n, other in enumerate(bands[1:])]]

    row = lax.axis_index("seq")
    seg = lax.dynamic_slice_in_dim(segment_ids, row, 1, 0)
    pad = lax.dynamic_slice_in_dim(pad_mask, row, 1, 0)

    if not plan.fast:
        side = jnp.pad(masters[6].T, ((0, 0), (0, 124)))
        side = jnp.concatenate([side, side], axis=1)
        one, two, three = (gather_whole(m) for m in ([*masters[0:3], side], masters[3:5], masters[5:6]))
        low_one, query, key, value, norms, whole_qkv, tokens = project(plan, to_rows(tokens_in), one)
        mixed_t, mixed, lse = mix(plan, query, key, value, seg, pad)
        mid, low_two, hidden, slope, *g_down, whole_ou, cot = widen(plan, tokens, mixed, to_rows(out_grad), norms, two)
        back, *g_up, part = narrow(plan, (0, 1), mid, None, None, low_two, hidden, slope, cot, whole_ou, three)
        back, *g_up, result = narrow(plan, (2, 3), part, back, g_up, low_two, hidden, slope, cot, whole_ou, three)
        mid_cot, mixed_cot, sums_two, *g_up = turn(plan, mid, back, cot, norms, mixed_t, whole_ou, g_up)
        halves = [
            attend_back(plan, side, low_one, query, key, value, lse, mixed_cot, seg, pad) for side in range(2)
        ]
        stream, sums_one = finish_tokens(plan, tokens, [h[0] for h in halves], mid_cot, norms, whole_qkv)
        grads = [
            lax.psum_scatter(g.astype(F32), AXES, scatter_dimension=0, tiled=True)
            for g in (halves[0][1], halves[1][1], *g_up, *g_down)
        ]
        grads = [jnp.concatenate(grads[:2], axis=1), *grads[2:]]
        grads.append(norm_slices(plan, sums_one, sums_two))
        return finish(plan, grads, masters, firsts, seconds, *to_pieces([result]), *to_pieces([stream]))

    first, second, third = prepare(plan, masters[:6], masters[6])
    block_one = blocks_of(plan, *first)
    near_one = along_z(plan, block_one)
    tokens = to_rows(after(tokens_in, first))
    block_two = blocks_of(plan, *second)
    block_three = blocks_of(plan, *third)
    near_one = after(near_one, tokens, block_two, block_three)

    def spread(near):
        return send(plan, near, plan.second), send(plan, near, plan.first)

    def cross(near, beside, across, corner):
        parts = [near, beside, across, corner]
        return parts + [send(plan, part, plan.core) for part in parts]

    beside_one, across_one = spread(near_one)
    near_two = along_z(plan, after(block_two, near_one))
    one = cross(near_one, beside_one, across_one, send(plan, beside_one, plan.first))
    low_one, query, key, value, norms, whole_qkv, tokens = project(plan, tokens, one)
    near_two = after(near_two, query)
    near_three = along_z(plan, after(block_three, near_two))
    beside_two, across_two = spread(near_two)
    query = after(query, near_two)
    cot = to_rows(after(out_grad, query))
    mixed_t, mixed, lse = mix(plan, query, key, value, seg, pad)
    beside_two, across_two = after((beside_two, across_two), lse)
    corner_two = send(plan, beside_two, plan.first)
    near_three = after(near_three, lse)
    beside_three, across_three = spread(near_three)
    two = cross(near_two, beside_two, across_two, corner_two)
    mid, low_two, hidden, slope, *g_down, whole_ou, cot = widen(plan, tokens, after(mixed, near_three), cot, norms, two)
    beside_three, across_three = after((beside_three, across_three), slope)
    corner_three = send(plan, beside_three, plan.first)
    three = cross(near_three, beside_three, across_three, corner_three)

    keep_d, go_d = g_down
    go_d, keep_d = fold(keep_d, send(plan, go_d, plan.core))
    got_d = send(plan, go_d, plan.first)
    back, *g_up, part = narrow(
        plan, (0, 1), after(mid, go_d), None, None, low_two, hidden, slope, cot, whole_ou, three
    )
    got_d = after(got_d, back)
    go_d, keep_d = fold(keep_d, got_d)
    got_d = send(plan, go_d, plan.second)
    back, *g_up_result = narrow(
        plan, (2, 3), after(part, go_d), back, g_up, low_two, hidden, slope, cot, whole_ou, three
    )
    g_up, result = g_up_result[:2], g_up_result[2:]
    output = to_pieces(result)
    block_d = add(keep_d, after(got_d, back)).astype(BF)
    blocks_d = along_z(plan, block_d)
    mid_cot, mixed_cot, sums_two, keep_u, go_u = turn(
        plan, mid, after(back, block_d), cot, norms, mixed_t, whole_ou, g_up
    )
    go_u, keep_u = fold(keep_u, send(plan, go_u, plan.core))
    got_u = send(plan, go_u, plan.first)
    mixed_cot = after(mixed_cot, go_u)
    spread_a, keep_a, go_a = attend_back(plan, 0, low_one, query, key, value, lse, mixed_cot, seg, pad)
    got_u, blocks_d, output = after((got_u, blocks_d, output), spread_a)
    grad_d = total(blocks_d)
    go_u, keep_u = fold(keep_u, got_u)
    got_u = send(plan, go_u, plan.second)
    go_a, keep_a = fold(keep_a, send(plan, go_a, plan.core))
    got_a = send(plan, go_a, plan.first)
    mixed_cot = after(mixed_cot, go_u, go_a)
    spread_b, keep_b, go_b = attend_back(plan, 1, low_one, query, key, value, lse, mixed_cot, seg, pad)
    go_b, keep_b = fold(keep_b, send(plan, go_b, plan.core))
    got_b = send(plan, go_b, plan.first)
    block_u = add(keep_u, after(got_u, spread_b)).astype(BF)
    blocks_u = along_z(plan, block_u)
    go_a, keep_a = fold(keep_a, after(got_a, spread_b))
    got_a = send(plan, go_a, plan.second)
    *stream, sums_one = finish_tokens(
        plan, tokens, [spread_a, spread_b], after(mid_cot, go_b, block_u, go_a), norms, whole_qkv
    )
    got_b, blocks_u = after((got_b, blocks_u), sums_one)
    input_grad = to_pieces(stream)
    go_b, keep_b = fold(keep_b, got_b)
    got_b = send(plan, go_b, plan.second)
    slices = norm_slices(plan, sums_one, sums_two)
    halves = [add(keep_a, after(got_a, sums_one)), add(keep_b, got_b)]
    blocks_ab = along_z(plan, after(jnp.concatenate(halves, axis=2).astype(BF), slices))
    grads = [total(blocks_ab), total(blocks_u), grad_d, slices]
    return finish(plan, grads, masters, firsts, seconds, *output, *input_grad)


def solution(mesh):
    plan = Plan(mesh, None)
    rows = P(AXES, None)
    weights = (*[rows] * 6, P(None, AXES))
    tokens = P("dp", "seq", None)
    return jax.shard_map(
        partial(on_device, plan),
        mesh=mesh,
        in_specs=(tokens, P("dp", None), P("dp", None), tokens, *weights * 3),
        out_specs=(tokens, tokens, P(), *weights * 3),
        check_vma=False,
    )
```

```python
from functools import partial

import jax
import jax.numpy as jnp
from jax import lax
from jax.experimental import pallas as pl
from jax.experimental.pallas import tpu as pltpu
from jax.sharding import PartitionSpec as P

D = 768
H = 12
HD = 64
FF = 3072
STEP = 7
HALF = D // 2
PAIRS = H // 2
BLOCKS = 4
BF = jnp.bfloat16
F32 = jnp.float32
AXES = ("dp", "seq")
clip_limit = 1.0
MIB = 2**20

VM = pl.BlockSpec(memory_space=pltpu.VMEM)
ANY = pl.BlockSpec(memory_space=pl.ANY)
FAR = pl.BlockSpec(memory_space=pltpu.HBM)


def dot(left, right, left_dim, right_dim):
    return lax.dot_general(
        left, right, (((left_dim,), (right_dim,)), ((), ())), preferred_element_type=F32
    )


def shape(dims, kind):
    return jax.ShapeDtypeStruct(dims, kind)


class Plan:
    def __init__(self, mesh, rows_each):
        self.dp = mesh.shape["dp"]
        self.seq = mesh.shape["seq"]
        self.count = self.dp * self.seq
        self.fast = (
            self.seq == 4
            and self.dp % 2 == 0
            and BLOCKS * 8 == self.count
            and (2 * D // self.count) % 16 == 0
        )
        self.nz = self.dp // 2
        self.rows = D // self.count
        self.far = FF // self.count
        both = range(self.count)
        self.core = [(d, d ^ 1) for d in both]
        self.first = [(d, d ^ (2 if d % 2 == 0 else 4)) for d in both]
        self.second = [(d, d ^ (4 if d % 2 == 0 else 2)) for d in both]
        self.groups = [list(range(low, self.dp, 2)) for low in range(2)]

    def wide(self, rows, columns):
        if self.fast:
            return (self.nz, 4, 2 * rows // self.count, columns)
        return (BLOCKS, 1, rows // BLOCKS, columns)

    def parts(self):
        return 8 if self.fast else 1

    def grads(self, rows, columns):
        if self.fast:
            half = shape((4, self.nz, rows // self.count, columns), BF)
            return [half, half]
        return [shape((rows, columns), BF)]

    def outs(self):
        return 2 if self.fast else 1

    def bands(self):
        return self.seq if self.fast else 1

    def band_shapes(self, length):
        return [shape((length // self.bands(), D), BF)] * self.bands()


def place():
    seq = lax.axis_index("seq")
    return seq & 1, seq >> 1, lax.axis_index("dp") & 1


def start_parts(plan, parts, whole, sems, pieces, blocks=None):
    blocks = slice(None) if blocks is None else pl.ds(blocks[0], len(blocks))
    for index, (first, size, to) in enumerate(pieces):
        columns = pl.ds(first, size)
        if len(parts) == 1:
            for half in range(2):
                pltpu.make_async_copy(
                    parts[0].at[half, blocks, :, :, columns], whole.at[..., pl.ds(to + half * size, size)], sems.at[index]
                ).start()
            continue
        core, mine_x, mine_y = place()
        for number, part in enumerate(parts):
            owner = core if number < 4 else 1 - core
            one, two = (number >> 1) & 1, number & 1
            off_x = jnp.where(owner == 0, one, two)
            off_y = jnp.where(owner == 0, two, one)
            spot = (mine_y ^ off_y) * 2 + (mine_x ^ off_x)
            target = pl.ds(pl.multiple_of(to + owner * size, 128), size)
            pltpu.make_async_copy(part.at[blocks, :, columns], whole.at[:, spot, :, target], sems.at[index]).start()


def wait_part(whole, sems, index, piece):
    view = whole.at[..., pl.ds(piece[2], 2 * piece[1])]
    pltpu.make_async_copy(view, view, sems.at[index]).wait()


def band(plan, number, length):
    if plan.bands() == 1:
        return pl.ds(0, length)
    size = length // plan.bands()
    return pl.ds(pl.multiple_of((lax.axis_index("seq") ^ number) * size, size), size)


def load_bands(plan, refs, whole, sems):
    copies = []
    for number, ref in enumerate(refs):
        source = ref.at[lax.axis_index("seq")] if number == 0 and plan.bands() > 1 else ref
        target = whole.at[band(plan, number, whole.shape[0]), :]
        copies.append(pltpu.make_async_copy(source, target, sems.at[number]))
    for copy in copies:
        copy.start()
    return copies


def flat(value):
    return value.reshape(-1, value.shape[-1])


def held_grad(plan, rows, columns):
    one = plan.grads(rows, columns)
    return pltpu.VMEM((len(one), *one[0].shape), BF)


def put_grad(held, outs, sems, held_view, out_view):
    copies = [
        pltpu.make_async_copy(held.at[(i, *held_view)], out.at[out_view], sems.at[i]) for i, out in enumerate(outs)
    ]
    for copy in copies:
        copy.start()
    return copies


def store_grad(plan, tile, held, rows, first_row, columns):
    if not plan.fast:
        held[0, pl.ds(first_row, tile.shape[0]), columns] = tile.astype(BF)
        return
    core, mine_x, mine_y = place()
    step = rows // plan.count

    def spot(pair, owner):
        off_x = (pair & 1) ^ mine_x
        off_y = ((pair >> 1) & 1) ^ mine_y
        return (off_x * 2 + off_y if owner == 0 else off_y * 2 + off_x), pair >> 2

    for local in range(tile.shape[0] // (2 * step)):
        pair = first_row // (2 * step) + local
        low = tile[2 * step * local : 2 * step * local + step]
        high = tile[2 * step * local + step : 2 * step * (local + 1)]
        held[core, *spot(pair, 0), :, columns] = low.astype(BF)
        held[1 - core, *spot(pair, 1), :, columns] = high.astype(BF)


class Io:
    def __init__(self, ins, outs, held_in, held_out, in_sems, out_sems):
        self.loads, self.running = {}, []
        for number, (index, ref, cut) in enumerate(ins):
            source = ref if cut is None else ref.at[:, pl.ds(*cut)]
            self.loads[index] = pltpu.make_async_copy(source, held_in[number], in_sems.at[number])
        self.outs = {
            index: (held_out[number], ref, out_sems.at[number]) for number, (index, ref) in enumerate(outs)
        }
        self.shipped = []

    def start(self, *indices):
        for index in indices or [i for i in self.loads if i not in self.running]:
            self.loads[index].start()
            self.running.append(index)

    def need(self, *indices):
        for index in indices:
            self.loads.pop(index).wait()

    def ship(self, index, columns=None):
        held, ref, sem = self.outs[index]
        if columns is None:
            pltpu.make_async_copy(held, ref, sem).start()
        else:
            pltpu.make_async_copy(held.at[..., columns], ref.at[..., columns], sem).start()
        if index not in self.shipped:
            self.shipped.append(index)

    def finish(self):
        self.need(*list(self.loads))
        for index in self.outs:
            if index not in self.shipped:
                self.ship(index)
        for held, ref, sem in self.outs.values():
            pltpu.make_async_copy(held, ref, sem).wait()


def call(name, body, ins, outs, scratch, limit, cost=10**11, aliases=None):
    staged_in = [i for i, item in enumerate(ins) if item[1] == "far"]
    staged_out = [i for i, item in enumerate(outs) if item[1] == "far"]
    cuts = {i: (ins[i][2] if len(ins[i]) > 2 else None) for i in staged_in}

    def held_shape(i):
        array = ins[i][0]
        dims = array.shape if cuts[i] is None else (array.shape[0], cuts[i][1])
        return pltpu.VMEM(dims, array.dtype)

    specs = {"near": VM, "far": FAR, "raw": FAR, "any": ANY}
    n_in, n_out, n_scratch = len(ins), len(outs), len(scratch)

    def kernel(*refs):
        in_refs, refs = list(refs[:n_in]), refs[n_in:]
        out_refs, refs = list(refs[:n_out]), refs[n_out:]
        own, refs = refs[:n_scratch], refs[n_scratch:]
        held_in, refs = refs[: len(staged_in)], refs[len(staged_in) :]
        held_out, refs = refs[: len(staged_out)], refs[len(staged_out) :]
        in_sems, out_sems = refs
        io = Io(
            [(i, in_refs[i], cuts[i]) for i in staged_in],
            [(i, out_refs[i]) for i in staged_out],
            held_in, held_out, in_sems, out_sems,
        )
        for number, i in enumerate(staged_in):
            in_refs[i] = held_in[number]
        for number, i in enumerate(staged_out):
            out_refs[i] = held_out[number]
        body(io, in_refs, out_refs, *own)
        io.finish()

    args = [
        pltpu.with_memory_space_constraint(item[0], pltpu.HBM) if item[1] in ("far", "raw") else item[0]
        for item in ins
    ]
    return pl.pallas_call(
        kernel,
        out_shape=[pltpu.HBM(o.shape, o.dtype) if kind in ("far", "raw") else o for o, kind in outs],
        in_specs=[specs[item[1]] for item in ins],
        out_specs=[specs[kind] for _, kind in outs],
        scratch_shapes=[
            *scratch,
            *[held_shape(i) for i in staged_in],
            *[pltpu.VMEM(outs[i][0].shape, outs[i][0].dtype) for i in staged_out],
            pltpu.SemaphoreType.DMA((max(1, len(staged_in)),)),
            pltpu.SemaphoreType.DMA((max(1, len(staged_out)),)),
        ],
        input_output_aliases=aliases or {},
        compiler_params=pltpu.CompilerParams(vmem_limit_bytes=limit * MIB),
        cost_estimate=pl.CostEstimate(flops=cost, bytes_accessed=1, transcendentals=0),
        name=name,
    )(*args)


def far(*arrays):
    return [(array, "far") for array in arrays]


def norm_of(values):
    center = values - jnp.mean(values, axis=-1, keepdims=True)
    inverse = lax.rsqrt(jnp.mean(center * center, axis=-1, keepdims=True) + 1e-05)
    return center * inverse, inverse


def norm_back(upstream, normed, inverse, gain):
    scaled = upstream * gain
    return inverse * (
        scaled
        - jnp.mean(scaled, axis=-1, keepdims=True)
        - normed * jnp.mean(scaled * normed, axis=-1, keepdims=True)
    )


def fill_bias(plan, bias, seg_ref, pad_ref):
    length = bias.shape[0]
    row = pl.ds(lax.axis_index("seq"), 1)
    seg, pad = seg_ref[row, :], pad_ref[row, :]
    code = (2 * seg + pad).astype(F32)
    wanted = (2 * seg + 1).astype(F32)
    coded = jnp.broadcast_to(code, (length, length)).T
    rows = lax.broadcasted_iota(jnp.int32, (length, length), 0)
    cols = lax.broadcasted_iota(jnp.int32, (length, length), 1)
    bias[...] = jnp.where((coded == wanted) | (rows == cols), 0.0, -1e30)


def halves_of(values):
    lane = lax.broadcasted_iota(jnp.int32, values.shape, 1)
    zero = jnp.zeros_like(values)
    return jnp.where(lane < HD, values, zero), jnp.where(lane < HD, zero, values)


def prepare(plan, matrices, norm_params):
    side = jnp.pad(norm_params.T, ((0, 0), (0, 128 - norm_params.shape[0])))
    matrices = [*matrices[0:3], jnp.concatenate([side, side], axis=1), *matrices[3:]]
    groups = [matrices[0:4], matrices[4:6], matrices[6:7]]

    def body(io, ins, outs):
        io.start()
        core = lax.axis_index("seq") & 1
        first = 0
        for number, group in enumerate(groups):
            at = 0
            for index in range(first, first + len(group)):
                io.need(index)
                size = ins[index].shape[1] // 2
                left, right = ins[index][:, :size], ins[index][:, size:]
                mine = jnp.where(core == 0, left, right).astype(BF)
                other = jnp.where(core == 0, right, left).astype(BF)
                outs[2 * number][:, at : at + size] = mine
                outs[2 * number + 1][:, at : at + size] = other
                at += size
            first += len(group)

    outs = []
    for group in groups:
        outs += [(shape((group[0].shape[0], sum(w.shape[1] for w in group) // 2), BF), "near")] * 2
    flat_outs = call("prepare", body, far(*matrices), outs, [], 8)
    return flat_outs[0:2], flat_outs[2:4], flat_outs[4:6]


def other_rows(plan, arrays):
    others = plan.seq - 1

    def body(io, ins, outs, held, in_sems, out_sems):
        mine = lax.axis_index("seq")
        loads = [
            pltpu.make_async_copy(ins[i // others].at[mine ^ (i % others + 1)], held.at[i], in_sems.at[i])
            for i in range(len(outs))
        ]
        for load in loads:
            load.start()
        puts = [pltpu.make_async_copy(held.at[i], outs[i], out_sems.at[i]) for i in range(len(outs))]
        for load, put in zip(loads, puts):
            load.wait()
            put.start()
        for put in puts:
            put.wait()

    part = arrays[0].shape[1:]
    count = others * len(arrays)
    outs = call(
        "other_rows", body, [(a, "raw") for a in arrays], [(shape(part, BF), "raw")] * count,
        [pltpu.VMEM((count, *part), BF), pltpu.SemaphoreType.DMA((count,)), pltpu.SemaphoreType.DMA((count,))],
        8,
    )
    return [outs[i * others : (i + 1) * others] for i in range(len(arrays))]


def row_blocks(length):
    for i in range(length // 128):
        yield slice(i * 128, (i + 1) * 128)


def project(plan, tokens, parts):
    length = tokens[0].size // D if len(tokens) == 1 else tokens[1].shape[0] * len(tokens)
    width = 3 * D + 256
    pieces = [(3 * HALF, 128, 3 * D), *[(m * HALF, HALF, m * D) for m in range(3)]]

    def body(io, ins, outs, whole, rows_in, sems, put_sems):
        h_ref, q_ref, k_ref, v_ref, n_ref, w_ref, x_ref = outs
        start_parts(plan, ins[len(tokens) :], whole, sems, pieces)
        loads = load_bands(plan, ins[: len(tokens)], rows_in, sems.at[pl.ds(4, len(tokens))])
        wait_part(whole, sems, 0, pieces[0])
        norms = flat(whole[:, :, :, 3 * D : 3 * D + 128]).astype(F32).T[0:8]
        n_ref[...] = norms
        for load in loads:
            load.wait()
        puts = [pltpu.make_async_copy(rows_in, x_ref, put_sems.at[1])]
        puts[0].start()
        for rows in row_blocks(length):
            normed, _ = norm_of(rows_in[rows, :].astype(F32))
            h_ref[rows, :] = (normed * norms[0:1, :] + norms[1:2, :]).astype(BF)
        io.ship(0)
        for m in range(3):
            wait_part(whole, sems, 1 + m, pieces[1 + m])
        puts.append(pltpu.make_async_copy(whole, w_ref, put_sems.at[0]))
        puts[1].start()
        for m, (out, scale) in enumerate(((q_ref, 0.125), (k_ref, 1.0), (v_ref, 1.0))):
            weight = flat(whole[:, :, :, m * D : (m + 1) * D])
            out[...] = (dot(h_ref[...], weight, 1, 0) * scale).astype(BF)
            io.ship(1 + m)
        for put in puts:
            put.wait()

    act = shape((length, D), BF)
    wide = plan.wide(D, width)
    return call(
        "project", body, [*[(t, "any") for t in tokens], *[(p, "any") for p in parts]],
        [*[(act, "far")] * 4, (shape((8, D), F32), "near"), (shape(wide, BF), "raw"), (act, "raw")],
        [
            pltpu.VMEM(wide, BF), pltpu.VMEM((length, D), BF),
            pltpu.SemaphoreType.DMA((4 + len(tokens),)), pltpu.SemaphoreType.DMA((2,)),
        ],
        20, 1,
    )


def mix(plan, query, key, value, seg, pad):
    length = query.shape[0]

    def body(io, ins, outs, bias):
        q_ref, k_ref, v_ref, seg_ref, pad_ref = ins
        at_ref, a_ref, l_ref = outs
        io.start()
        fill_bias(plan, bias, seg_ref, pad_ref)
        io.need(0, 1, 2)

        @pl.loop(0, PAIRS, unroll=True)
        def _(p):
            cols = pl.ds(pl.multiple_of(p * 128, 128), 128)
            keys = k_ref[:, cols]
            turned = v_ref[:, cols].T
            for half, query in enumerate(halves_of(q_ref[:, cols])):
                scores = dot(keys, query, 1, 1) + bias[...]
                top = jnp.max(scores, axis=0, keepdims=True)
                lifted = jnp.exp(scores - top)
                total = jnp.sum(lifted, axis=0, keepdims=True)
                soft = (lifted * (1.0 / total)).astype(BF)
                mixed = dot(turned[half * HD : (half + 1) * HD], soft, 1, 0)
                at_ref[pl.ds(pl.multiple_of(p * 128 + half * HD, HD), HD), :] = mixed.astype(BF)
                l_ref[pl.ds(2 * p + half, 1), :] = top + jnp.log(total)
            a_ref[:, cols] = at_ref[pl.ds(pl.multiple_of(p * 128, 128), 128), :].T

    return call(
        "mix", body, [*far(query, key, value), (seg, "near"), (pad, "near")],
        [(shape((D, length), BF), "far"), (shape((length, D), BF), "far"), (shape((H, length), F32), "far")],
        [pltpu.VMEM((length, length), F32)],
        14,
    )


def widen(plan, tokens, mixed, norms, parts):
    length = tokens.shape[0]
    pieces = [(0, HALF, 0), (HALF, 2 * D, D)]

    def body(io, ins, outs, whole, sems, put_sems):
        x_ref, a_ref, n_ref, *part_refs = ins
        m_ref, h_ref, z_ref, s_ref, w_ref = outs
        io.start(1)
        start_parts(plan, part_refs, whole, sems, pieces[:1])
        io.start(0)
        start_parts(plan, part_refs, whole, sems.at[pl.ds(1, 1)], pieces[1:])
        io.need(0, 1)
        wait_part(whole, sems, 0, pieces[0])
        m_ref[...] = x_ref[...].astype(F32) + dot(a_ref[...], flat(whole[:, :, :, 0:D]), 1, 0)
        io.ship(0)
        for rows in row_blocks(length):
            normed, _ = norm_of(m_ref[rows, :])
            h_ref[rows, :] = (normed * n_ref[2:3, :] + n_ref[3:4, :]).astype(BF)
        io.ship(1)
        wait_part(whole, sems, 1, pieces[1])
        put = pltpu.make_async_copy(whole, w_ref, put_sems.at[0])
        put.start()
        for block in range(BLOCKS):
            cols = slice(block * D, (block + 1) * D)
            up = dot(h_ref[...], flat(whole[:, :, :, (block + 1) * D : (block + 2) * D]), 1, 0)
            bell = 0.5 + 0.5 * lax.erf(up * 0.7071067811865476)
            z_ref[:, cols] = (up * bell).astype(BF)
            s_ref[:, cols] = (bell + up * (jnp.exp(-0.5 * up * up) * 0.3989422804014327)).astype(BF)
            io.ship(2, pl.ds(block * D, D))
            io.ship(3, pl.ds(block * D, D))
        put.wait()

    act = shape((length, D), BF)
    wide = plan.wide(D, D + FF)
    hidden = shape((length, FF), BF)
    outs = [shape((length, D), F32), act, hidden, hidden]
    return call(
        "widen", body, [*far(tokens, mixed), (norms, "near"), *[(p, "any") for p in parts]],
        [*[(o, "far") for o in outs], (shape(wide, BF), "raw")],
        [pltpu.VMEM(wide, BF), pltpu.SemaphoreType.DMA((2,)), pltpu.SemaphoreType.DMA((1,))],
        28,
    )


def grad_of_down(plan, hidden, cot):
    length = hidden.shape[0]

    def body(io, ins, outs, g_in, z_in, sems, z_sems, put_sems, g_sem, held):
        z_ref, *bands = ins
        *grads, g_out = outs
        loads = load_bands(plan, bands, g_in, sems)
        z_loads = [
            pltpu.make_async_copy(z_ref.at[:, pl.ds(i * D, D)], z_in.at[:, pl.ds(i * D, D)], z_sems.at[i])
            for i in range(BLOCKS)
        ]
        for load in z_loads:
            load.start()
        for load in loads:
            load.wait()
        puts = [pltpu.make_async_copy(g_in, g_out, g_sem.at[0])]
        puts[0].start()
        for block in range(BLOCKS):
            z_loads[block].wait()
            tile = dot(z_in[:, block * D : (block + 1) * D], g_in[...], 0, 0)
            store_grad(plan, tile, held, FF, block * D, slice(None))
            view = (slice(None), pl.ds(block, 1)) if plan.fast else (pl.ds(block * D, D),)
            puts += put_grad(held, grads, put_sems.at[block], view, view)
        for put in puts:
            put.wait()

    act = shape((length, D), BF)
    grads = plan.grads(FF, D)
    return call(
        "grad_of_down", body, [(hidden, "raw"), *[(c, "any") for c in cot]],
        [*[(g, "raw") for g in grads], (act, "raw")],
        [
            pltpu.VMEM((length, D), BF), pltpu.VMEM((length, FF), BF),
            pltpu.SemaphoreType.DMA((len(cot),)), pltpu.SemaphoreType.DMA((BLOCKS,)),
            pltpu.SemaphoreType.DMA((BLOCKS, len(grads))), pltpu.SemaphoreType.DMA((1,)),
            held_grad(plan, FF, D),
        ],
        28,
    )


def narrow(plan, blocks, mid, below, grads, low, hidden, slope, cot, whole_ou, parts_down):
    length = mid.shape[0]
    count = len(blocks)
    start, final = blocks[0] == 0, blocks[-1] == BLOCKS - 1
    cut = (blocks[0] * D, count * D)
    n_out = plan.outs()

    def body(io, ins, outs, *scratch):
        m_ref, h_ref, z_ref, s_ref, g_ref, up_ref, *rest = ins
        downs = rest[: len(parts_down)]
        b_ref, *grad_refs = outs[: 1 + n_out]
        o_refs = outs[1 + n_out :]
        held, du_ref, acc, whole_up, whole_down, sems, put_sems = scratch
        copies = []
        down = (0, HALF, 0)
        io.start(4)
        start_parts(plan, downs, whole_down, sems.at[pl.ds(0, 1)], [down], blocks)
        io.start(3, 1)
        up = pltpu.make_async_copy(up_ref.at[..., pl.ds(D + cut[0], cut[1])], whole_up, sems.at[1])
        up.start()
        io.start()
        io.need(4)
        wait_part(whole_down, sems, 0, down)
        io.need(3, 1)
        for number, block in enumerate(blocks):
            local = slice(number * D, (number + 1) * D)
            back = dot(g_ref[...], flat(whole_down[number]), 1, 1)
            du_ref[:, local] = (back * s_ref[:, local]).astype(BF)
            tile = dot(h_ref[...], du_ref[:, local], 0, 0)
            store_grad(plan, tile, held, D, 0, local)
            views = [(*[slice(None)] * (plan.grads(D, D)[0].ndim - 1), pl.ds(at * D, D)) for at in (number, block)]
            copies += put_grad(held, grad_refs, put_sems.at[number], *views)
        up.wait()
        lower = dot(du_ref[...], flat(whole_up[...]), 1, 1)
        if start:
            b_ref[...] = lower
        else:
            io.need(6 + len(parts_down))
            b_ref[...] = rest[len(parts_down)][...] + lower
        io.ship(0)
        io.need(0, 2)
        gain = m_ref[...] + dot(z_ref[...], whole_down[...].reshape(count * D, D), 1, 0)
        if final:
            acc[...] = gain
            for number, o_ref in enumerate(o_refs):
                o_ref[...] = acc[band(plan, number, length), :].astype(BF)
        else:
            o_refs[0][...] = gain
        for copy in copies:
            copy.wait()

    deep = plan.wide(FF, D)
    ins = [
        *far(mid, low), (hidden, "far", cut), (slope, "far", cut), *far(cot), (whole_ou, "raw"),
        *[(p, "any") for p in parts_down],
    ]
    aliases = {}
    if not start:
        ins += far(below)
        aliases = {len(ins) + i: 1 + i for i in range(n_out)}
        ins += [(g, "raw") for g in grads]
    return call(
        "narrow" + str(blocks[0]), body, ins,
        [
            (shape((length, D), F32), "far"), *[(g, "raw") for g in plan.grads(D, FF)],
            *[(o, "far") for o in (plan.band_shapes(length) if final else [shape((length, D), F32)])],
        ],
        [
            held_grad(plan, D, count * D),
            pltpu.VMEM((length, count * D), BF),
            pltpu.VMEM((length, D), F32),
            pltpu.VMEM(plan.wide(D, count * D), BF),
            pltpu.VMEM((count, *deep[1:]), BF),
            pltpu.SemaphoreType.DMA((2,)),
            pltpu.SemaphoreType.DMA((count, n_out)),
        ],
        40, aliases=aliases,
    )


def turn(plan, mid, back, cot, norms, whole_ou):
    length = mid.shape[0]

    def body(io, ins, outs, whole, sems):
        m_ref, b_ref, g_ref, n_ref, w_ref = ins
        x_ref, low, d_ref, s_ref = outs
        io.start()
        load = pltpu.make_async_copy(w_ref.at[..., pl.ds(0, D)], whole, sems.at[0])
        load.start()
        s_ref[...] = jnp.zeros_like(s_ref)
        io.need(0, 1, 2)
        for rows in row_blocks(length):
            normed, inverse = norm_of(m_ref[rows, :])
            upstream = b_ref[rows, :]
            total = g_ref[rows, :].astype(F32) + norm_back(upstream, normed, inverse, n_ref[2:3, :])
            x_ref[rows, :] = total
            low[rows, :] = total.astype(BF)
            s_ref[0:1, :] += jnp.sum(upstream * normed, axis=0, keepdims=True)
            s_ref[1:2, :] += jnp.sum(upstream, axis=0, keepdims=True)
        io.ship(0)
        io.ship(1)
        load.wait()
        d_ref[...] = dot(low[...], flat(whole[...]), 1, 1).astype(BF)

    act = shape((length, D), BF)
    return call(
        "turn", body, [*far(mid, back, cot), (norms, "near"), (whole_ou, "raw")],
        [(shape((length, D), F32), "far"), (act, "far"), (act, "far"), (shape((2, D), F32), "near")],
        [pltpu.VMEM(plan.wide(D, D), BF), pltpu.SemaphoreType.DMA((1,))],
        24,
    )


def attend_back(plan, side, low, query, key, value, lse, cot, seg, pad, extra=()):
    length = low.shape[0]
    width = 3 * HALF + (D if extra else 0)
    cut = (side * HALF, HALF)

    def body(io, ins, outs, bias, held, put_sems):
        h_ref, q_ref, k_ref, v_ref, c_ref, l_ref, seg_ref, pad_ref, *more = ins
        d_ref, *grads = outs
        io.start(1, 2, 3, 4, 5)
        io.start()
        fill_bias(plan, bias, seg_ref, pad_ref)
        io.need(1, 2, 3, 4, 5)

        @pl.loop(0, PAIRS // 2)
        def _(local):
            p = local + side * (PAIRS // 2)
            first = pl.multiple_of(local * 128, 128)
            cols = pl.ds(first, 128)
            keys, values = k_ref[:, cols], v_ref[:, cols]
            turned = keys.T
            queries, cots = halves_of(q_ref[:, cols]), halves_of(c_ref[:, cols])
            dv = dk = None
            dqs = []
            for half in range(2):
                scores = dot(keys, queries[half], 1, 1) + bias[...]
                soft = jnp.exp(scores - l_ref[pl.ds(2 * p + half, 1), :])
                gain = dot(soft.astype(BF), cots[half], 1, 0)
                dv = gain if dv is None else dv + gain
                dp = dot(values, cots[half], 1, 1)
                share = jnp.sum(soft * dp, axis=0, keepdims=True)
                ds = (soft * (dp - share)).astype(BF)
                gain = dot(ds, queries[half], 1, 0)
                dk = gain if dk is None else dk + gain
                dqs.append(dot(turned[half * HD : (half + 1) * HD], ds, 1, 0) * 0.125)
            d_ref[:, cols] = jnp.concatenate(dqs, axis=0).T.astype(BF)
            d_ref[:, pl.ds(first + HALF, 128)] = dk.astype(BF)
            d_ref[:, pl.ds(first + 2 * HALF, 128)] = dv.astype(BF)

        io.ship(0)
        io.need(0)
        lead, copies = [slice(None)] * (len(grads[0].shape) - 1), []
        if extra:
            io.need(8, 9)
            tile = dot(more[0][...], more[1][...], 1, 0)
            store_grad(plan, tile, held, D, 0, slice(3 * HALF, width))
            view = (*lead, pl.ds(3 * HALF, D))
            copies += put_grad(held, grads, put_sems.at[3], view, view)
        for m in range(3):
            cols = slice(m * HALF, (m + 1) * HALF)
            store_grad(plan, dot(h_ref[...], d_ref[:, cols], 0, 0), held, D, 0, cols)
            view = (*lead, pl.ds(m * HALF, HALF))
            copies += put_grad(held, grads, put_sems.at[m], view, view)
        for copy in copies:
            copy.wait()

    return call(
        "attend_back" + str(side), body,
        [
            *far(low), *[(a, "far", cut) for a in (query, key, value, cot)], *far(lse),
            (seg, "near"), (pad, "near"), *far(*extra),
        ],
        [(shape((length, 3 * HALF), BF), "far"), *[(g, "raw") for g in plan.grads(D, width)]],
        [
            pltpu.VMEM((length, length), F32), held_grad(plan, D, width),
            pltpu.SemaphoreType.DMA((4, plan.outs())),
        ],
        26,
    )


def finish_tokens(plan, tokens, spreads, mid_cot, norms, whole_qkv):
    length = tokens.shape[0]

    def body(io, ins, outs, back, whole, sems):
        x_ref, d0_ref, d1_ref, c_ref, n_ref, w_ref = ins
        *o_refs, s_ref = outs
        io.start(1, 2)
        load = pltpu.make_async_copy(w_ref.at[..., pl.ds(0, 3 * D)], whole, sems.at[0])
        load.start()
        io.start()
        s_ref[...] = jnp.zeros_like(s_ref)
        io.need(1, 2)
        load.wait()
        back[...] = sum(
            dot(
                jnp.concatenate([d[:, m * HALF : (m + 1) * HALF] for d in (d0_ref, d1_ref)], axis=1),
                flat(whole[:, :, :, m * D : (m + 1) * D]), 1, 1,
            )
            for m in range(3)
        )
        io.need(0, 3)
        for rows in row_blocks(length):
            normed, inverse = norm_of(x_ref[rows, :].astype(F32))
            upstream = back[rows, :]
            c_ref[rows, :] += norm_back(upstream, normed, inverse, n_ref[0:1, :])
            s_ref[0:1, :] += jnp.sum(upstream * normed, axis=0, keepdims=True)
            s_ref[1:2, :] += jnp.sum(upstream, axis=0, keepdims=True)
        for number, o_ref in enumerate(o_refs):
            o_ref[...] = c_ref[band(plan, number, length), :].astype(BF)

    return call(
        "finish_tokens", body, [*far(tokens, *spreads, mid_cot), (norms, "near"), (whole_qkv, "raw")],
        [*[(o, "far") for o in plan.band_shapes(length)], (shape((2, D), F32), "near")],
        [pltpu.VMEM((length, D), F32), pltpu.VMEM(plan.wide(D, 3 * D), BF), pltpu.SemaphoreType.DMA((1,))],
        20, 1,
    )


def sum_up(plan, blocks, others, slices):
    nz, rows, columns = blocks.shape
    wide = 4 * D // plan.count

    def body(io, ins, outs, held, sems):
        blocks_ref, others_ref, slice_ref = ins
        g_ref, card_ref = outs
        loads = [pltpu.make_async_copy(blocks_ref.at[i], held.at[i], sems.at[i]) for i in range(nz)]
        for load in loads:
            load.start()
        for load in loads:
            load.wait()
        value = jnp.sum(held[...].astype(F32), axis=0)
        g_ref[...] = value
        left = jnp.sum(jnp.sum(value * value, axis=0, keepdims=True), axis=1, keepdims=True) + others_ref[0:1, 0:1]
        lane = lax.broadcasted_iota(jnp.int32, slice_ref.shape, 1)
        card = slice_ref[...]
        for i in range(3):
            piece = left.astype(BF).astype(F32)
            card = jnp.where(lane == wide + i, piece, card)
            left = left - piece
        card = card.astype(BF)
        for i in range(plan.count):
            card_ref[i] = card

    return call(
        "sum_up", body, [(blocks, "any"), (others, "near"), (slices, "near")],
        [(shape((rows, columns), F32), "near"), (shape((plan.count, *slices.shape), BF), "near")],
        [pltpu.VMEM(blocks.shape, BF), pltpu.SemaphoreType.DMA((nz,))], 8,
    )


def update(plan, grads, cards, masters, firsts, seconds, passed):
    rates = [D**-0.5] * 3 + [4.0 * D**-0.5, D**-0.5, FF**-0.5, 0.2]
    decays = [0.01] * 6 + [0.0]
    count = len(masters)
    given = len(grads)

    def body(io, ins, outs, total, sems):
        grad_refs, card_ref = ins[:given], ins[given]
        first = given + 1
        io.start(*(first + k * count + i for i in reversed(range(count)) for k in range(3)))
        io.start()
        total[...] = jnp.sum(card_ref[...].astype(F32), axis=0)
        rows, wide = total.shape[0], 4 * D // plan.count
        all_norms = total[...]
        lane = lax.broadcasted_iota(jnp.int32, all_norms.shape, 1)
        own = jnp.where(lane < wide, all_norms * all_norms, all_norms * (1.0 / rows))
        square = jnp.sum(jnp.sum(own, axis=0, keepdims=True), axis=1, keepdims=True)
        norm = jnp.sqrt(square)
        outs[0][...] = jnp.broadcast_to(norm, outs[0].shape)
        factor = jnp.minimum(1.0, clip_limit / (norm + 1e-06))
        mine = total[pl.ds(lax.axis_index("dp") * plan.seq + lax.axis_index("seq"), 1), :]
        each = wide // 4
        grad_norms = jnp.concatenate([mine[:, p * each : (p + 1) * each] for p in range(4)], axis=0)
        for i in reversed(range(count)):
            w_ref, m_ref, s_ref = (ins[first + k * count + i] for k in range(3))
            io.need(*(first + k * count + i for k in range(3)))
            if i < 3:
                cols = [
                    (slice(h * HALF, (h + 1) * HALF), grad_refs[0][:, (5 * h + i) * HALF : (5 * h + i + 1) * HALF])
                    for h in range(2)
                ]
            elif i == 3:
                cols = [(slice(None), grad_refs[0][:, 3 * HALF : 5 * HALF])]
            elif i < 6:
                cols = [(slice(None), grad_refs[i - 3][...])]
            else:
                cols = [(slice(None), grad_norms)]
            for where, grad in cols:
                clipped = factor * grad
                one = 0.5 * m_ref[:, where] + 0.5 * clipped
                two = 0.55 * s_ref[:, where] + 0.45 * clipped * clipped
                root = jnp.sqrt(two * (1.0 / (1.0 - 0.55**STEP))) + 1e-08
                weight = w_ref[:, where]
                step = (one * (1.0 / (1.0 - 0.5**STEP))) / root + decays[i] * weight
                outs[1 + i][:, where] = weight - rates[i] * step
                outs[1 + count + i][:, where] = one
                outs[1 + 2 * count + i][:, where] = two
            for k in range(3):
                io.ship(1 + k * count + i)
        last = first + 3 * count
        copies = []
        for number in range(len(passed)):
            which, place_in = number // plan.bands(), number % plan.bands()
            io.need(last + number)
            target = outs[1 + 3 * count + which]
            if plan.bands() > 1:
                target = target.at[lax.axis_index("seq") ^ place_in]
            copies.append(pltpu.make_async_copy(ins[last + number], target, sems.at[number]))
            copies[-1].start()
        for copy in copies:
            copy.wait()

    like = [(shape(w.shape, F32), "far") for w in masters] * 3
    pieces = [shape((plan.bands(), *p.shape), BF) if plan.bands() > 1 else p for p in passed[:: plan.bands()]]
    return call(
        "update", body, [*[(g, "near") for g in grads], (cards, "near"), *far(*masters, *firsts, *seconds, *passed)],
        [(shape((1, 128), F32), "near"), *like, *[(o, "raw") for o in pieces]],
        [pltpu.VMEM(cards.shape[1:], F32), pltpu.SemaphoreType.DMA((len(passed),))], 20,
    )


def after(values, *others):
    return lax.optimization_barrier((values, others))[0]


def meet(*values):
    return lax.optimization_barrier(values)


def send(plan, values, perm):
    return lax.ppermute(values, AXES, perm)


def block_of(plan, mine, other):
    core = lax.axis_index("seq") & 1
    got = send(plan, other, plan.core)
    return jnp.where(core == 0, jnp.concatenate([mine, got]), jnp.concatenate([got, mine]))


def copies_of(plan, block):
    return jnp.broadcast_to(block[None], (plan.nz, *block.shape))


def along_z(plan, values):
    return lax.all_to_all(values, "dp", 0, 0, axis_index_groups=plan.groups, tiled=True)


def gather_whole(matrices):
    split = [w.reshape(w.shape[0], 2, -1) for w in matrices]
    halves = jnp.concatenate(split, axis=2).transpose(1, 0, 2).astype(BF)
    full = lax.all_gather(halves, AXES, axis=1, tiled=True)
    return [full.reshape(2, BLOCKS, 1, -1, full.shape[-1])]


def add(one, two):
    return one.astype(F32) + two.astype(F32)


def fold(keep, got):
    if keep.ndim == 4:
        keep, got = (v.reshape(-1, *v.shape[2:]) for v in (keep, got))
    size = keep.shape[0] // 2
    return add(keep[size:], got[size:]).astype(BF), add(keep[:size], got[:size]).astype(BF)


def total(blocks):
    return jnp.sum(blocks.astype(F32), axis=0)


def finish(plan, grads, sums, masters, firsts, seconds, *passed):
    wide = sums.shape[0] * D // plan.count
    slices = sums.reshape(sums.shape[0], plan.count, -1).transpose(1, 0, 2).reshape(plan.count, wide)
    slices = jnp.pad(slices, ((0, 0), (0, 128 - wide)))
    if plan.fast:
        blocks, *others = grads
        left = jnp.broadcast_to(sum(jnp.sum(g * g) for g in others), (1, 128))
        left, slices, blocks, early = meet(left, slices, blocks, passed[:-1])
        passed = [*early, passed[-1]]
        last, cards = sum_up(plan, blocks, left, slices)
        grads = [last, *others]
        cards = lax.all_to_all(cards, AXES, 0, 0, tiled=True)
    else:
        left = jnp.broadcast_to(sum(jnp.sum(g * g) for g in grads), (plan.count, 1))
        cards = lax.psum(slices + jnp.pad(left, ((0, 0), (wide, 127 - wide))), AXES)[None]
    norm, *updated, output, input_grad = update(plan, grads, cards, masters, firsts, seconds, passed)
    return (output, input_grad, norm[0, 0], *updated)


def on_device(plan, *args):
    tokens_in, segment_ids, pad_mask, out_grad = args[:4]
    masters, firsts, seconds = args[4:11], args[11:18], args[18:25]
    each, piece, _ = tokens_in.shape
    length = each // plan.seq * plan.seq * piece

    plan.fast = plan.fast and each == plan.seq

    def swap(values, number):
        return lax.ppermute(values, "seq", [(i, i ^ number) for i in range(plan.seq)])

    def to_rows(values, others=None):
        if not plan.fast:
            return [lax.all_to_all(values, "seq", 0, 0, tiled=True).reshape(length, D)]
        return [values, *[swap(other, 1 + n) for n, other in enumerate(others)]]

    def to_pieces(bands):
        if not plan.fast:
            return [lax.all_to_all(bands[0].reshape(each, piece, D), "seq", 0, 0, tiled=True)]
        return [bands[0], *[swap(other, 1 + n) for n, other in enumerate(bands[1:])]]

    seg, pad = segment_ids, pad_mask

    if not plan.fast:
        side = jnp.pad(masters[6].T, ((0, 0), (0, 124)))
        side = jnp.concatenate([side, side], axis=1)
        one, two, three = (gather_whole(m) for m in ([*masters[0:3], side], masters[3:5], masters[5:6]))
        low_one, query, key, value, norms, whole_qkv, tokens = project(plan, to_rows(tokens_in), one)
        mixed_t, mixed, lse = mix(plan, query, key, value, seg, pad)
        mid, low_two, hidden, slope, whole_ou = widen(plan, tokens, mixed, norms, two)
        *g_down, cot = grad_of_down(plan, hidden, to_rows(out_grad))
        back, *g_up, part = narrow(plan, (0, 1), mid, None, None, low_two, hidden, slope, cot, whole_ou, three)
        back, *g_up, result = narrow(plan, (2, 3), part, back, g_up, low_two, hidden, slope, cot, whole_ou, three)
        mid_cot, low_cot, mixed_cot, sums_two = turn(plan, mid, back, cot, norms, whole_ou)
        halves = [
            attend_back(plan, side, low_one, query, key, value, lse, mixed_cot, seg, pad, extra)
            for side, extra in enumerate(((mixed_t, low_cot), ()))
        ]
        stream, sums_one = finish_tokens(plan, tokens, [h[0] for h in halves], mid_cot, norms, whole_qkv)
        grads = [
            lax.psum_scatter(g.astype(F32), AXES, scatter_dimension=0, tiled=True)
            for g in (halves[0][1], halves[1][1], *g_up, *g_down)
        ]
        grads = [jnp.concatenate(grads[:2], axis=1), *grads[2:]]
        sums = jnp.concatenate([sums_one, sums_two], axis=0)
        return finish(plan, grads, sums, masters, firsts, seconds, *to_pieces([result]), *to_pieces([stream]))

    first, second, third = prepare(plan, masters[:6], masters[6])
    block = block_of(plan, *first)
    near_one = along_z(plan, copies_of(plan, block))
    others, others_cot = other_rows(plan, [after(tokens_in, block), out_grad])
    tokens = to_rows(tokens_in, others)
    block_two = block_of(plan, *second)
    spread_two = copies_of(plan, block_two)
    spread_three = copies_of(plan, block_of(plan, *third))
    near_one, tokens, spread_two, spread_three = meet(near_one, tokens, spread_two, spread_three)

    def spread(near):
        return send(plan, near, plan.second), send(plan, near, plan.first)

    def to_core(*parts):
        return [send(plan, part, plan.core) for part in parts]

    beside_one, across_one = spread(near_one)
    near_two = along_z(plan, spread_two)
    beside_one, across_one = meet(beside_one, across_one)
    corner_one = send(plan, beside_one, plan.first)
    one = [near_one, beside_one, across_one]
    one_core = to_core(*one)
    corner_one, one_core = meet(corner_one, one_core)
    one = [*one, corner_one, *one_core, *to_core(corner_one)]
    low_one, query, key, value, norms, whole_qkv, tokens = project(plan, tokens, one)
    cot = to_rows(out_grad, after(others_cot, corner_one))
    near_two, query, cot = meet(near_two, query, cot)
    beside_two, across_two = spread(near_two)
    near_three = along_z(plan, after(spread_three, near_two))
    mixed_t, mixed, lse = mix(plan, query, key, value, seg, pad)
    beside_two, across_two, near_three, mixed, lse, mixed_t = meet(
        beside_two, across_two, near_three, mixed, lse, mixed_t
    )
    corner_two = send(plan, beside_two, plan.first)
    beside_three, across_three = spread(near_three)
    two = [near_two, beside_two, across_two]
    two_core = to_core(*two)
    corner_two, two_core = meet(corner_two, two_core)
    two = [*two, corner_two, *two_core, *to_core(corner_two)]
    mid, low_two, hidden, slope, whole_ou = widen(plan, tokens, mixed, norms, two)
    beside_three, across_three, hidden = meet(beside_three, across_three, hidden)
    corner_three = send(plan, beside_three, plan.first)
    three = [near_three, beside_three, across_three]
    three_core = to_core(*three)
    keep_d, go_d, cot = grad_of_down(plan, hidden, cot)
    corner_three, three_core, keep_d, go_d, cot = meet(corner_three, three_core, keep_d, go_d, cot)
    three = [*three, corner_three, *three_core, *to_core(corner_three)]

    got_d = send(plan, go_d, plan.core)
    back, *g_up, part = narrow(plan, (0, 1), mid, None, None, low_two, hidden, slope, cot, whole_ou, three)
    got_d, back, part = meet(got_d, back, part)
    go_d, keep_d = fold(keep_d, got_d)
    got_d = send(plan, go_d, plan.first)
    part = after(part, go_d)
    back, *rest = narrow(plan, (2, 3), part, back, g_up, low_two, hidden, slope, cot, whole_ou, three)
    got_d, back, rest = meet(got_d, back, rest)
    (keep_u, go_u), result = rest[:2], rest[2:]
    got_u = send(plan, go_u, plan.core)
    go_d, keep_d = fold(keep_d, got_d)
    got_d = send(plan, go_d, plan.second)
    back = after(back, go_d)
    mid_cot, low_cot, mixed_cot, sums_two = turn(plan, mid, back, cot, norms, whole_ou)
    got_u, mixed_cot, low_cot, mid_cot, result = meet(got_u, mixed_cot, low_cot, mid_cot, result)
    go_u, keep_u = fold(keep_u, got_u)
    got_d, go_u = meet(got_d, go_u)
    got_u = send(plan, go_u, plan.first)
    mixed_cot = after(mixed_cot, go_u)
    spread_a, keep_a, go_a = attend_back(
        plan, 0, low_one, query, key, value, lse, mixed_cot, seg, pad, (mixed_t, low_cot)
    )
    got_u, keep_a, spread_a = meet(got_u, keep_a, spread_a)
    got_a = send(plan, go_a, plan.core)
    block_d = add(keep_d, got_d).astype(BF)
    blocks_d = along_z(plan, block_d)
    go_u, keep_u = fold(keep_u, got_u)
    got_u = send(plan, go_u, plan.second)
    go_a, keep_a = fold(keep_a, got_a)
    got_a = send(plan, go_a, plan.first)
    mixed_cot = after(mixed_cot, go_u, go_a, block_d)
    spread_b, keep_b, go_b = attend_back(plan, 1, low_one, query, key, value, lse, mixed_cot, seg, pad)
    blocks_d, got_u, got_a, go_b, keep_b, spread_b = meet(blocks_d, got_u, got_a, go_b, keep_b, spread_b)
    got_b = send(plan, go_b, plan.core)
    block_u = add(keep_u, got_u).astype(BF)
    blocks_u = along_z(plan, block_u)
    go_b, keep_b = fold(keep_b, after(got_b, block_u))
    got_b = send(plan, go_b, plan.first)
    go_a, keep_a = fold(keep_a, after(got_a, go_b))
    got_a = send(plan, go_a, plan.second)
    mid_cot = after(mid_cot, go_a, go_b)
    *stream, sums_one = finish_tokens(plan, tokens, [spread_a, spread_b], mid_cot, norms, whole_qkv)
    got_b, sums_one, stream = meet(got_b, sums_one, stream)
    go_b, keep_b = fold(keep_b, got_b)
    got_b = send(plan, go_b, plan.second)
    got_a = after(got_a, go_b)
    output = to_pieces(after(result, go_b))
    input_grad = to_pieces(after(stream, go_b))
    halves = [add(keep_a, got_a), add(keep_b, got_b)]
    blocks_ab = along_z(plan, jnp.concatenate(halves, axis=2).astype(BF))
    grads = [blocks_ab, total(blocks_u), total(blocks_d)]
    sums = jnp.concatenate([sums_one, sums_two], axis=0)
    return finish(plan, grads, sums, masters, firsts, seconds, *output, *input_grad)


def solution(mesh):
    plan = Plan(mesh, None)
    rows = P(AXES, None)
    weights = (*[rows] * 6, P(None, AXES))
    tokens = P("dp", "seq", None)
    return jax.shard_map(
        partial(on_device, plan),
        mesh=mesh,
        in_specs=(tokens, P("dp", None), P("dp", None), tokens, *weights * 3),
        out_specs=(tokens, tokens, P(), *weights * 3),
        check_vma=False,
    )
```

```python
from functools import partial

import jax
import jax.numpy as jnp
from jax import lax
from jax.experimental import pallas as pl
from jax.experimental.pallas import tpu as pltpu
from jax.sharding import PartitionSpec as P

D = 768
H = 12
HD = 64
FF = 3072
STEP = 7
HALF = D // 2
PAIRS = H // 2
BLOCKS = 4
BF = jnp.bfloat16
F32 = jnp.float32
AXES = ("dp", "seq")
clip_limit = 1.0
MIB = 2**20

VM = pl.BlockSpec(memory_space=pltpu.VMEM)
ANY = pl.BlockSpec(memory_space=pl.ANY)
FAR = pl.BlockSpec(memory_space=pltpu.HBM)


def dot(left, right, left_dim, right_dim):
    return lax.dot_general(
        left, right, (((left_dim,), (right_dim,)), ((), ())), preferred_element_type=F32
    )


def shape(dims, kind):
    return jax.ShapeDtypeStruct(dims, kind)


class Plan:
    def __init__(self, mesh, rows_each):
        self.dp = mesh.shape["dp"]
        self.seq = mesh.shape["seq"]
        self.count = self.dp * self.seq
        self.fast = (
            self.seq == 4
            and self.dp % 2 == 0
            and BLOCKS * 8 == self.count
            and (2 * D // self.count) % 16 == 0
        )
        self.nz = self.dp // 2
        self.rows = D // self.count
        self.far = FF // self.count
        both = range(self.count)
        self.core = [(d, d ^ 1) for d in both]
        self.first = [(d, d ^ (2 if d % 2 == 0 else 4)) for d in both]
        self.second = [(d, d ^ (4 if d % 2 == 0 else 2)) for d in both]
        self.groups = [list(range(low, self.dp, 2)) for low in range(2)]

    def wide(self, rows, columns):
        if self.fast:
            return (self.nz, 4, 2 * rows // self.count, columns)
        return (BLOCKS, 1, rows // BLOCKS, columns)

    def parts(self):
        return 8 if self.fast else 1

    def grads(self, rows, columns):
        if self.fast:
            half = shape((4, self.nz, rows // self.count, columns), BF)
            return [half, half]
        return [shape((rows, columns), BF)]

    def outs(self):
        return 2 if self.fast else 1

    def bands(self):
        return self.seq if self.fast else 1

    def band_shapes(self, length):
        return [shape((length // self.bands(), D), BF)] * self.bands()


def place():
    seq = lax.axis_index("seq")
    return seq & 1, seq >> 1, lax.axis_index("dp") & 1


def start_parts(plan, parts, whole, sems, pieces, blocks=None):
    blocks = slice(None) if blocks is None else pl.ds(blocks[0], len(blocks))
    for index, (first, size, to) in enumerate(pieces):
        columns = pl.ds(first, size)
        if len(parts) == 1:
            for half in range(2):
                pltpu.make_async_copy(
                    parts[0].at[half, blocks, :, :, columns], whole.at[..., pl.ds(to + half * size, size)], sems.at[index]
                ).start()
            continue
        core, mine_x, mine_y = place()
        for number, part in enumerate(parts):
            owner = core if number < 4 else 1 - core
            one, two = (number >> 1) & 1, number & 1
            off_x = jnp.where(owner == 0, one, two)
            off_y = jnp.where(owner == 0, two, one)
            spot = (mine_y ^ off_y) * 2 + (mine_x ^ off_x)
            target = pl.ds(pl.multiple_of(to + owner * size, 128), size)
            pltpu.make_async_copy(part.at[blocks, :, columns], whole.at[:, spot, :, target], sems.at[index]).start()


def wait_part(whole, sems, index, piece):
    view = whole.at[..., pl.ds(piece[2], 2 * piece[1])]
    pltpu.make_async_copy(view, view, sems.at[index]).wait()


def band(plan, number, length):
    if plan.bands() == 1:
        return pl.ds(0, length)
    size = length // plan.bands()
    return pl.ds(pl.multiple_of((lax.axis_index("seq") ^ number) * size, size), size)


def load_bands(plan, refs, whole, sems):
    copies = []
    for number, ref in enumerate(refs):
        source = ref.at[lax.axis_index("seq")] if number == 0 and plan.bands() > 1 else ref
        target = whole.at[band(plan, number, whole.shape[0]), :]
        copies.append(pltpu.make_async_copy(source, target, sems.at[number]))
    for copy in copies:
        copy.start()
    return copies


def flat(value):
    return value.reshape(-1, value.shape[-1])


def held_grad(plan, rows, columns):
    one = plan.grads(rows, columns)
    return pltpu.VMEM((len(one), *one[0].shape), BF)


def put_grad(held, outs, sems, held_view, out_view):
    copies = [
        pltpu.make_async_copy(held.at[(i, *held_view)], out.at[out_view], sems.at[i]) for i, out in enumerate(outs)
    ]
    for copy in copies:
        copy.start()
    return copies


def store_grad(plan, tile, held, rows, first_row, columns):
    if not plan.fast:
        held[0, pl.ds(first_row, tile.shape[0]), columns] = tile.astype(BF)
        return
    core, mine_x, mine_y = place()
    step = rows // plan.count

    def spot(pair, owner):
        off_x = (pair & 1) ^ mine_x
        off_y = ((pair >> 1) & 1) ^ mine_y
        return (off_x * 2 + off_y if owner == 0 else off_y * 2 + off_x), pair >> 2

    for local in range(tile.shape[0] // (2 * step)):
        pair = first_row // (2 * step) + local
        low = tile[2 * step * local : 2 * step * local + step]
        high = tile[2 * step * local + step : 2 * step * (local + 1)]
        held[core, *spot(pair, 0), :, columns] = low.astype(BF)
        held[1 - core, *spot(pair, 1), :, columns] = high.astype(BF)


class Io:
    def __init__(self, ins, outs, held_in, held_out, in_sems, out_sems):
        self.loads, self.running = {}, []
        for number, (index, ref, cut) in enumerate(ins):
            source = ref if cut is None else ref.at[:, pl.ds(*cut)]
            self.loads[index] = pltpu.make_async_copy(source, held_in[number], in_sems.at[number])
        self.outs = {
            index: (held_out[number], ref, out_sems.at[number]) for number, (index, ref) in enumerate(outs)
        }
        self.shipped = []

    def start(self, *indices):
        for index in indices or [i for i in self.loads if i not in self.running]:
            self.loads[index].start()
            self.running.append(index)

    def need(self, *indices):
        for index in indices:
            self.loads.pop(index).wait()

    def ship(self, index, columns=None):
        held, ref, sem = self.outs[index]
        if columns is None:
            pltpu.make_async_copy(held, ref, sem).start()
        else:
            pltpu.make_async_copy(held.at[..., columns], ref.at[..., columns], sem).start()
        if index not in self.shipped:
            self.shipped.append(index)

    def finish(self):
        self.need(*list(self.loads))
        for index in self.outs:
            if index not in self.shipped:
                self.ship(index)
        for held, ref, sem in self.outs.values():
            pltpu.make_async_copy(held, ref, sem).wait()


def call(name, body, ins, outs, scratch, limit, cost=10**11, aliases=None):
    staged_in = [i for i, item in enumerate(ins) if item[1] == "far"]
    staged_out = [i for i, item in enumerate(outs) if item[1] == "far"]
    cuts = {i: (ins[i][2] if len(ins[i]) > 2 else None) for i in staged_in}

    def held_shape(i):
        array = ins[i][0]
        dims = array.shape if cuts[i] is None else (array.shape[0], cuts[i][1])
        return pltpu.VMEM(dims, array.dtype)

    specs = {"near": VM, "far": FAR, "raw": FAR, "any": ANY}
    n_in, n_out, n_scratch = len(ins), len(outs), len(scratch)

    def kernel(*refs):
        in_refs, refs = list(refs[:n_in]), refs[n_in:]
        out_refs, refs = list(refs[:n_out]), refs[n_out:]
        own, refs = refs[:n_scratch], refs[n_scratch:]
        held_in, refs = refs[: len(staged_in)], refs[len(staged_in) :]
        held_out, refs = refs[: len(staged_out)], refs[len(staged_out) :]
        in_sems, out_sems = refs
        io = Io(
            [(i, in_refs[i], cuts[i]) for i in staged_in],
            [(i, out_refs[i]) for i in staged_out],
            held_in, held_out, in_sems, out_sems,
        )
        for number, i in enumerate(staged_in):
            in_refs[i] = held_in[number]
        for number, i in enumerate(staged_out):
            out_refs[i] = held_out[number]
        body(io, in_refs, out_refs, *own)
        io.finish()

    args = [
        pltpu.with_memory_space_constraint(item[0], pltpu.HBM) if item[1] in ("far", "raw") else item[0]
        for item in ins
    ]
    return pl.pallas_call(
        kernel,
        out_shape=[pltpu.HBM(o.shape, o.dtype) if kind in ("far", "raw") else o for o, kind in outs],
        in_specs=[specs[item[1]] for item in ins],
        out_specs=[specs[kind] for _, kind in outs],
        scratch_shapes=[
            *scratch,
            *[held_shape(i) for i in staged_in],
            *[pltpu.VMEM(outs[i][0].shape, outs[i][0].dtype) for i in staged_out],
            pltpu.SemaphoreType.DMA((max(1, len(staged_in)),)),
            pltpu.SemaphoreType.DMA((max(1, len(staged_out)),)),
        ],
        input_output_aliases=aliases or {},
        compiler_params=pltpu.CompilerParams(vmem_limit_bytes=limit * MIB),
        cost_estimate=pl.CostEstimate(flops=cost, bytes_accessed=1, transcendentals=0),
        name=name,
    )(*args)


def far(*arrays):
    return [(array, "far") for array in arrays]


def norm_of(values):
    center = values - jnp.mean(values, axis=-1, keepdims=True)
    inverse = lax.rsqrt(jnp.mean(center * center, axis=-1, keepdims=True) + 1e-05)
    return center * inverse, inverse


def norm_back(upstream, normed, inverse, gain):
    scaled = upstream * gain
    return inverse * (
        scaled
        - jnp.mean(scaled, axis=-1, keepdims=True)
        - normed * jnp.mean(scaled * normed, axis=-1, keepdims=True)
    )


def fill_bias(plan, bias, seg_ref, pad_ref):
    length = bias.shape[0]
    row = pl.ds(lax.axis_index("seq"), 1)
    seg, pad = seg_ref[row, :], pad_ref[row, :]
    code = (2 * seg + pad).astype(F32)
    wanted = (2 * seg + 1).astype(F32)
    coded = jnp.broadcast_to(code, (length, length)).T
    rows = lax.broadcasted_iota(jnp.int32, (length, length), 0)
    cols = lax.broadcasted_iota(jnp.int32, (length, length), 1)
    bias[...] = jnp.where((coded == wanted) | (rows == cols), 0.0, -1e30)


def halves_of(values):
    lane = lax.broadcasted_iota(jnp.int32, values.shape, 1)
    zero = jnp.zeros_like(values)
    return jnp.where(lane < HD, values, zero), jnp.where(lane < HD, zero, values)


def prepare(plan, matrices, norm_params):
    groups = [matrices[0:3], matrices[3:5], matrices[5:6]]

    def body(io, ins, outs):
        io.start()
        core = lax.axis_index("seq") & 1
        first = 0
        rows = norm_params.shape[1]
        same = lax.broadcasted_iota(jnp.int32, (rows, rows), 0) == lax.broadcasted_iota(jnp.int32, (rows, rows), 1)
        lane = lax.broadcasted_iota(jnp.int32, (rows, 128), 1)
        side = jnp.zeros((rows, 128), F32)
        for p in range(norm_params.shape[0]):
            row = jnp.broadcast_to(ins[-1][p : p + 1, :], (rows, rows))
            column = jnp.sum(jnp.where(same, row, 0.0), axis=1, keepdims=True)
            side = jnp.where(lane == p, column, side)
        for out in outs[:2]:
            out[:, 3 * HALF :] = side.astype(BF)
        for number, group in enumerate(groups):
            at = 0
            for index in range(first, first + len(group)):
                io.need(index)
                size = ins[index].shape[1] // 2
                left, right = ins[index][:, :size], ins[index][:, size:]
                mine = jnp.where(core == 0, left, right).astype(BF)
                other = jnp.where(core == 0, right, left).astype(BF)
                outs[2 * number][:, at : at + size] = mine
                outs[2 * number + 1][:, at : at + size] = other
                at += size
            first += len(group)

    outs = []
    for group in groups:
        width = sum(w.shape[1] for w in group) // 2 + (128 if group is groups[0] else 0)
        outs += [(shape((group[0].shape[0], width), BF), "near")] * 2
    flat_outs = call("prepare", body, [*far(*matrices), (norm_params, "near")], outs, [], 8)
    return flat_outs[0:2], flat_outs[2:4], flat_outs[4:6]


def other_rows(plan, arrays):
    others = plan.seq - 1

    def body(io, ins, outs, held, in_sems, out_sems):
        mine = lax.axis_index("seq")
        loads = [
            pltpu.make_async_copy(ins[i // others].at[mine ^ (i % others + 1)], held.at[i], in_sems.at[i])
            for i in range(len(outs))
        ]
        for load in loads:
            load.start()
        puts = [pltpu.make_async_copy(held.at[i], outs[i], out_sems.at[i]) for i in range(len(outs))]
        for load, put in zip(loads, puts):
            load.wait()
            put.start()
        for put in puts:
            put.wait()

    part = arrays[0].shape[1:]
    count = others * len(arrays)
    outs = call(
        "other_rows", body, [(a, "raw") for a in arrays], [(shape(part, BF), "raw")] * count,
        [pltpu.VMEM((count, *part), BF), pltpu.SemaphoreType.DMA((count,)), pltpu.SemaphoreType.DMA((count,))],
        8,
    )
    return [outs[i * others : (i + 1) * others] for i in range(len(arrays))]


def row_blocks(length):
    for i in range(length // 128):
        yield slice(i * 128, (i + 1) * 128)


def project(plan, tokens, parts):
    length = tokens[0].size // D if len(tokens) == 1 else tokens[1].shape[0] * len(tokens)
    width = 3 * D + 256
    pieces = [(3 * HALF, 128, 3 * D), *[(m * HALF, HALF, m * D) for m in range(3)]]

    def body(io, ins, outs, whole, rows_in, sems, put_sems):
        h_ref, q_ref, k_ref, v_ref, n_ref, w_ref, x_ref = outs
        start_parts(plan, ins[len(tokens) :], whole, sems, pieces)
        loads = load_bands(plan, ins[: len(tokens)], rows_in, sems.at[pl.ds(4, len(tokens))])
        wait_part(whole, sems, 0, pieces[0])
        norms = flat(whole[:, :, :, 3 * D : 3 * D + 128]).astype(F32).T[0:8]
        n_ref[...] = norms
        for load in loads:
            load.wait()
        puts = [pltpu.make_async_copy(rows_in, x_ref, put_sems.at[1])]
        puts[0].start()
        for rows in row_blocks(length):
            normed, _ = norm_of(rows_in[rows, :].astype(F32))
            h_ref[rows, :] = (normed * norms[0:1, :] + norms[1:2, :]).astype(BF)
        io.ship(0)
        for m in range(3):
            wait_part(whole, sems, 1 + m, pieces[1 + m])
        puts.append(pltpu.make_async_copy(whole, w_ref, put_sems.at[0]))
        puts[1].start()
        for m, (out, scale) in enumerate(((q_ref, 0.125), (k_ref, 1.0), (v_ref, 1.0))):
            weight = flat(whole[:, :, :, m * D : (m + 1) * D])
            out[...] = (dot(h_ref[...], weight, 1, 0) * scale).astype(BF)
            io.ship(1 + m)
        for put in puts:
            put.wait()

    act = shape((length, D), BF)
    wide = plan.wide(D, width)
    return call(
        "project", body, [*[(t, "any") for t in tokens], *[(p, "any") for p in parts]],
        [*[(act, "far")] * 4, (shape((8, D), F32), "near"), (shape(wide, BF), "raw"), (act, "raw")],
        [
            pltpu.VMEM(wide, BF), pltpu.VMEM((length, D), BF),
            pltpu.SemaphoreType.DMA((4 + len(tokens),)), pltpu.SemaphoreType.DMA((2,)),
        ],
        20, 1,
    )


def mix(plan, query, key, value, seg, pad):
    length = query.shape[0]

    def body(io, ins, outs, bias):
        q_ref, k_ref, v_ref, seg_ref, pad_ref = ins
        at_ref, a_ref, l_ref = outs
        io.start()
        fill_bias(plan, bias, seg_ref, pad_ref)
        io.need(0, 1, 2)

        @pl.loop(0, PAIRS, unroll=True)
        def _(p):
            cols = pl.ds(pl.multiple_of(p * 128, 128), 128)
            keys = k_ref[:, cols]
            turned = v_ref[:, cols].T
            for half, query in enumerate(halves_of(q_ref[:, cols])):
                scores = dot(keys, query, 1, 1) + bias[...]
                top = jnp.max(scores, axis=0, keepdims=True)
                lifted = jnp.exp(scores - top)
                total = jnp.sum(lifted, axis=0, keepdims=True)
                soft = (lifted * (1.0 / total)).astype(BF)
                mixed = dot(turned[half * HD : (half + 1) * HD], soft, 1, 0)
                at_ref[pl.ds(pl.multiple_of(p * 128 + half * HD, HD), HD), :] = mixed.astype(BF)
                l_ref[pl.ds(2 * p + half, 1), :] = top + jnp.log(total)
            a_ref[:, cols] = at_ref[pl.ds(pl.multiple_of(p * 128, 128), 128), :].T

    return call(
        "mix", body, [*far(query, key, value), (seg, "near"), (pad, "near")],
        [(shape((D, length), BF), "far"), (shape((length, D), BF), "far"), (shape((H, length), F32), "far")],
        [pltpu.VMEM((length, length), F32)],
        14,
    )


def widen(plan, tokens, mixed, norms, parts):
    length = tokens.shape[0]
    pieces = [(0, HALF, 0), (HALF, 2 * D, D)]

    def body(io, ins, outs, whole, sems, put_sems):
        x_ref, a_ref, n_ref, *part_refs = ins
        m_ref, h_ref, z_ref, s_ref, w_ref = outs
        io.start(1)
        start_parts(plan, part_refs, whole, sems, pieces[:1])
        io.start(0)
        start_parts(plan, part_refs, whole, sems.at[pl.ds(1, 1)], pieces[1:])
        io.need(0, 1)
        wait_part(whole, sems, 0, pieces[0])
        m_ref[...] = x_ref[...].astype(F32) + dot(a_ref[...], flat(whole[:, :, :, 0:D]), 1, 0)
        io.ship(0)
        for rows in row_blocks(length):
            normed, _ = norm_of(m_ref[rows, :])
            h_ref[rows, :] = (normed * n_ref[2:3, :] + n_ref[3:4, :]).astype(BF)
        io.ship(1)
        wait_part(whole, sems, 1, pieces[1])
        put = pltpu.make_async_copy(whole, w_ref, put_sems.at[0])
        put.start()
        for block in range(BLOCKS):
            cols = slice(block * D, (block + 1) * D)
            up = dot(h_ref[...], flat(whole[:, :, :, (block + 1) * D : (block + 2) * D]), 1, 0)
            bell = 0.5 + 0.5 * lax.erf(up * 0.7071067811865476)
            z_ref[:, cols] = (up * bell).astype(BF)
            s_ref[:, cols] = (bell + up * (jnp.exp(-0.5 * up * up) * 0.3989422804014327)).astype(BF)
            io.ship(2, pl.ds(block * D, D))
            io.ship(3, pl.ds(block * D, D))
        put.wait()

    act = shape((length, D), BF)
    wide = plan.wide(D, D + FF)
    hidden = shape((length, FF), BF)
    outs = [shape((length, D), F32), act, hidden, hidden]
    return call(
        "widen", body, [*far(tokens, mixed), (norms, "near"), *[(p, "any") for p in parts]],
        [*[(o, "far") for o in outs], (shape(wide, BF), "raw")],
        [pltpu.VMEM(wide, BF), pltpu.SemaphoreType.DMA((2,)), pltpu.SemaphoreType.DMA((1,))],
        28,
    )


def grad_of_down(plan, hidden, cot):
    length = hidden.shape[0]

    def body(io, ins, outs, g_in, z_in, sems, z_sems, put_sems, g_sem, held):
        z_ref, *bands = ins
        *grads, g_out = outs
        loads = load_bands(plan, bands, g_in, sems)
        z_loads = [
            pltpu.make_async_copy(z_ref.at[:, pl.ds(i * D, D)], z_in.at[:, pl.ds(i * D, D)], z_sems.at[i])
            for i in range(BLOCKS)
        ]
        for load in z_loads:
            load.start()
        for load in loads:
            load.wait()
        puts = [pltpu.make_async_copy(g_in, g_out, g_sem.at[0])]
        puts[0].start()
        for block in range(BLOCKS):
            z_loads[block].wait()
            tile = dot(z_in[:, block * D : (block + 1) * D], g_in[...], 0, 0)
            store_grad(plan, tile, held, FF, block * D, slice(None))
            view = (slice(None), pl.ds(block, 1)) if plan.fast else (pl.ds(block * D, D),)
            puts += put_grad(held, grads, put_sems.at[block], view, view)
        for put in puts:
            put.wait()

    act = shape((length, D), BF)
    grads = plan.grads(FF, D)
    return call(
        "grad_of_down", body, [(hidden, "raw"), *[(c, "any") for c in cot]],
        [*[(g, "raw") for g in grads], (act, "raw")],
        [
            pltpu.VMEM((length, D), BF), pltpu.VMEM((length, FF), BF),
            pltpu.SemaphoreType.DMA((len(cot),)), pltpu.SemaphoreType.DMA((BLOCKS,)),
            pltpu.SemaphoreType.DMA((BLOCKS, len(grads))), pltpu.SemaphoreType.DMA((1,)),
            held_grad(plan, FF, D),
        ],
        28,
    )


def narrow(plan, blocks, mid, below, grads, low, hidden, slope, cot, whole_ou, parts_down):
    length = mid.shape[0]
    count = len(blocks)
    start, final = blocks[0] == 0, blocks[-1] == BLOCKS - 1
    cut = (blocks[0] * D, count * D)
    n_out = plan.outs()

    def body(io, ins, outs, *scratch):
        m_ref, h_ref, z_ref, s_ref, g_ref, up_ref, *rest = ins
        downs = rest[: len(parts_down)]
        b_ref, *grad_refs = outs[: 1 + n_out]
        o_refs = outs[1 + n_out :]
        held, du_ref, acc, whole_up, whole_down, sems, put_sems = scratch
        copies = []
        down = (0, HALF, 0)
        io.start(4)
        start_parts(plan, downs, whole_down, sems.at[pl.ds(0, 1)], [down], blocks)
        io.start(3, 1)
        up = pltpu.make_async_copy(up_ref.at[..., pl.ds(D + cut[0], cut[1])], whole_up, sems.at[1])
        up.start()
        io.start()
        io.need(4)
        wait_part(whole_down, sems, 0, down)
        io.need(3, 1)
        for number, block in enumerate(blocks):
            local = slice(number * D, (number + 1) * D)
            back = dot(g_ref[...], flat(whole_down[number]), 1, 1)
            du_ref[:, local] = (back * s_ref[:, local]).astype(BF)
            tile = dot(h_ref[...], du_ref[:, local], 0, 0)
            store_grad(plan, tile, held, D, 0, local)
            views = [(*[slice(None)] * (plan.grads(D, D)[0].ndim - 1), pl.ds(at * D, D)) for at in (number, block)]
            copies += put_grad(held, grad_refs, put_sems.at[number], *views)
        up.wait()
        lower = dot(du_ref[...], flat(whole_up[...]), 1, 1)
        if start:
            b_ref[...] = lower
        else:
            io.need(6 + len(parts_down))
            b_ref[...] = rest[len(parts_down)][...] + lower
        io.ship(0)
        io.need(0, 2)
        gain = m_ref[...] + dot(z_ref[...], whole_down[...].reshape(count * D, D), 1, 0)
        if final:
            acc[...] = gain
            for number, o_ref in enumerate(o_refs):
                o_ref[...] = acc[band(plan, number, length), :].astype(BF)
        else:
            o_refs[0][...] = gain
        for copy in copies:
            copy.wait()

    deep = plan.wide(FF, D)
    ins = [
        *far(mid, low), (hidden, "far", cut), (slope, "far", cut), *far(cot), (whole_ou, "raw"),
        *[(p, "any") for p in parts_down],
    ]
    aliases = {}
    if not start:
        ins += far(below)
        aliases = {len(ins) + i: 1 + i for i in range(n_out)}
        ins += [(g, "raw") for g in grads]
    return call(
        "narrow" + str(blocks[0]), body, ins,
        [
            (shape((length, D), F32), "far"), *[(g, "raw") for g in plan.grads(D, FF)],
            *[(o, "far") for o in (plan.band_shapes(length) if final else [shape((length, D), F32)])],
        ],
        [
            held_grad(plan, D, count * D),
            pltpu.VMEM((length, count * D), BF),
            pltpu.VMEM((length, D), F32),
            pltpu.VMEM(plan.wide(D, count * D), BF),
            pltpu.VMEM((count, *deep[1:]), BF),
            pltpu.SemaphoreType.DMA((2,)),
            pltpu.SemaphoreType.DMA((count, n_out)),
        ],
        40, aliases=aliases,
    )


def turn(plan, mid, back, cot, norms, whole_ou):
    length = mid.shape[0]

    def body(io, ins, outs, whole, sems):
        m_ref, b_ref, g_ref, n_ref, w_ref = ins
        x_ref, low, d_ref, s_ref = outs
        io.start()
        load = pltpu.make_async_copy(w_ref.at[..., pl.ds(0, D)], whole, sems.at[0])
        load.start()
        s_ref[...] = jnp.zeros_like(s_ref)
        io.need(0, 1, 2)
        for rows in row_blocks(length):
            normed, inverse = norm_of(m_ref[rows, :])
            upstream = b_ref[rows, :]
            total = g_ref[rows, :].astype(F32) + norm_back(upstream, normed, inverse, n_ref[2:3, :])
            x_ref[rows, :] = total
            low[rows, :] = total.astype(BF)
            s_ref[0:1, :] += jnp.sum(upstream * normed, axis=0, keepdims=True)
            s_ref[1:2, :] += jnp.sum(upstream, axis=0, keepdims=True)
        io.ship(0)
        io.ship(1)
        load.wait()
        d_ref[...] = dot(low[...], flat(whole[...]), 1, 1).astype(BF)

    act = shape((length, D), BF)
    return call(
        "turn", body, [*far(mid, back, cot), (norms, "near"), (whole_ou, "raw")],
        [(shape((length, D), F32), "far"), (act, "far"), (act, "far"), (shape((2, D), F32), "near")],
        [pltpu.VMEM(plan.wide(D, D), BF), pltpu.SemaphoreType.DMA((1,))],
        24,
    )


def attend_back(plan, side, low, query, key, value, lse, cot, seg, pad, extra=()):
    length = low.shape[0]
    width = 3 * HALF + (D if extra else 0)
    cut = (side * HALF, HALF)

    def body(io, ins, outs, bias, held, put_sems):
        h_ref, q_ref, k_ref, v_ref, c_ref, l_ref, seg_ref, pad_ref, *more = ins
        d_ref, *grads = outs
        io.start(1, 2, 3, 4, 5)
        io.start()
        fill_bias(plan, bias, seg_ref, pad_ref)
        io.need(1, 2, 3, 4, 5)

        @pl.loop(0, PAIRS // 2)
        def _(local):
            p = local + side * (PAIRS // 2)
            first = pl.multiple_of(local * 128, 128)
            cols = pl.ds(first, 128)
            keys, values = k_ref[:, cols], v_ref[:, cols]
            turned = keys.T
            queries, cots = halves_of(q_ref[:, cols]), halves_of(c_ref[:, cols])
            dv = dk = None
            dqs = []
            for half in range(2):
                scores = dot(keys, queries[half], 1, 1) + bias[...]
                soft = jnp.exp(scores - l_ref[pl.ds(2 * p + half, 1), :])
                gain = dot(soft.astype(BF), cots[half], 1, 0)
                dv = gain if dv is None else dv + gain
                dp = dot(values, cots[half], 1, 1)
                share = jnp.sum(soft * dp, axis=0, keepdims=True)
                ds = (soft * (dp - share)).astype(BF)
                gain = dot(ds, queries[half], 1, 0)
                dk = gain if dk is None else dk + gain
                dqs.append(dot(turned[half * HD : (half + 1) * HD], ds, 1, 0) * 0.125)
            d_ref[:, cols] = jnp.concatenate(dqs, axis=0).T.astype(BF)
            d_ref[:, pl.ds(first + HALF, 128)] = dk.astype(BF)
            d_ref[:, pl.ds(first + 2 * HALF, 128)] = dv.astype(BF)

        io.ship(0)
        io.need(0)
        lead, copies = [slice(None)] * (len(grads[0].shape) - 1), []
        if extra:
            io.need(8, 9)
            tile = dot(more[0][...], more[1][...], 1, 0)
            store_grad(plan, tile, held, D, 0, slice(3 * HALF, width))
            view = (*lead, pl.ds(3 * HALF, D))
            copies += put_grad(held, grads, put_sems.at[3], view, view)
        for m in range(3):
            cols = slice(m * HALF, (m + 1) * HALF)
            store_grad(plan, dot(h_ref[...], d_ref[:, cols], 0, 0), held, D, 0, cols)
            view = (*lead, pl.ds(m * HALF, HALF))
            copies += put_grad(held, grads, put_sems.at[m], view, view)
        for copy in copies:
            copy.wait()

    return call(
        "attend_back" + str(side), body,
        [
            *far(low), *[(a, "far", cut) for a in (query, key, value, cot)], *far(lse),
            (seg, "near"), (pad, "near"), *far(*extra),
        ],
        [(shape((length, 3 * HALF), BF), "far"), *[(g, "raw") for g in plan.grads(D, width)]],
        [
            pltpu.VMEM((length, length), F32), held_grad(plan, D, width),
            pltpu.SemaphoreType.DMA((4, plan.outs())),
        ],
        26,
    )


def finish_tokens(plan, tokens, spreads, mid_cot, norms, whole_qkv):
    length = tokens.shape[0]

    def body(io, ins, outs, back, whole, sems):
        x_ref, d0_ref, d1_ref, c_ref, n_ref, w_ref = ins
        *o_refs, s_ref = outs
        io.start(1, 2)
        load = pltpu.make_async_copy(w_ref.at[..., pl.ds(0, 3 * D)], whole, sems.at[0])
        load.start()
        io.start()
        s_ref[...] = jnp.zeros_like(s_ref)
        io.need(1, 2)
        load.wait()
        back[...] = sum(
            dot(
                jnp.concatenate([d[:, m * HALF : (m + 1) * HALF] for d in (d0_ref, d1_ref)], axis=1),
                flat(whole[:, :, :, m * D : (m + 1) * D]), 1, 1,
            )
            for m in range(3)
        )
        io.need(0, 3)
        for rows in row_blocks(length):
            normed, inverse = norm_of(x_ref[rows, :].astype(F32))
            upstream = back[rows, :]
            c_ref[rows, :] += norm_back(upstream, normed, inverse, n_ref[0:1, :])
            s_ref[0:1, :] += jnp.sum(upstream * normed, axis=0, keepdims=True)
            s_ref[1:2, :] += jnp.sum(upstream, axis=0, keepdims=True)
        for number, o_ref in enumerate(o_refs):
            o_ref[...] = c_ref[band(plan, number, length), :].astype(BF)

    return call(
        "finish_tokens", body, [*far(tokens, *spreads, mid_cot), (norms, "near"), (whole_qkv, "raw")],
        [*[(o, "far") for o in plan.band_shapes(length)], (shape((2, D), F32), "near")],
        [pltpu.VMEM((length, D), F32), pltpu.VMEM(plan.wide(D, 3 * D), BF), pltpu.SemaphoreType.DMA((1,))],
        20, 1,
    )


def sum_up(plan, blocks, others, slices):
    nz, rows, columns = blocks.shape
    wide = 4 * D // plan.count

    def body(io, ins, outs, held, sems):
        blocks_ref, others_ref, slice_ref = ins
        g_ref, card_ref = outs
        loads = [pltpu.make_async_copy(blocks_ref.at[i], held.at[i], sems.at[i]) for i in range(nz)]
        for load in loads:
            load.start()
        for load in loads:
            load.wait()
        value = jnp.sum(held[...].astype(F32), axis=0)
        g_ref[...] = value
        left = jnp.sum(jnp.sum(value * value, axis=0, keepdims=True), axis=1, keepdims=True) + others_ref[0:1, 0:1]
        lane = lax.broadcasted_iota(jnp.int32, slice_ref.shape, 1)
        card = slice_ref[...]
        for i in range(3):
            piece = left.astype(BF).astype(F32)
            card = jnp.where(lane == wide + i, piece, card)
            left = left - piece
        card = card.astype(BF)
        for i in range(plan.count):
            card_ref[i] = card

    return call(
        "sum_up", body, [(blocks, "any"), (others, "near"), (slices, "near")],
        [(shape((rows, columns), F32), "near"), (shape((plan.count, *slices.shape), BF), "near")],
        [pltpu.VMEM(blocks.shape, BF), pltpu.SemaphoreType.DMA((nz,))], 8,
    )


def update(plan, grads, cards, masters, firsts, seconds, passed):
    rates = [D**-0.5] * 3 + [4.0 * D**-0.5, D**-0.5, FF**-0.5, 0.2]
    decays = [0.01] * 6 + [0.0]
    count = len(masters)
    given = len(grads)

    def body(io, ins, outs, total, sems):
        grad_refs, card_ref = ins[:given], ins[given]
        first = given + 1
        io.start(*(first + k * count + i for i in reversed(range(count)) for k in range(3)))
        io.start()
        sources, rows, _ = card_ref.shape
        split = min(2, sources)
        for c in range(split):
            cards_c = [card_ref[i].astype(F32) for i in range(c, sources, split)]
            total[c * rows : (c + 1) * rows, :] = sum(cards_c[1:], cards_c[0])
        wide = 4 * D // plan.count
        all_norms = total[...]
        lane = lax.broadcasted_iota(jnp.int32, all_norms.shape, 1)
        own = jnp.where(lane < wide, all_norms * all_norms, all_norms * (1.0 / rows))
        square = jnp.sum(jnp.sum(own, axis=0, keepdims=True), axis=1, keepdims=True)
        norm = jnp.sqrt(square)
        outs[0][...] = jnp.broadcast_to(norm, outs[0].shape)
        factor = jnp.minimum(1.0, clip_limit / (norm + 1e-06))
        place_of = lax.axis_index("dp") * plan.seq + lax.axis_index("seq")
        if split == 2:
            place_of = (place_of & 1) * rows + (place_of >> 1)
        mine = total[pl.ds(place_of, 1), :]
        each = wide // 4
        grad_norms = jnp.concatenate([mine[:, p * each : (p + 1) * each] for p in range(4)], axis=0)
        for i in reversed(range(count)):
            w_ref, m_ref, s_ref = (ins[first + k * count + i] for k in range(3))
            io.need(*(first + k * count + i for k in range(3)))
            if i < 3:
                cols = [
                    (slice(h * HALF, (h + 1) * HALF), grad_refs[0][:, (5 * h + i) * HALF : (5 * h + i + 1) * HALF])
                    for h in range(2)
                ]
            elif i == 3:
                cols = [(slice(None), grad_refs[0][:, 3 * HALF : 5 * HALF])]
            elif i < 6:
                cols = [(slice(None), grad_refs[i - 3][...])]
            else:
                cols = [(slice(None), grad_norms)]
            for where, grad in cols:
                clipped = factor * grad
                one = 0.5 * m_ref[:, where] + 0.5 * clipped
                two = 0.55 * s_ref[:, where] + 0.45 * clipped * clipped
                root = jnp.sqrt(two * (1.0 / (1.0 - 0.55**STEP))) + 1e-08
                weight = w_ref[:, where]
                step = (one * (1.0 / (1.0 - 0.5**STEP))) / root + decays[i] * weight
                outs[1 + i][:, where] = weight - rates[i] * step
                outs[1 + count + i][:, where] = one
                outs[1 + 2 * count + i][:, where] = two
            for k in range(3):
                io.ship(1 + k * count + i)
        last = first + 3 * count
        copies = []
        for number in range(len(passed)):
            which, place_in = number // plan.bands(), number % plan.bands()
            io.need(last + number)
            target = outs[1 + 3 * count + which]
            if plan.bands() > 1:
                target = target.at[lax.axis_index("seq") ^ place_in]
            copies.append(pltpu.make_async_copy(ins[last + number], target, sems.at[number]))
            copies[-1].start()
        for copy in copies:
            copy.wait()

    like = [(shape(w.shape, F32), "far") for w in masters] * 3
    pieces = [shape((plan.bands(), *p.shape), BF) if plan.bands() > 1 else p for p in passed[:: plan.bands()]]
    return call(
        "update", body, [*[(g, "near") for g in grads], (cards, "near"), *far(*masters, *firsts, *seconds, *passed)],
        [(shape((1, 128), F32), "near"), *like, *[(o, "raw") for o in pieces]],
        [pltpu.VMEM((min(2, cards.shape[0]) * cards.shape[1], 128), F32), pltpu.SemaphoreType.DMA((len(passed),))], 20,
    )


def after(values, *others):
    return lax.optimization_barrier((values, others))[0]


def meet(*values):
    return lax.optimization_barrier(values)


def send(plan, values, perm):
    return lax.ppermute(values, AXES, perm)


def block_of(plan, mine, other):
    core = lax.axis_index("seq") & 1
    got = send(plan, other, plan.core)
    return jnp.where(core == 0, jnp.concatenate([mine, got]), jnp.concatenate([got, mine]))


def copies_of(plan, block):
    return jnp.broadcast_to(block[None], (plan.nz, *block.shape))


def along_z(plan, values):
    return lax.all_to_all(values, "dp", 0, 0, axis_index_groups=plan.groups, tiled=True)


def gather_whole(matrices):
    split = [w.reshape(w.shape[0], 2, -1) for w in matrices]
    halves = jnp.concatenate(split, axis=2).transpose(1, 0, 2).astype(BF)
    full = lax.all_gather(halves, AXES, axis=1, tiled=True)
    return [full.reshape(2, BLOCKS, 1, -1, full.shape[-1])]


def add(one, two):
    return one.astype(F32) + two.astype(F32)


def fold(keep, got):
    if keep.ndim == 4:
        keep, got = (v.reshape(-1, *v.shape[2:]) for v in (keep, got))
    size = keep.shape[0] // 2
    return add(keep[size:], got[size:]).astype(BF), add(keep[:size], got[:size]).astype(BF)


def total(blocks):
    return jnp.sum(blocks.astype(F32), axis=0)


def finish(plan, grads, sums, masters, firsts, seconds, *passed):
    wide = sums.shape[0] * D // plan.count
    slices = sums.reshape(sums.shape[0], plan.count, -1).transpose(1, 0, 2).reshape(plan.count, wide)
    slices = jnp.pad(slices, ((0, 0), (0, 128 - wide)))
    if plan.fast:
        core = lax.axis_index("seq") & 1
        pairs = slices.reshape(-1, 2, 128)
        mine, other = (lax.dynamic_index_in_dim(pairs, c, 1, keepdims=False) for c in (core, 1 - core))
        slices = mine + send(plan, other, plan.core)
        blocks, *others = grads
        left = jnp.broadcast_to(sum(jnp.sum(g * g) for g in others), (1, 128))
        left, slices, blocks, early = meet(left, slices, blocks, passed[:-1])
        passed = [*early, passed[-1]]
        last, cards = sum_up(plan, blocks, left, slices)
        grads = [last, *others]
        cards = lax.all_to_all(cards, AXES, 0, 0, tiled=True)
    else:
        left = jnp.broadcast_to(sum(jnp.sum(g * g) for g in grads), (plan.count, 1))
        cards = lax.psum(slices + jnp.pad(left, ((0, 0), (wide, 127 - wide))), AXES)[None]
    norm, *updated, output, input_grad = update(plan, grads, cards, masters, firsts, seconds, passed)
    return (output, input_grad, norm[0, 0], *updated)


def on_device(plan, *args):
    tokens_in, segment_ids, pad_mask, out_grad = args[:4]
    masters, firsts, seconds = args[4:11], args[11:18], args[18:25]
    each, piece, _ = tokens_in.shape
    length = each // plan.seq * plan.seq * piece

    plan.fast = plan.fast and each == plan.seq

    def swap(values, number):
        return lax.ppermute(values, "seq", [(i, i ^ number) for i in range(plan.seq)])

    def to_rows(values, others=None):
        if not plan.fast:
            return [lax.all_to_all(values, "seq", 0, 0, tiled=True).reshape(length, D)]
        return [values, *[swap(other, 1 + n) for n, other in enumerate(others)]]

    def to_pieces(bands):
        if not plan.fast:
            return [lax.all_to_all(bands[0].reshape(each, piece, D), "seq", 0, 0, tiled=True)]
        return [bands[0], *[swap(other, 1 + n) for n, other in enumerate(bands[1:])]]

    seg, pad = segment_ids, pad_mask

    if not plan.fast:
        side = jnp.pad(masters[6].T, ((0, 0), (0, 124)))
        side = jnp.concatenate([side, side], axis=1)
        one, two, three = (gather_whole(m) for m in ([*masters[0:3], side], masters[3:5], masters[5:6]))
        low_one, query, key, value, norms, whole_qkv, tokens = project(plan, to_rows(tokens_in), one)
        mixed_t, mixed, lse = mix(plan, query, key, value, seg, pad)
        mid, low_two, hidden, slope, whole_ou = widen(plan, tokens, mixed, norms, two)
        *g_down, cot = grad_of_down(plan, hidden, to_rows(out_grad))
        back, *g_up, part = narrow(plan, (0, 1), mid, None, None, low_two, hidden, slope, cot, whole_ou, three)
        back, *g_up, result = narrow(plan, (2, 3), part, back, g_up, low_two, hidden, slope, cot, whole_ou, three)
        mid_cot, low_cot, mixed_cot, sums_two = turn(plan, mid, back, cot, norms, whole_ou)
        halves = [
            attend_back(plan, side, low_one, query, key, value, lse, mixed_cot, seg, pad, extra)
            for side, extra in enumerate(((mixed_t, low_cot), ()))
        ]
        stream, sums_one = finish_tokens(plan, tokens, [h[0] for h in halves], mid_cot, norms, whole_qkv)
        grads = [
            lax.psum_scatter(g.astype(F32), AXES, scatter_dimension=0, tiled=True)
            for g in (halves[0][1], halves[1][1], *g_up, *g_down)
        ]
        grads = [jnp.concatenate(grads[:2], axis=1), *grads[2:]]
        sums = jnp.concatenate([sums_one, sums_two], axis=0)
        return finish(plan, grads, sums, masters, firsts, seconds, *to_pieces([result]), *to_pieces([stream]))

    first, second, third = prepare(plan, masters[:6], masters[6])
    block = block_of(plan, *first)
    near_one = along_z(plan, copies_of(plan, block))
    others, others_cot = other_rows(plan, [after(tokens_in, block), out_grad])
    tokens = to_rows(tokens_in, others)
    block_two = block_of(plan, *second)
    spread_two = copies_of(plan, block_two)
    spread_three = copies_of(plan, block_of(plan, *third))
    near_one, tokens, spread_two, spread_three = meet(near_one, tokens, spread_two, spread_three)

    def spread(near):
        return send(plan, near, plan.second), send(plan, near, plan.first)

    def to_core(*parts):
        return [send(plan, part, plan.core) for part in parts]

    beside_one, across_one = spread(near_one)
    near_two = along_z(plan, spread_two)
    beside_one, across_one = meet(beside_one, across_one)
    corner_one = send(plan, beside_one, plan.first)
    one = [near_one, beside_one, across_one]
    one_core = to_core(*one)
    corner_one, one_core = meet(corner_one, one_core)
    one = [*one, corner_one, *one_core, *to_core(corner_one)]
    low_one, query, key, value, norms, whole_qkv, tokens = project(plan, tokens, one)
    cot = to_rows(out_grad, after(others_cot, corner_one))
    near_two, query, cot = meet(near_two, query, cot)
    beside_two, across_two = spread(near_two)
    near_three = along_z(plan, after(spread_three, near_two))
    mixed_t, mixed, lse = mix(plan, query, key, value, seg, pad)
    beside_two, across_two, near_three, mixed, lse, mixed_t = meet(
        beside_two, across_two, near_three, mixed, lse, mixed_t
    )
    corner_two = send(plan, beside_two, plan.first)
    beside_three, across_three = spread(near_three)
    two = [near_two, beside_two, across_two]
    two_core = to_core(*two)
    corner_two, two_core = meet(corner_two, two_core)
    two = [*two, corner_two, *two_core, *to_core(corner_two)]
    mid, low_two, hidden, slope, whole_ou = widen(plan, tokens, mixed, norms, two)
    beside_three, across_three, hidden = meet(beside_three, across_three, hidden)
    corner_three = send(plan, beside_three, plan.first)
    three = [near_three, beside_three, across_three]
    three_core = to_core(*three)
    keep_d, go_d, cot = grad_of_down(plan, hidden, cot)
    corner_three, three_core, keep_d, go_d, cot = meet(corner_three, three_core, keep_d, go_d, cot)
    three = [*three, corner_three, *three_core, *to_core(corner_three)]

    got_d = send(plan, go_d, plan.core)
    back, *g_up, part = narrow(plan, (0, 1), mid, None, None, low_two, hidden, slope, cot, whole_ou, three)
    got_d, back, part = meet(got_d, back, part)
    go_d, keep_d = fold(keep_d, got_d)
    got_d = send(plan, go_d, plan.first)
    part = after(part, go_d)
    back, *rest = narrow(plan, (2, 3), part, back, g_up, low_two, hidden, slope, cot, whole_ou, three)
    got_d, back, rest = meet(got_d, back, rest)
    (keep_u, go_u), result = rest[:2], rest[2:]
    got_u = send(plan, go_u, plan.core)
    go_d, keep_d = fold(keep_d, got_d)
    got_d = send(plan, go_d, plan.second)
    back = after(back, go_d)
    mid_cot, low_cot, mixed_cot, sums_two = turn(plan, mid, back, cot, norms, whole_ou)
    got_u, mixed_cot, low_cot, mid_cot, result = meet(got_u, mixed_cot, low_cot, mid_cot, result)
    go_u, keep_u = fold(keep_u, got_u)
    got_d, go_u = meet(got_d, go_u)
    got_u = send(plan, go_u, plan.first)
    mixed_cot = after(mixed_cot, go_u)
    spread_a, keep_a, go_a = attend_back(
        plan, 0, low_one, query, key, value, lse, mixed_cot, seg, pad, (mixed_t, low_cot)
    )
    got_u, keep_a, spread_a = meet(got_u, keep_a, spread_a)
    got_a = send(plan, go_a, plan.core)
    block_d = add(keep_d, got_d).astype(BF)
    blocks_d = along_z(plan, block_d)
    go_u, keep_u = fold(keep_u, got_u)
    got_u = send(plan, go_u, plan.second)
    go_a, keep_a = fold(keep_a, got_a)
    got_a = send(plan, go_a, plan.first)
    mixed_cot = after(mixed_cot, go_u, go_a, block_d)
    spread_b, keep_b, go_b = attend_back(plan, 1, low_one, query, key, value, lse, mixed_cot, seg, pad)
    blocks_d, got_u, got_a, keep_b, spread_b = meet(blocks_d, got_u, got_a, keep_b, spread_b)
    got_b = send(plan, go_b, plan.core)
    block_u = add(keep_u, got_u).astype(BF)
    blocks_u = along_z(plan, block_u)
    go_b, keep_b = fold(keep_b, after(got_b, block_u))
    got_b = send(plan, go_b, plan.first)
    go_a, keep_a = fold(keep_a, after(got_a, go_b))
    got_a = send(plan, go_a, plan.second)
    mid_cot = after(mid_cot, go_a, go_b)
    *stream, sums_one = finish_tokens(plan, tokens, [spread_a, spread_b], mid_cot, norms, whole_qkv)
    got_b, sums_one, stream = meet(got_b, sums_one, stream)
    go_b, keep_b = fold(keep_b, got_b)
    got_b = send(plan, go_b, plan.second)
    got_a = after(got_a, go_b)
    output = to_pieces(after(result, go_b))
    input_grad = to_pieces(after(stream, go_b))
    halves = [add(keep_a, got_a), add(keep_b, got_b)]
    blocks_ab = along_z(plan, jnp.concatenate(halves, axis=2).astype(BF))
    grads = [blocks_ab, total(blocks_u), total(blocks_d)]
    sums = jnp.concatenate([sums_one, sums_two], axis=0)
    return finish(plan, grads, sums, masters, firsts, seconds, *output, *input_grad)


def solution(mesh):
    plan = Plan(mesh, None)
    rows = P(AXES, None)
    weights = (*[rows] * 6, P(None, AXES))
    tokens = P("dp", "seq", None)
    return jax.shard_map(
        partial(on_device, plan),
        mesh=mesh,
        in_specs=(tokens, P("dp", None), P("dp", None), tokens, *weights * 3),
        out_specs=(tokens, tokens, P(), *weights * 3),
        check_vma=False,
    )
```

```python
from functools import partial

import jax
import jax.numpy as jnp
from jax import lax
from jax.experimental import pallas as pl
from jax.experimental.pallas import tpu as pltpu
from jax.sharding import PartitionSpec as P

D = 768
H = 12
HD = 64
FF = 3072
STEP = 7
HALF = D // 2
PAIRS = H // 2
BLOCKS = 4
BF = jnp.bfloat16
F32 = jnp.float32
AXES = ("dp", "seq")
clip_limit = 1.0
MIB = 2**20

VM = pl.BlockSpec(memory_space=pltpu.VMEM)
ANY = pl.BlockSpec(memory_space=pl.ANY)
FAR = pl.BlockSpec(memory_space=pltpu.HBM)


def dot(left, right, left_dim, right_dim):
    return lax.dot_general(
        left, right, (((left_dim,), (right_dim,)), ((), ())), preferred_element_type=F32
    )


def shape(dims, kind):
    return jax.ShapeDtypeStruct(dims, kind)


class Plan:
    def __init__(self, mesh, rows_each):
        self.dp = mesh.shape["dp"]
        self.seq = mesh.shape["seq"]
        self.count = self.dp * self.seq
        self.fast = (
            self.seq == 4
            and self.dp % 2 == 0
            and BLOCKS * 8 == self.count
            and (2 * D // self.count) % 16 == 0
        )
        self.nz = self.dp // 2
        self.rows = D // self.count
        self.far = FF // self.count
        both = range(self.count)
        self.core = [(d, d ^ 1) for d in both]
        self.first = [(d, d ^ (2 if d % 2 == 0 else 4)) for d in both]
        self.second = [(d, d ^ (4 if d % 2 == 0 else 2)) for d in both]
        self.groups = [list(range(low, self.dp, 2)) for low in range(2)]

    def wide(self, rows, columns):
        if self.fast:
            return (self.nz, 4, 2 * rows // self.count, columns)
        return (BLOCKS, 1, rows // BLOCKS, columns)

    def parts(self):
        return 8 if self.fast else 1

    def grads(self, rows, columns):
        if self.fast:
            half = shape((4, self.nz, rows // self.count, columns), BF)
            return [half, half]
        return [shape((rows, columns), BF)]

    def outs(self):
        return 2 if self.fast else 1

    def bands(self):
        return self.seq if self.fast else 1

    def band_shapes(self, length):
        return [shape((length // self.bands(), D), BF)] * self.bands()


def place():
    seq = lax.axis_index("seq")
    return seq & 1, seq >> 1, lax.axis_index("dp") & 1


def start_parts(plan, parts, whole, sems, pieces, blocks=None):
    blocks = slice(None) if blocks is None else pl.ds(blocks[0], len(blocks))
    for index, (first, size, to) in enumerate(pieces):
        columns = pl.ds(first, size)
        if len(parts) == 1:
            for half in range(2):
                pltpu.make_async_copy(
                    parts[0].at[half, blocks, :, :, columns], whole.at[..., pl.ds(to + half * size, size)], sems.at[index]
                ).start()
            continue
        core, mine_x, mine_y = place()
        for number, part in enumerate(parts):
            owner = core if number < 4 else 1 - core
            one, two = (number >> 1) & 1, number & 1
            off_x = jnp.where(owner == 0, one, two)
            off_y = jnp.where(owner == 0, two, one)
            spot = (mine_y ^ off_y) * 2 + (mine_x ^ off_x)
            target = pl.ds(pl.multiple_of(to + owner * size, 128), size)
            pltpu.make_async_copy(part.at[blocks, :, columns], whole.at[:, spot, :, target], sems.at[index]).start()


def wait_part(whole, sems, index, piece):
    view = whole.at[..., pl.ds(piece[2], 2 * piece[1])]
    pltpu.make_async_copy(view, view, sems.at[index]).wait()


def band(plan, number, length):
    if plan.bands() == 1:
        return pl.ds(0, length)
    size = length // plan.bands()
    return pl.ds(pl.multiple_of((lax.axis_index("seq") ^ number) * size, size), size)


def load_bands(plan, refs, whole, sems):
    copies = []
    for number, ref in enumerate(refs):
        source = ref.at[lax.axis_index("seq")] if number == 0 and plan.bands() > 1 else ref
        target = whole.at[band(plan, number, whole.shape[0]), :]
        copies.append(pltpu.make_async_copy(source, target, sems.at[number]))
    for copy in copies:
        copy.start()
    return copies


def flat(value):
    return value.reshape(-1, value.shape[-1])


def held_grad(plan, rows, columns):
    one = plan.grads(rows, columns)
    return pltpu.VMEM((len(one), *one[0].shape), BF)


def put_grad(held, outs, sems, held_view, out_view):
    copies = [
        pltpu.make_async_copy(held.at[(i, *held_view)], out.at[out_view], sems.at[i]) for i, out in enumerate(outs)
    ]
    for copy in copies:
        copy.start()
    return copies


def store_grad(plan, tile, held, rows, first_row, columns):
    if not plan.fast:
        held[0, pl.ds(first_row, tile.shape[0]), columns] = tile.astype(BF)
        return
    core, mine_x, mine_y = place()
    step = rows // plan.count

    def spot(pair, owner):
        off_x = (pair & 1) ^ mine_x
        off_y = ((pair >> 1) & 1) ^ mine_y
        return (off_x * 2 + off_y if owner == 0 else off_y * 2 + off_x), pair >> 2

    for local in range(tile.shape[0] // (2 * step)):
        pair = first_row // (2 * step) + local
        low = tile[2 * step * local : 2 * step * local + step]
        high = tile[2 * step * local + step : 2 * step * (local + 1)]
        held[core, *spot(pair, 0), :, columns] = low.astype(BF)
        held[1 - core, *spot(pair, 1), :, columns] = high.astype(BF)


class Io:
    def __init__(self, ins, outs, held_in, held_out, in_sems, out_sems):
        self.loads, self.running = {}, []
        for number, (index, ref, cut) in enumerate(ins):
            source = ref if cut is None else ref.at[:, pl.ds(*cut)]
            self.loads[index] = pltpu.make_async_copy(source, held_in[number], in_sems.at[number])
        self.outs = {
            index: (held_out[number], ref, out_sems.at[number]) for number, (index, ref) in enumerate(outs)
        }
        self.shipped = []

    def start(self, *indices):
        for index in indices or [i for i in self.loads if i not in self.running]:
            self.loads[index].start()
            self.running.append(index)

    def need(self, *indices):
        for index in indices:
            self.loads.pop(index).wait()

    def ship(self, index, columns=None):
        held, ref, sem = self.outs[index]
        if columns is None:
            pltpu.make_async_copy(held, ref, sem).start()
        else:
            pltpu.make_async_copy(held.at[..., columns], ref.at[..., columns], sem).start()
        if index not in self.shipped:
            self.shipped.append(index)

    def finish(self):
        self.need(*list(self.loads))
        for index in self.outs:
            if index not in self.shipped:
                self.ship(index)
        for held, ref, sem in self.outs.values():
            pltpu.make_async_copy(held, ref, sem).wait()


def call(name, body, ins, outs, scratch, limit, cost=10**11, aliases=None):
    staged_in = [i for i, item in enumerate(ins) if item[1] == "far"]
    staged_out = [i for i, item in enumerate(outs) if item[1] == "far"]
    cuts = {i: (ins[i][2] if len(ins[i]) > 2 else None) for i in staged_in}

    def held_shape(i):
        array = ins[i][0]
        dims = array.shape if cuts[i] is None else (array.shape[0], cuts[i][1])
        return pltpu.VMEM(dims, array.dtype)

    specs = {"near": VM, "far": FAR, "raw": FAR, "any": ANY}
    n_in, n_out, n_scratch = len(ins), len(outs), len(scratch)

    def kernel(*refs):
        in_refs, refs = list(refs[:n_in]), refs[n_in:]
        out_refs, refs = list(refs[:n_out]), refs[n_out:]
        own, refs = refs[:n_scratch], refs[n_scratch:]
        held_in, refs = refs[: len(staged_in)], refs[len(staged_in) :]
        held_out, refs = refs[: len(staged_out)], refs[len(staged_out) :]
        in_sems, out_sems = refs
        io = Io(
            [(i, in_refs[i], cuts[i]) for i in staged_in],
            [(i, out_refs[i]) for i in staged_out],
            held_in, held_out, in_sems, out_sems,
        )
        for number, i in enumerate(staged_in):
            in_refs[i] = held_in[number]
        for number, i in enumerate(staged_out):
            out_refs[i] = held_out[number]
        body(io, in_refs, out_refs, *own)
        io.finish()

    args = [
        pltpu.with_memory_space_constraint(item[0], pltpu.HBM) if item[1] in ("far", "raw") else item[0]
        for item in ins
    ]
    return pl.pallas_call(
        kernel,
        out_shape=[pltpu.HBM(o.shape, o.dtype) if kind in ("far", "raw") else o for o, kind in outs],
        in_specs=[specs[item[1]] for item in ins],
        out_specs=[specs[kind] for _, kind in outs],
        scratch_shapes=[
            *scratch,
            *[held_shape(i) for i in staged_in],
            *[pltpu.VMEM(outs[i][0].shape, outs[i][0].dtype) for i in staged_out],
            pltpu.SemaphoreType.DMA((max(1, len(staged_in)),)),
            pltpu.SemaphoreType.DMA((max(1, len(staged_out)),)),
        ],
        input_output_aliases=aliases or {},
        compiler_params=pltpu.CompilerParams(vmem_limit_bytes=limit * MIB),
        cost_estimate=pl.CostEstimate(flops=cost, bytes_accessed=1, transcendentals=0),
        name=name,
    )(*args)


def far(*arrays):
    return [(array, "far") for array in arrays]


def norm_of(values):
    center = values - jnp.mean(values, axis=-1, keepdims=True)
    inverse = lax.rsqrt(jnp.mean(center * center, axis=-1, keepdims=True) + 1e-05)
    return center * inverse, inverse


def norm_back(upstream, normed, inverse, gain):
    scaled = upstream * gain
    return inverse * (
        scaled
        - jnp.mean(scaled, axis=-1, keepdims=True)
        - normed * jnp.mean(scaled * normed, axis=-1, keepdims=True)
    )


def fill_bias(plan, bias, seg_ref, pad_ref):
    length = bias.shape[0]
    row = pl.ds(lax.axis_index("seq"), 1)
    seg, pad = seg_ref[row, :], pad_ref[row, :]
    code = (2 * seg + pad).astype(F32)
    wanted = (2 * seg + 1).astype(F32)
    coded = jnp.broadcast_to(code, (length, length)).T
    rows = lax.broadcasted_iota(jnp.int32, (length, length), 0)
    cols = lax.broadcasted_iota(jnp.int32, (length, length), 1)
    bias[...] = jnp.where((coded == wanted) | (rows == cols), 0.0, -1e30)


def halves_of(values):
    lane = lax.broadcasted_iota(jnp.int32, values.shape, 1)
    zero = jnp.zeros_like(values)
    return jnp.where(lane < HD, values, zero), jnp.where(lane < HD, zero, values)


def prepare(plan, matrices, norm_params):
    groups = [matrices[0:3], matrices[3:5], matrices[5:6]]

    def body(io, ins, outs):
        io.start()
        core = lax.axis_index("seq") & 1
        first = 0
        rows = norm_params.shape[1]
        same = lax.broadcasted_iota(jnp.int32, (rows, rows), 0) == lax.broadcasted_iota(jnp.int32, (rows, rows), 1)
        lane = lax.broadcasted_iota(jnp.int32, (rows, 128), 1)
        side = jnp.zeros((rows, 128), F32)
        for p in range(norm_params.shape[0]):
            row = jnp.broadcast_to(ins[-1][p : p + 1, :], (rows, rows))
            column = jnp.sum(jnp.where(same, row, 0.0), axis=1, keepdims=True)
            side = jnp.where(lane == p, column, side)
        for out in outs[:2]:
            out[:, 3 * HALF :] = side.astype(BF)
        for number, group in enumerate(groups):
            at = 0
            for index in range(first, first + len(group)):
                io.need(index)
                size = ins[index].shape[1] // 2
                left, right = ins[index][:, :size], ins[index][:, size:]
                mine = jnp.where(core == 0, left, right).astype(BF)
                other = jnp.where(core == 0, right, left).astype(BF)
                outs[2 * number][:, at : at + size] = mine
                outs[2 * number + 1][:, at : at + size] = other
                at += size
            first += len(group)

    outs = []
    for group in groups:
        width = sum(w.shape[1] for w in group) // 2 + (128 if group is groups[0] else 0)
        outs += [(shape((group[0].shape[0], width), BF), "near")] * 2
    flat_outs = call("prepare", body, [*far(*matrices), (norm_params, "near")], outs, [], 8)
    return flat_outs[0:2], flat_outs[2:4], flat_outs[4:6]


def other_rows(plan, arrays):
    others = plan.seq - 1

    def body(io, ins, outs, held, in_sems, out_sems):
        mine = lax.axis_index("seq")
        loads = [
            pltpu.make_async_copy(ins[i // others].at[mine ^ (i % others + 1)], held.at[i], in_sems.at[i])
            for i in range(len(outs))
        ]
        for load in loads:
            load.start()
        puts = [pltpu.make_async_copy(held.at[i], outs[i], out_sems.at[i]) for i in range(len(outs))]
        for load, put in zip(loads, puts):
            load.wait()
            put.start()
        for put in puts:
            put.wait()

    part = arrays[0].shape[1:]
    count = others * len(arrays)
    outs = call(
        "other_rows", body, [(a, "raw") for a in arrays], [(shape(part, BF), "raw")] * count,
        [pltpu.VMEM((count, *part), BF), pltpu.SemaphoreType.DMA((count,)), pltpu.SemaphoreType.DMA((count,))],
        8,
    )
    return [outs[i * others : (i + 1) * others] for i in range(len(arrays))]


def row_blocks(length):
    for i in range(length // 128):
        yield slice(i * 128, (i + 1) * 128)


def project(plan, tokens, parts):
    length = tokens[0].size // D if len(tokens) == 1 else tokens[1].shape[0] * len(tokens)
    width = 3 * D + 256
    pieces = [(3 * HALF, 128, 3 * D), *[(m * HALF, HALF, m * D) for m in range(3)]]

    def body(io, ins, outs, whole, rows_in, sems, put_sems):
        h_ref, q_ref, k_ref, v_ref, n_ref, w_ref, x_ref = outs
        start_parts(plan, ins[len(tokens) :], whole, sems, pieces)
        loads = load_bands(plan, ins[: len(tokens)], rows_in, sems.at[pl.ds(4, len(tokens))])
        wait_part(whole, sems, 0, pieces[0])
        norms = flat(whole[:, :, :, 3 * D : 3 * D + 128]).astype(F32).T[0:8]
        n_ref[...] = norms
        for load in loads:
            load.wait()
        puts = [pltpu.make_async_copy(rows_in, x_ref, put_sems.at[1])]
        puts[0].start()
        for rows in row_blocks(length):
            normed, _ = norm_of(rows_in[rows, :].astype(F32))
            h_ref[rows, :] = (normed * norms[0:1, :] + norms[1:2, :]).astype(BF)
        io.ship(0)
        for m in range(3):
            wait_part(whole, sems, 1 + m, pieces[1 + m])
        puts.append(pltpu.make_async_copy(whole, w_ref, put_sems.at[0]))
        puts[1].start()
        for m, (out, scale) in enumerate(((q_ref, 0.125), (k_ref, 1.0), (v_ref, 1.0))):
            weight = flat(whole[:, :, :, m * D : (m + 1) * D])
            out[...] = (dot(h_ref[...], weight, 1, 0) * scale).astype(BF)
            io.ship(1 + m)
        for put in puts:
            put.wait()

    act = shape((length, D), BF)
    wide = plan.wide(D, width)
    return call(
        "project", body, [*[(t, "any") for t in tokens], *[(p, "any") for p in parts]],
        [*[(act, "far")] * 4, (shape((8, D), F32), "near"), (shape(wide, BF), "raw"), (act, "raw")],
        [
            pltpu.VMEM(wide, BF), pltpu.VMEM((length, D), BF),
            pltpu.SemaphoreType.DMA((4 + len(tokens),)), pltpu.SemaphoreType.DMA((2,)),
        ],
        20, 1,
    )


def mix(plan, query, key, value, seg, pad):
    length = query.shape[0]

    def body(io, ins, outs, bias):
        q_ref, k_ref, v_ref, seg_ref, pad_ref = ins
        at_ref, a_ref, l_ref = outs
        io.start()
        fill_bias(plan, bias, seg_ref, pad_ref)
        io.need(0, 1, 2)

        @pl.loop(0, PAIRS, unroll=True)
        def _(p):
            cols = pl.ds(pl.multiple_of(p * 128, 128), 128)
            keys = k_ref[:, cols]
            turned = v_ref[:, cols].T
            for half, query in enumerate(halves_of(q_ref[:, cols])):
                scores = dot(keys, query, 1, 1) + bias[...]
                top = jnp.max(scores, axis=0, keepdims=True)
                lifted = jnp.exp(scores - top)
                total = jnp.sum(lifted, axis=0, keepdims=True)
                soft = (lifted * (1.0 / total)).astype(BF)
                mixed = dot(turned[half * HD : (half + 1) * HD], soft, 1, 0)
                at_ref[pl.ds(pl.multiple_of(p * 128 + half * HD, HD), HD), :] = mixed.astype(BF)
                l_ref[pl.ds(2 * p + half, 1), :] = top + jnp.log(total)
            a_ref[:, cols] = at_ref[pl.ds(pl.multiple_of(p * 128, 128), 128), :].T

    return call(
        "mix", body, [*far(query, key, value), (seg, "near"), (pad, "near")],
        [(shape((D, length), BF), "far"), (shape((length, D), BF), "far"), (shape((H, length), F32), "far")],
        [pltpu.VMEM((length, length), F32)],
        14,
    )


def widen(plan, tokens, mixed, norms, parts):
    length = tokens.shape[0]
    pieces = [(0, HALF, 0), (HALF, 2 * D, D)]

    def body(io, ins, outs, whole, sems, put_sems):
        x_ref, a_ref, n_ref, *part_refs = ins
        m_ref, h_ref, z_ref, s_ref, w_ref = outs
        io.start(1)
        start_parts(plan, part_refs, whole, sems, pieces[:1])
        io.start(0)
        start_parts(plan, part_refs, whole, sems.at[pl.ds(1, 1)], pieces[1:])
        io.need(0, 1)
        wait_part(whole, sems, 0, pieces[0])
        m_ref[...] = x_ref[...].astype(F32) + dot(a_ref[...], flat(whole[:, :, :, 0:D]), 1, 0)
        io.ship(0)
        for rows in row_blocks(length):
            normed, _ = norm_of(m_ref[rows, :])
            h_ref[rows, :] = (normed * n_ref[2:3, :] + n_ref[3:4, :]).astype(BF)
        io.ship(1)
        wait_part(whole, sems, 1, pieces[1])
        put = pltpu.make_async_copy(whole, w_ref, put_sems.at[0])
        put.start()
        for block in range(BLOCKS):
            cols = slice(block * D, (block + 1) * D)
            up = dot(h_ref[...], flat(whole[:, :, :, (block + 1) * D : (block + 2) * D]), 1, 0)
            bell = 0.5 + 0.5 * lax.erf(up * 0.7071067811865476)
            z_ref[:, cols] = (up * bell).astype(BF)
            s_ref[:, cols] = (bell + up * (jnp.exp(-0.5 * up * up) * 0.3989422804014327)).astype(BF)
            io.ship(2, pl.ds(block * D, D))
            io.ship(3, pl.ds(block * D, D))
        put.wait()

    act = shape((length, D), BF)
    wide = plan.wide(D, D + FF)
    hidden = shape((length, FF), BF)
    outs = [shape((length, D), F32), act, hidden, hidden]
    return call(
        "widen", body, [*far(tokens, mixed), (norms, "near"), *[(p, "any") for p in parts]],
        [*[(o, "far") for o in outs], (shape(wide, BF), "raw")],
        [pltpu.VMEM(wide, BF), pltpu.SemaphoreType.DMA((2,)), pltpu.SemaphoreType.DMA((1,))],
        28,
    )


def grad_of_down(plan, hidden, cot):
    length = hidden.shape[0]

    def body(io, ins, outs, g_in, z_in, sems, z_sems, put_sems, g_sem, held):
        z_ref, *bands = ins
        *grads, g_out = outs
        loads = load_bands(plan, bands, g_in, sems)
        z_loads = [
            pltpu.make_async_copy(z_ref.at[:, pl.ds(i * D, D)], z_in.at[:, pl.ds(i * D, D)], z_sems.at[i])
            for i in range(BLOCKS)
        ]
        for load in z_loads:
            load.start()
        for load in loads:
            load.wait()
        puts = [pltpu.make_async_copy(g_in, g_out, g_sem.at[0])]
        puts[0].start()
        for block in range(BLOCKS):
            z_loads[block].wait()
            tile = dot(z_in[:, block * D : (block + 1) * D], g_in[...], 0, 0)
            store_grad(plan, tile, held, FF, block * D, slice(None))
            view = (slice(None), pl.ds(block, 1)) if plan.fast else (pl.ds(block * D, D),)
            puts += put_grad(held, grads, put_sems.at[block], view, view)
        for put in puts:
            put.wait()

    act = shape((length, D), BF)
    grads = plan.grads(FF, D)
    return call(
        "grad_of_down", body, [(hidden, "raw"), *[(c, "any") for c in cot]],
        [*[(g, "raw") for g in grads], (act, "raw")],
        [
            pltpu.VMEM((length, D), BF), pltpu.VMEM((length, FF), BF),
            pltpu.SemaphoreType.DMA((len(cot),)), pltpu.SemaphoreType.DMA((BLOCKS,)),
            pltpu.SemaphoreType.DMA((BLOCKS, len(grads))), pltpu.SemaphoreType.DMA((1,)),
            held_grad(plan, FF, D),
        ],
        28,
    )


def narrow(plan, blocks, mid, below, grads, low, hidden, slope, cot, whole_ou, parts_down):
    length = mid.shape[0]
    count = len(blocks)
    start, final = blocks[0] == 0, blocks[-1] == BLOCKS - 1
    cut = (blocks[0] * D, count * D)
    n_out = plan.outs()

    def body(io, ins, outs, *scratch):
        m_ref, h_ref, z_ref, s_ref, g_ref, up_ref, *rest = ins
        downs = rest[: len(parts_down)]
        b_ref, *grad_refs = outs[: 1 + n_out]
        o_refs = outs[1 + n_out :]
        held, du_ref, acc, whole_up, whole_down, sems, put_sems = scratch
        copies = []
        down = (0, HALF, 0)
        io.start(4)
        start_parts(plan, downs, whole_down, sems.at[pl.ds(0, 1)], [down], blocks)
        io.start(3, 1)
        up = pltpu.make_async_copy(up_ref.at[..., pl.ds(D + cut[0], cut[1])], whole_up, sems.at[1])
        up.start()
        io.start()
        io.need(4)
        wait_part(whole_down, sems, 0, down)
        io.need(3, 1)
        for number, block in enumerate(blocks):
            local = slice(number * D, (number + 1) * D)
            back = dot(g_ref[...], flat(whole_down[number]), 1, 1)
            du_ref[:, local] = (back * s_ref[:, local]).astype(BF)
            tile = dot(h_ref[...], du_ref[:, local], 0, 0)
            store_grad(plan, tile, held, D, 0, local)
            views = [(*[slice(None)] * (plan.grads(D, D)[0].ndim - 1), pl.ds(at * D, D)) for at in (number, block)]
            copies += put_grad(held, grad_refs, put_sems.at[number], *views)
        up.wait()
        lower = dot(du_ref[...], flat(whole_up[...]), 1, 1)
        if start:
            b_ref[...] = lower
        else:
            io.need(6 + len(parts_down))
            b_ref[...] = rest[len(parts_down)][...] + lower
        io.ship(0)
        io.need(0, 2)
        gain = m_ref[...] + dot(z_ref[...], whole_down[...].reshape(count * D, D), 1, 0)
        if final:
            acc[...] = gain
            for number, o_ref in enumerate(o_refs):
                o_ref[...] = acc[band(plan, number, length), :].astype(BF)
        else:
            o_refs[0][...] = gain
        for copy in copies:
            copy.wait()

    deep = plan.wide(FF, D)
    ins = [
        *far(mid, low), (hidden, "far", cut), (slope, "far", cut), *far(cot), (whole_ou, "raw"),
        *[(p, "any") for p in parts_down],
    ]
    aliases = {}
    if not start:
        ins += far(below)
        aliases = {len(ins) + i: 1 + i for i in range(n_out)}
        ins += [(g, "raw") for g in grads]
    return call(
        "narrow" + str(blocks[0]), body, ins,
        [
            (shape((length, D), F32), "far"), *[(g, "raw") for g in plan.grads(D, FF)],
            *[(o, "far") for o in (plan.band_shapes(length) if final else [shape((length, D), F32)])],
        ],
        [
            held_grad(plan, D, count * D),
            pltpu.VMEM((length, count * D), BF),
            pltpu.VMEM((length, D), F32),
            pltpu.VMEM(plan.wide(D, count * D), BF),
            pltpu.VMEM((count, *deep[1:]), BF),
            pltpu.SemaphoreType.DMA((2,)),
            pltpu.SemaphoreType.DMA((count, n_out)),
        ],
        40, aliases=aliases,
    )


def turn(plan, mid, back, cot, norms, whole_ou):
    length = mid.shape[0]

    def body(io, ins, outs, whole, sems):
        m_ref, b_ref, g_ref, n_ref, w_ref = ins
        x_ref, low, d_ref, s_ref = outs
        io.start()
        load = pltpu.make_async_copy(w_ref.at[..., pl.ds(0, D)], whole, sems.at[0])
        load.start()
        s_ref[...] = jnp.zeros_like(s_ref)
        io.need(0, 1, 2)
        for rows in row_blocks(length):
            normed, inverse = norm_of(m_ref[rows, :])
            upstream = b_ref[rows, :]
            total = g_ref[rows, :].astype(F32) + norm_back(upstream, normed, inverse, n_ref[2:3, :])
            x_ref[rows, :] = total
            low[rows, :] = total.astype(BF)
            s_ref[0:1, :] += jnp.sum(upstream * normed, axis=0, keepdims=True)
            s_ref[1:2, :] += jnp.sum(upstream, axis=0, keepdims=True)
        io.ship(0)
        io.ship(1)
        load.wait()
        d_ref[...] = dot(low[...], flat(whole[...]), 1, 1).astype(BF)

    act = shape((length, D), BF)
    return call(
        "turn", body, [*far(mid, back, cot), (norms, "near"), (whole_ou, "raw")],
        [(shape((length, D), F32), "far"), (act, "far"), (act, "far"), (shape((2, D), F32), "near")],
        [pltpu.VMEM(plan.wide(D, D), BF), pltpu.SemaphoreType.DMA((1,))],
        24,
    )


def attend_back(plan, side, low, query, key, value, lse, cot, seg, pad, extra=()):
    length = low.shape[0]
    width = 3 * HALF + (D if extra else 0)
    cut = (side * HALF, HALF)

    def body(io, ins, outs, bias, held, put_sems):
        h_ref, q_ref, k_ref, v_ref, c_ref, l_ref, seg_ref, pad_ref, *more = ins
        d_ref, *grads = outs
        io.start(1, 2, 3, 4, 5)
        io.start()
        fill_bias(plan, bias, seg_ref, pad_ref)
        io.need(1, 2, 3, 4, 5)

        @pl.loop(0, PAIRS // 2)
        def _(local):
            p = local + side * (PAIRS // 2)
            first = pl.multiple_of(local * 128, 128)
            cols = pl.ds(first, 128)
            keys, values = k_ref[:, cols], v_ref[:, cols]
            turned = keys.T
            queries, cots = halves_of(q_ref[:, cols]), halves_of(c_ref[:, cols])
            dv = dk = None
            dqs = []
            for half in range(2):
                scores = dot(keys, queries[half], 1, 1) + bias[...]
                soft = jnp.exp(scores - l_ref[pl.ds(2 * p + half, 1), :])
                gain = dot(soft.astype(BF), cots[half], 1, 0)
                dv = gain if dv is None else dv + gain
                dp = dot(values, cots[half], 1, 1)
                share = jnp.sum(soft * dp, axis=0, keepdims=True)
                ds = (soft * (dp - share)).astype(BF)
                gain = dot(ds, queries[half], 1, 0)
                dk = gain if dk is None else dk + gain
                dqs.append(dot(turned[half * HD : (half + 1) * HD], ds, 1, 0) * 0.125)
            d_ref[:, cols] = jnp.concatenate(dqs, axis=0).T.astype(BF)
            d_ref[:, pl.ds(first + HALF, 128)] = dk.astype(BF)
            d_ref[:, pl.ds(first + 2 * HALF, 128)] = dv.astype(BF)

        io.ship(0)
        io.need(0)
        lead, copies = [slice(None)] * (len(grads[0].shape) - 1), []
        if extra:
            io.need(8, 9)
            tile = dot(more[0][...], more[1][...], 1, 0)
            store_grad(plan, tile, held, D, 0, slice(3 * HALF, width))
            view = (*lead, pl.ds(3 * HALF, D))
            copies += put_grad(held, grads, put_sems.at[3], view, view)
        for m in range(3):
            cols = slice(m * HALF, (m + 1) * HALF)
            store_grad(plan, dot(h_ref[...], d_ref[:, cols], 0, 0), held, D, 0, cols)
            view = (*lead, pl.ds(m * HALF, HALF))
            copies += put_grad(held, grads, put_sems.at[m], view, view)
        for copy in copies:
            copy.wait()

    return call(
        "attend_back" + str(side), body,
        [
            *far(low), *[(a, "far", cut) for a in (query, key, value, cot)], *far(lse),
            (seg, "near"), (pad, "near"), *far(*extra),
        ],
        [(shape((length, 3 * HALF), BF), "far"), *[(g, "raw") for g in plan.grads(D, width)]],
        [
            pltpu.VMEM((length, length), F32), held_grad(plan, D, width),
            pltpu.SemaphoreType.DMA((4, plan.outs())),
        ],
        26,
    )


def finish_tokens(plan, tokens, spreads, mid_cot, norms, whole_qkv):
    length = tokens.shape[0]

    def body(io, ins, outs, back, whole, sems):
        x_ref, d0_ref, d1_ref, c_ref, n_ref, w_ref = ins
        *o_refs, s_ref = outs
        io.start(1, 2)
        load = pltpu.make_async_copy(w_ref.at[..., pl.ds(0, 3 * D)], whole, sems.at[0])
        load.start()
        io.start()
        s_ref[...] = jnp.zeros_like(s_ref)
        io.need(1, 2)
        load.wait()
        back[...] = sum(
            dot(
                jnp.concatenate([d[:, m * HALF : (m + 1) * HALF] for d in (d0_ref, d1_ref)], axis=1),
                flat(whole[:, :, :, m * D : (m + 1) * D]), 1, 1,
            )
            for m in range(3)
        )
        io.need(0, 3)
        for rows in row_blocks(length):
            normed, inverse = norm_of(x_ref[rows, :].astype(F32))
            upstream = back[rows, :]
            c_ref[rows, :] += norm_back(upstream, normed, inverse, n_ref[0:1, :])
            s_ref[0:1, :] += jnp.sum(upstream * normed, axis=0, keepdims=True)
            s_ref[1:2, :] += jnp.sum(upstream, axis=0, keepdims=True)
        for number, o_ref in enumerate(o_refs):
            o_ref[...] = c_ref[band(plan, number, length), :].astype(BF)

    return call(
        "finish_tokens", body, [*far(tokens, *spreads, mid_cot), (norms, "near"), (whole_qkv, "raw")],
        [*[(o, "far") for o in plan.band_shapes(length)], (shape((2, D), F32), "near")],
        [pltpu.VMEM((length, D), F32), pltpu.VMEM(plan.wide(D, 3 * D), BF), pltpu.SemaphoreType.DMA((1,))],
        20, 1,
    )


def sum_up(plan, blocks, others, slices):
    nz, rows, columns = blocks.shape
    wide = 4 * D // plan.count

    def body(io, ins, outs, held, sems):
        blocks_ref, others_ref, slice_ref = ins
        g_ref, card_ref = outs
        loads = [pltpu.make_async_copy(blocks_ref.at[i], held.at[i], sems.at[i]) for i in range(nz)]
        for load in loads:
            load.start()
        for load in loads:
            load.wait()
        value = jnp.sum(held[...].astype(F32), axis=0)
        g_ref[...] = value
        left = jnp.sum(jnp.sum(value * value, axis=0, keepdims=True), axis=1, keepdims=True) + others_ref[0:1, 0:1]
        lane = lax.broadcasted_iota(jnp.int32, slice_ref.shape, 1)
        card = slice_ref[...]
        for i in range(3):
            piece = left.astype(BF).astype(F32)
            card = jnp.where(lane == wide + i, piece, card)
            left = left - piece
        card = card.astype(BF)
        for i in range(plan.count):
            card_ref[i] = card

    return call(
        "sum_up", body, [(blocks, "any"), (others, "near"), (slices, "near")],
        [(shape((rows, columns), F32), "near"), (shape((plan.count, *slices.shape), BF), "near")],
        [pltpu.VMEM(blocks.shape, BF), pltpu.SemaphoreType.DMA((nz,))], 8,
    )


def update(plan, grads, cards, masters, firsts, seconds, passed):
    rates = [D**-0.5] * 3 + [4.0 * D**-0.5, D**-0.5, FF**-0.5, 0.2]
    decays = [0.01] * 6 + [0.0]
    count = len(masters)
    given = len(grads)

    def body(io, ins, outs, total, sems):
        grad_refs, card_ref = ins[:given], ins[given]
        first = given + 1
        io.start(*(first + k * count + i for i in reversed(range(count)) for k in range(3)))
        io.start()
        sources, rows, _ = card_ref.shape
        split = min(2, sources)
        for c in range(split):
            cards_c = [card_ref[i].astype(F32) for i in range(c, sources, split)]
            total[c * rows : (c + 1) * rows, :] = sum(cards_c[1:], cards_c[0])
        wide = 4 * D // plan.count
        all_norms = total[...]
        lane = lax.broadcasted_iota(jnp.int32, all_norms.shape, 1)
        own = jnp.where(lane < wide, all_norms * all_norms, all_norms * (1.0 / rows))
        square = jnp.sum(jnp.sum(own, axis=0, keepdims=True), axis=1, keepdims=True)
        norm = jnp.sqrt(square)
        outs[0][...] = jnp.broadcast_to(norm, outs[0].shape)
        factor = jnp.minimum(1.0, clip_limit / (norm + 1e-06))
        place_of = lax.axis_index("dp") * plan.seq + lax.axis_index("seq")
        if split == 2:
            place_of = (place_of & 1) * rows + (place_of >> 1)
        mine = total[pl.ds(place_of, 1), :]
        each = wide // 4
        grad_norms = jnp.concatenate([mine[:, p * each : (p + 1) * each] for p in range(4)], axis=0)
        for i in reversed(range(count)):
            w_ref, m_ref, s_ref = (ins[first + k * count + i] for k in range(3))
            io.need(*(first + k * count + i for k in range(3)))
            if i < 3:
                cols = [
                    (slice(h * HALF, (h + 1) * HALF), grad_refs[0][:, (5 * h + i) * HALF : (5 * h + i + 1) * HALF])
                    for h in range(2)
                ]
            elif i == 3:
                cols = [(slice(None), grad_refs[0][:, 3 * HALF : 5 * HALF])]
            elif i < 6:
                cols = [(slice(None), grad_refs[i - 3][...])]
            else:
                cols = [(slice(None), grad_norms)]
            for where, grad in cols:
                clipped = factor * grad
                one = 0.5 * m_ref[:, where] + 0.5 * clipped
                two = 0.55 * s_ref[:, where] + 0.45 * clipped * clipped
                root = jnp.sqrt(two * (1.0 / (1.0 - 0.55**STEP))) + 1e-08
                weight = w_ref[:, where]
                step = (one * (1.0 / (1.0 - 0.5**STEP))) / root + decays[i] * weight
                outs[1 + i][:, where] = weight - rates[i] * step
                outs[1 + count + i][:, where] = one
                outs[1 + 2 * count + i][:, where] = two
            for k in range(3):
                io.ship(1 + k * count + i)
        last = first + 3 * count
        copies = []
        for number in range(len(passed)):
            which, place_in = number // plan.bands(), number % plan.bands()
            io.need(last + number)
            target = outs[1 + 3 * count + which]
            if plan.bands() > 1:
                target = target.at[lax.axis_index("seq") ^ place_in]
            copies.append(pltpu.make_async_copy(ins[last + number], target, sems.at[number]))
            copies[-1].start()
        for copy in copies:
            copy.wait()

    like = [(shape(w.shape, F32), "far") for w in masters] * 3
    pieces = [shape((plan.bands(), *p.shape), BF) if plan.bands() > 1 else p for p in passed[:: plan.bands()]]
    return call(
        "update", body, [*[(g, "near") for g in grads], (cards, "near"), *far(*masters, *firsts, *seconds, *passed)],
        [(shape((1, 128), F32), "near"), *like, *[(o, "raw") for o in pieces]],
        [pltpu.VMEM((min(2, cards.shape[0]) * cards.shape[1], 128), F32), pltpu.SemaphoreType.DMA((len(passed),))], 20,
    )


def after(values, *others):
    return lax.optimization_barrier((values, others))[0]


def meet(*values):
    return lax.optimization_barrier(values)


def send(plan, values, perm):
    return lax.ppermute(values, AXES, perm)


def block_of(plan, mine, other):
    core = lax.axis_index("seq") & 1
    got = send(plan, other, plan.core)
    return jnp.where(core == 0, jnp.concatenate([mine, got]), jnp.concatenate([got, mine]))


def copies_of(plan, block):
    return jnp.broadcast_to(block[None], (plan.nz, *block.shape))


def along_z(plan, values):
    return lax.all_to_all(values, "dp", 0, 0, axis_index_groups=plan.groups, tiled=True)


def gather_whole(matrices):
    split = [w.reshape(w.shape[0], 2, -1) for w in matrices]
    halves = jnp.concatenate(split, axis=2).transpose(1, 0, 2).astype(BF)
    full = lax.all_gather(halves, AXES, axis=1, tiled=True)
    return [full.reshape(2, BLOCKS, 1, -1, full.shape[-1])]


def add(one, two):
    return one.astype(F32) + two.astype(F32)


def fold(keep, got):
    if keep.ndim == 4:
        keep, got = (v.reshape(-1, *v.shape[2:]) for v in (keep, got))
    size = keep.shape[0] // 2
    return add(keep[size:], got[size:]).astype(BF), add(keep[:size], got[:size]).astype(BF)


def total(blocks):
    return jnp.sum(blocks.astype(F32), axis=0)


def finish(plan, grads, sums, masters, firsts, seconds, *passed):
    wide = sums.shape[0] * D // plan.count
    slices = sums.reshape(sums.shape[0], plan.count, -1).transpose(1, 0, 2).reshape(plan.count, wide)
    slices = jnp.pad(slices, ((0, 0), (0, 128 - wide)))
    if plan.fast:
        core = lax.axis_index("seq") & 1
        pairs = slices.reshape(-1, 2, 128)
        mine, other = (lax.dynamic_index_in_dim(pairs, c, 1, keepdims=False) for c in (core, 1 - core))
        slices = mine + send(plan, other, plan.core)
        blocks, *others = grads
        left = jnp.broadcast_to(sum(jnp.sum(g * g) for g in others), (1, 128))
        left, slices, blocks, early = meet(left, slices, blocks, passed[:-1])
        passed = [*early, passed[-1]]
        last, cards = sum_up(plan, blocks, left, slices)
        grads = [last, *others]
        cards = lax.all_to_all(cards, AXES, 0, 0, tiled=True)
    else:
        left = jnp.broadcast_to(sum(jnp.sum(g * g) for g in grads), (plan.count, 1))
        cards = lax.psum(slices + jnp.pad(left, ((0, 0), (wide, 127 - wide))), AXES)[None]
    norm, *updated, output, input_grad = update(plan, grads, cards, masters, firsts, seconds, passed)
    return (output, input_grad, norm[0, 0], *updated)


def on_device(plan, *args):
    tokens_in, segment_ids, pad_mask, out_grad = args[:4]
    masters, firsts, seconds = args[4:11], args[11:18], args[18:25]
    each, piece, _ = tokens_in.shape
    length = each // plan.seq * plan.seq * piece

    plan.fast = plan.fast and each == plan.seq

    def swap(values, number):
        return lax.ppermute(values, "seq", [(i, i ^ number) for i in range(plan.seq)])

    def to_rows(values, others=None):
        if not plan.fast:
            return [lax.all_to_all(values, "seq", 0, 0, tiled=True).reshape(length, D)]
        return [values, *[swap(other, 1 + n) for n, other in enumerate(others)]]

    def to_pieces(bands):
        if not plan.fast:
            return [lax.all_to_all(bands[0].reshape(each, piece, D), "seq", 0, 0, tiled=True)]
        return [bands[0], *[swap(other, 1 + n) for n, other in enumerate(bands[1:])]]

    seg, pad = segment_ids, pad_mask

    if not plan.fast:
        side = jnp.pad(masters[6].T, ((0, 0), (0, 124)))
        side = jnp.concatenate([side, side], axis=1)
        one, two, three = (gather_whole(m) for m in ([*masters[0:3], side], masters[3:5], masters[5:6]))
        low_one, query, key, value, norms, whole_qkv, tokens = project(plan, to_rows(tokens_in), one)
        mixed_t, mixed, lse = mix(plan, query, key, value, seg, pad)
        mid, low_two, hidden, slope, whole_ou = widen(plan, tokens, mixed, norms, two)
        *g_down, cot = grad_of_down(plan, hidden, to_rows(out_grad))
        back, *g_up, part = narrow(plan, (0, 1), mid, None, None, low_two, hidden, slope, cot, whole_ou, three)
        back, *g_up, result = narrow(plan, (2, 3), part, back, g_up, low_two, hidden, slope, cot, whole_ou, three)
        mid_cot, low_cot, mixed_cot, sums_two = turn(plan, mid, back, cot, norms, whole_ou)
        halves = [
            attend_back(plan, side, low_one, query, key, value, lse, mixed_cot, seg, pad, extra)
            for side, extra in enumerate(((mixed_t, low_cot), ()))
        ]
        stream, sums_one = finish_tokens(plan, tokens, [h[0] for h in halves], mid_cot, norms, whole_qkv)
        grads = [
            lax.psum_scatter(g.astype(F32), AXES, scatter_dimension=0, tiled=True)
            for g in (halves[0][1], halves[1][1], *g_up, *g_down)
        ]
        grads = [jnp.concatenate(grads[:2], axis=1), *grads[2:]]
        sums = jnp.concatenate([sums_one, sums_two], axis=0)
        return finish(plan, grads, sums, masters, firsts, seconds, *to_pieces([result]), *to_pieces([stream]))

    first, second, third = prepare(plan, masters[:6], masters[6])
    block = block_of(plan, *first)
    near_one = along_z(plan, copies_of(plan, block))
    others, others_cot = other_rows(plan, [after(tokens_in, block), out_grad])
    tokens = to_rows(tokens_in, others)
    block_two = block_of(plan, *second)
    spread_two = copies_of(plan, block_two)
    spread_three = copies_of(plan, block_of(plan, *third))
    near_one, tokens, spread_two, spread_three = meet(near_one, tokens, spread_two, spread_three)

    def spread(near):
        return send(plan, near, plan.second), send(plan, near, plan.first)

    def to_core(*parts):
        return [send(plan, part, plan.core) for part in parts]

    beside_one, across_one = spread(near_one)
    near_two = along_z(plan, spread_two)
    beside_one, across_one = meet(beside_one, across_one)
    corner_one = send(plan, beside_one, plan.first)
    one = [near_one, beside_one, across_one]
    one_core = to_core(*one)
    corner_one, one_core = meet(corner_one, one_core)
    one = [*one, corner_one, *one_core, *to_core(corner_one)]
    low_one, query, key, value, norms, whole_qkv, tokens = project(plan, tokens, one)
    cot = to_rows(out_grad, after(others_cot, corner_one))
    near_two, query = meet(near_two, query)
    beside_two, across_two = spread(near_two)
    spread_three, cot = meet(after(spread_three, near_two), cot)
    near_three = along_z(plan, spread_three)
    mixed_t, mixed, lse = mix(plan, query, key, value, seg, pad)
    beside_two, across_two, mixed, lse, mixed_t = meet(beside_two, across_two, mixed, lse, mixed_t)
    corner_two = send(plan, beside_two, plan.first)
    two = [near_two, beside_two, across_two]
    two_core = to_core(*two)
    corner_two, two_core, near_three = meet(corner_two, two_core, near_three)
    beside_three, across_three = spread(near_three)
    two = [*two, corner_two, *two_core, *to_core(corner_two)]
    mid, low_two, hidden, slope, whole_ou = widen(plan, tokens, mixed, norms, two)
    beside_three, across_three, hidden = meet(beside_three, across_three, hidden)
    corner_three = send(plan, beside_three, plan.first)
    three = [near_three, beside_three, across_three]
    three_core = to_core(*three)
    keep_d, go_d, cot = grad_of_down(plan, hidden, cot)
    corner_three, three_core, keep_d, go_d, cot = meet(corner_three, three_core, keep_d, go_d, cot)
    three = [*three, corner_three, *three_core, *to_core(corner_three)]

    got_d = send(plan, go_d, plan.core)
    back, *g_up, part = narrow(plan, (0, 1), mid, None, None, low_two, hidden, slope, cot, whole_ou, three)
    got_d, back, part = meet(got_d, back, part)
    go_d, keep_d = fold(keep_d, got_d)
    got_d = send(plan, go_d, plan.first)
    part = after(part, go_d)
    back, *rest = narrow(plan, (2, 3), part, back, g_up, low_two, hidden, slope, cot, whole_ou, three)
    got_d, back, rest = meet(got_d, back, rest)
    (keep_u, go_u), result = rest[:2], rest[2:]
    got_u = send(plan, go_u, plan.core)
    go_d, keep_d = fold(keep_d, got_d)
    got_d = send(plan, go_d, plan.second)
    back = after(back, go_d)
    mid_cot, low_cot, mixed_cot, sums_two = turn(plan, mid, back, cot, norms, whole_ou)
    got_u, mixed_cot, low_cot, mid_cot, result = meet(got_u, mixed_cot, low_cot, mid_cot, result)
    go_u, keep_u = fold(keep_u, got_u)
    got_d, go_u = meet(got_d, go_u)
    got_u = send(plan, go_u, plan.first)
    mixed_cot = after(mixed_cot, go_u)
    spread_a, keep_a, go_a = attend_back(
        plan, 0, low_one, query, key, value, lse, mixed_cot, seg, pad, (mixed_t, low_cot)
    )
    got_u, keep_a, spread_a = meet(got_u, keep_a, spread_a)
    got_a = send(plan, go_a, plan.core)
    block_d = add(keep_d, got_d).astype(BF)
    blocks_d = along_z(plan, block_d)
    go_u, keep_u = fold(keep_u, got_u)
    got_u = send(plan, go_u, plan.second)
    go_a, keep_a = fold(keep_a, got_a)
    got_a = send(plan, go_a, plan.first)
    mixed_cot = after(mixed_cot, go_u, go_a, block_d)
    spread_b, keep_b, go_b = attend_back(plan, 1, low_one, query, key, value, lse, mixed_cot, seg, pad)
    blocks_d, got_u, got_a, keep_b, spread_b = meet(blocks_d, got_u, got_a, keep_b, spread_b)
    got_b = send(plan, go_b, plan.core)
    block_u = add(keep_u, got_u).astype(BF)
    blocks_u = along_z(plan, block_u)
    go_b, keep_b = fold(keep_b, after(got_b, block_u))
    got_b = send(plan, go_b, plan.first)
    go_a, keep_a = fold(keep_a, after(got_a, go_b))
    got_a = send(plan, go_a, plan.second)
    mid_cot = after(mid_cot, go_a, go_b)
    *stream, sums_one = finish_tokens(plan, tokens, [spread_a, spread_b], mid_cot, norms, whole_qkv)
    got_b, sums_one, stream = meet(got_b, sums_one, stream)
    go_b, keep_b = fold(keep_b, got_b)
    got_b = send(plan, go_b, plan.second)
    got_a = after(got_a, go_b)
    output = to_pieces(after(result, go_b))
    input_grad = to_pieces(after(stream, go_b))
    halves = [add(keep_a, got_a), add(keep_b, got_b)]
    blocks_ab = along_z(plan, jnp.concatenate(halves, axis=2).astype(BF))
    grads = [blocks_ab, total(blocks_u), total(blocks_d)]
    sums = jnp.concatenate([sums_one, sums_two], axis=0)
    return finish(plan, grads, sums, masters, firsts, seconds, *output, *input_grad)


def solution(mesh):
    plan = Plan(mesh, None)
    rows = P(AXES, None)
    weights = (*[rows] * 6, P(None, AXES))
    tokens = P("dp", "seq", None)
    return jax.shard_map(
        partial(on_device, plan),
        mesh=mesh,
        in_specs=(tokens, P("dp", None), P("dp", None), tokens, *weights * 3),
        out_specs=(tokens, tokens, P(), *weights * 3),
        check_vma=False,
    )
```

```python
from functools import partial

import jax
import jax.numpy as jnp
from jax import lax
from jax.experimental import pallas as pl
from jax.experimental.pallas import tpu as pltpu
from jax.sharding import PartitionSpec as P

D = 768
H = 12
HD = 64
FF = 3072
STEP = 7
HALF = D // 2
PAIRS = H // 2
BLOCKS = 4
BF = jnp.bfloat16
F32 = jnp.float32
AXES = ("dp", "seq")
clip_limit = 1.0
MIB = 2**20

VM = pl.BlockSpec(memory_space=pltpu.VMEM)
ANY = pl.BlockSpec(memory_space=pl.ANY)
FAR = pl.BlockSpec(memory_space=pltpu.HBM)


def dot(left, right, left_dim, right_dim):
    return lax.dot_general(
        left, right, (((left_dim,), (right_dim,)), ((), ())), preferred_element_type=F32
    )


def shape(dims, kind):
    return jax.ShapeDtypeStruct(dims, kind)


class Plan:
    def __init__(self, mesh, rows_each):
        self.dp = mesh.shape["dp"]
        self.seq = mesh.shape["seq"]
        self.count = self.dp * self.seq
        self.fast = (
            self.seq == 4
            and self.dp % 2 == 0
            and BLOCKS * 8 == self.count
            and (2 * D // self.count) % 16 == 0
        )
        self.nz = self.dp // 2
        self.rows = D // self.count
        self.far = FF // self.count
        both = range(self.count)
        self.core = [(d, d ^ 1) for d in both]
        self.first = [(d, d ^ (2 if d % 2 == 0 else 4)) for d in both]
        self.second = [(d, d ^ (4 if d % 2 == 0 else 2)) for d in both]
        self.groups = [list(range(low, self.dp, 2)) for low in range(2)]

    def wide(self, rows, columns):
        if self.fast:
            return (self.nz, 4, 2 * rows // self.count, columns)
        return (BLOCKS, 1, rows // BLOCKS, columns)

    def parts(self):
        return 8 if self.fast else 1

    def grads(self, rows, columns):
        if self.fast:
            half = shape((4, self.nz, rows // self.count, columns), BF)
            return [half, half]
        return [shape((rows, columns), BF)]

    def outs(self):
        return 2 if self.fast else 1

    def bands(self):
        return self.seq if self.fast else 1

    def band_shapes(self, length):
        return [shape((length // self.bands(), D), BF)] * self.bands()


def place():
    seq = lax.axis_index("seq")
    return seq & 1, seq >> 1, lax.axis_index("dp") & 1


def start_parts(plan, parts, whole, sems, pieces, blocks=None):
    blocks = slice(None) if blocks is None else pl.ds(blocks[0], len(blocks))
    for index, (first, size, to) in enumerate(pieces):
        columns = pl.ds(first, size)
        if len(parts) == 1:
            for half in range(2):
                pltpu.make_async_copy(
                    parts[0].at[half, blocks, :, :, columns], whole.at[..., pl.ds(to + half * size, size)], sems.at[index]
                ).start()
            continue
        core, mine_x, mine_y = place()
        for number, part in enumerate(parts):
            owner = core if number < 4 else 1 - core
            one, two = (number >> 1) & 1, number & 1
            off_x = jnp.where(owner == 0, one, two)
            off_y = jnp.where(owner == 0, two, one)
            spot = (mine_y ^ off_y) * 2 + (mine_x ^ off_x)
            target = pl.ds(pl.multiple_of(to + owner * size, 128), size)
            pltpu.make_async_copy(part.at[blocks, :, columns], whole.at[:, spot, :, target], sems.at[index]).start()


def wait_part(whole, sems, index, piece):
    view = whole.at[..., pl.ds(piece[2], 2 * piece[1])]
    pltpu.make_async_copy(view, view, sems.at[index]).wait()


def band(plan, number, length):
    if plan.bands() == 1:
        return pl.ds(0, length)
    size = length // plan.bands()
    return pl.ds(pl.multiple_of((lax.axis_index("seq") ^ number) * size, size), size)


def load_bands(plan, refs, whole, sems):
    copies = []
    for number, ref in enumerate(refs):
        source = ref.at[lax.axis_index("seq")] if number == 0 and plan.bands() > 1 else ref
        target = whole.at[band(plan, number, whole.shape[0]), :]
        copies.append(pltpu.make_async_copy(source, target, sems.at[number]))
    for copy in copies:
        copy.start()
    return copies


def flat(value):
    return value.reshape(-1, value.shape[-1])


def held_grad(plan, rows, columns):
    one = plan.grads(rows, columns)
    return pltpu.VMEM((len(one), *one[0].shape), BF)


def put_grad(held, outs, sems, held_view, out_view):
    copies = [
        pltpu.make_async_copy(held.at[(i, *held_view)], out.at[out_view], sems.at[i]) for i, out in enumerate(outs)
    ]
    for copy in copies:
        copy.start()
    return copies


def store_grad(plan, tile, held, rows, first_row, columns):
    if not plan.fast:
        held[0, pl.ds(first_row, tile.shape[0]), columns] = tile.astype(BF)
        return
    core, mine_x, mine_y = place()
    step = rows // plan.count

    def spot(pair, owner):
        off_x = (pair & 1) ^ mine_x
        off_y = ((pair >> 1) & 1) ^ mine_y
        return (off_x * 2 + off_y if owner == 0 else off_y * 2 + off_x), pair >> 2

    for local in range(tile.shape[0] // (2 * step)):
        pair = first_row // (2 * step) + local
        low = tile[2 * step * local : 2 * step * local + step]
        high = tile[2 * step * local + step : 2 * step * (local + 1)]
        held[core, *spot(pair, 0), :, columns] = low.astype(BF)
        held[1 - core, *spot(pair, 1), :, columns] = high.astype(BF)


class Io:
    def __init__(self, ins, outs, held_in, held_out, in_sems, out_sems):
        self.loads, self.running = {}, []
        for number, (index, ref, cut) in enumerate(ins):
            source = ref if cut is None else ref.at[:, pl.ds(*cut)]
            self.loads[index] = pltpu.make_async_copy(source, held_in[number], in_sems.at[number])
        self.outs = {
            index: (held_out[number], ref, out_sems.at[number]) for number, (index, ref) in enumerate(outs)
        }
        self.shipped = []

    def start(self, *indices):
        for index in indices or [i for i in self.loads if i not in self.running]:
            self.loads[index].start()
            self.running.append(index)

    def need(self, *indices):
        for index in indices:
            self.loads.pop(index).wait()

    def ship(self, index, columns=None):
        held, ref, sem = self.outs[index]
        if columns is None:
            pltpu.make_async_copy(held, ref, sem).start()
        else:
            pltpu.make_async_copy(held.at[..., columns], ref.at[..., columns], sem).start()
        if index not in self.shipped:
            self.shipped.append(index)

    def finish(self):
        self.need(*list(self.loads))
        for index in self.outs:
            if index not in self.shipped:
                self.ship(index)
        for held, ref, sem in self.outs.values():
            pltpu.make_async_copy(held, ref, sem).wait()


def call(name, body, ins, outs, scratch, limit, cost=10**11, aliases=None):
    staged_in = [i for i, item in enumerate(ins) if item[1] == "far"]
    staged_out = [i for i, item in enumerate(outs) if item[1] == "far"]
    cuts = {i: (ins[i][2] if len(ins[i]) > 2 else None) for i in staged_in}

    def held_shape(i):
        array = ins[i][0]
        dims = array.shape if cuts[i] is None else (array.shape[0], cuts[i][1])
        return pltpu.VMEM(dims, array.dtype)

    specs = {"near": VM, "far": FAR, "raw": FAR, "any": ANY}
    n_in, n_out, n_scratch = len(ins), len(outs), len(scratch)

    def kernel(*refs):
        in_refs, refs = list(refs[:n_in]), refs[n_in:]
        out_refs, refs = list(refs[:n_out]), refs[n_out:]
        own, refs = refs[:n_scratch], refs[n_scratch:]
        held_in, refs = refs[: len(staged_in)], refs[len(staged_in) :]
        held_out, refs = refs[: len(staged_out)], refs[len(staged_out) :]
        in_sems, out_sems = refs
        io = Io(
            [(i, in_refs[i], cuts[i]) for i in staged_in],
            [(i, out_refs[i]) for i in staged_out],
            held_in, held_out, in_sems, out_sems,
        )
        for number, i in enumerate(staged_in):
            in_refs[i] = held_in[number]
        for number, i in enumerate(staged_out):
            out_refs[i] = held_out[number]
        body(io, in_refs, out_refs, *own)
        io.finish()

    args = [
        pltpu.with_memory_space_constraint(item[0], pltpu.HBM) if item[1] in ("far", "raw") else item[0]
        for item in ins
    ]
    return pl.pallas_call(
        kernel,
        out_shape=[pltpu.HBM(o.shape, o.dtype) if kind in ("far", "raw") else o for o, kind in outs],
        in_specs=[specs[item[1]] for item in ins],
        out_specs=[specs[kind] for _, kind in outs],
        scratch_shapes=[
            *scratch,
            *[held_shape(i) for i in staged_in],
            *[pltpu.VMEM(outs[i][0].shape, outs[i][0].dtype) for i in staged_out],
            pltpu.SemaphoreType.DMA((max(1, len(staged_in)),)),
            pltpu.SemaphoreType.DMA((max(1, len(staged_out)),)),
        ],
        input_output_aliases=aliases or {},
        compiler_params=pltpu.CompilerParams(vmem_limit_bytes=limit * MIB),
        cost_estimate=pl.CostEstimate(flops=cost, bytes_accessed=1, transcendentals=0),
        name=name,
    )(*args)


def far(*arrays):
    return [(array, "far") for array in arrays]


def norm_of(values):
    center = values - jnp.mean(values, axis=-1, keepdims=True)
    inverse = lax.rsqrt(jnp.mean(center * center, axis=-1, keepdims=True) + 1e-05)
    return center * inverse, inverse


def norm_back(upstream, normed, inverse, gain):
    scaled = upstream * gain
    return inverse * (
        scaled
        - jnp.mean(scaled, axis=-1, keepdims=True)
        - normed * jnp.mean(scaled * normed, axis=-1, keepdims=True)
    )


def fill_bias(plan, bias, seg_ref, pad_ref):
    length = bias.shape[0]
    row = pl.ds(lax.axis_index("seq"), 1)
    seg, pad = seg_ref[row, :], pad_ref[row, :]
    code = (2 * seg + pad).astype(F32)
    wanted = (2 * seg + 1).astype(F32)
    coded = jnp.broadcast_to(code, (length, length)).T
    rows = lax.broadcasted_iota(jnp.int32, (length, length), 0)
    cols = lax.broadcasted_iota(jnp.int32, (length, length), 1)
    bias[...] = jnp.where((coded == wanted) | (rows == cols), 0.0, -1e30)


def halves_of(values):
    lane = lax.broadcasted_iota(jnp.int32, values.shape, 1)
    zero = jnp.zeros_like(values)
    return jnp.where(lane < HD, values, zero), jnp.where(lane < HD, zero, values)


def prepare(plan, matrices, norm_params):
    groups = [matrices[0:3], matrices[3:5], matrices[5:6]]

    def body(io, ins, outs):
        io.start()
        core = lax.axis_index("seq") & 1
        first = 0
        rows = norm_params.shape[1]
        same = lax.broadcasted_iota(jnp.int32, (rows, rows), 0) == lax.broadcasted_iota(jnp.int32, (rows, rows), 1)
        lane = lax.broadcasted_iota(jnp.int32, (rows, 128), 1)
        side = jnp.zeros((rows, 128), F32)
        for p in range(norm_params.shape[0]):
            row = jnp.broadcast_to(ins[-1][p : p + 1, :], (rows, rows))
            column = jnp.sum(jnp.where(same, row, 0.0), axis=1, keepdims=True)
            side = jnp.where(lane == p, column, side)
        for out in outs[:2]:
            out[:, 3 * HALF :] = side.astype(BF)
        for number, group in enumerate(groups):
            at = 0
            for index in range(first, first + len(group)):
                io.need(index)
                size = ins[index].shape[1] // 2
                left, right = ins[index][:, :size], ins[index][:, size:]
                mine = jnp.where(core == 0, left, right).astype(BF)
                other = jnp.where(core == 0, right, left).astype(BF)
                outs[2 * number][:, at : at + size] = mine
                outs[2 * number + 1][:, at : at + size] = other
                at += size
            first += len(group)

    outs = []
    for group in groups:
        width = sum(w.shape[1] for w in group) // 2 + (128 if group is groups[0] else 0)
        outs += [(shape((group[0].shape[0], width), BF), "near")] * 2
    flat_outs = call("prepare", body, [*far(*matrices), (norm_params, "near")], outs, [], 8)
    return flat_outs[0:2], flat_outs[2:4], flat_outs[4:6]


def other_rows(plan, arrays):
    others = plan.seq - 1

    def body(io, ins, outs, held, in_sems, out_sems):
        mine = lax.axis_index("seq")
        loads = [
            pltpu.make_async_copy(ins[i // others].at[mine ^ (i % others + 1)], held.at[i], in_sems.at[i])
            for i in range(len(outs))
        ]
        for load in loads:
            load.start()
        puts = [pltpu.make_async_copy(held.at[i], outs[i], out_sems.at[i]) for i in range(len(outs))]
        for load, put in zip(loads, puts):
            load.wait()
            put.start()
        for put in puts:
            put.wait()

    part = arrays[0].shape[1:]
    count = others * len(arrays)
    outs = call(
        "other_rows", body, [(a, "raw") for a in arrays], [(shape(part, BF), "raw")] * count,
        [pltpu.VMEM((count, *part), BF), pltpu.SemaphoreType.DMA((count,)), pltpu.SemaphoreType.DMA((count,))],
        8,
    )
    return [outs[i * others : (i + 1) * others] for i in range(len(arrays))]


def row_blocks(length):
    for i in range(length // 128):
        yield slice(i * 128, (i + 1) * 128)


def project(plan, tokens, parts):
    length = tokens[0].size // D if len(tokens) == 1 else tokens[1].shape[0] * len(tokens)
    width = 3 * D + 256
    pieces = [(3 * HALF, 128, 3 * D), *[(m * HALF, HALF, m * D) for m in range(3)]]

    def body(io, ins, outs, whole, rows_in, sems, put_sems):
        h_ref, q_ref, k_ref, v_ref, n_ref, w_ref, x_ref = outs
        start_parts(plan, ins[len(tokens) :], whole, sems, pieces)
        loads = load_bands(plan, ins[: len(tokens)], rows_in, sems.at[pl.ds(4, len(tokens))])
        wait_part(whole, sems, 0, pieces[0])
        norms = flat(whole[:, :, :, 3 * D : 3 * D + 128]).astype(F32).T[0:8]
        n_ref[...] = norms
        for load in loads:
            load.wait()
        puts = [pltpu.make_async_copy(rows_in, x_ref, put_sems.at[1])]
        puts[0].start()
        for rows in row_blocks(length):
            normed, _ = norm_of(rows_in[rows, :].astype(F32))
            h_ref[rows, :] = (normed * norms[0:1, :] + norms[1:2, :]).astype(BF)
        io.ship(0)
        for m in range(3):
            wait_part(whole, sems, 1 + m, pieces[1 + m])
        puts.append(pltpu.make_async_copy(whole, w_ref, put_sems.at[0]))
        puts[1].start()
        for m, (out, scale) in enumerate(((q_ref, 0.125), (k_ref, 1.0), (v_ref, 1.0))):
            weight = flat(whole[:, :, :, m * D : (m + 1) * D])
            out[...] = (dot(h_ref[...], weight, 1, 0) * scale).astype(BF)
            io.ship(1 + m)
        for put in puts:
            put.wait()

    act = shape((length, D), BF)
    wide = plan.wide(D, width)
    return call(
        "project", body, [*[(t, "any") for t in tokens], *[(p, "any") for p in parts]],
        [*[(act, "far")] * 4, (shape((8, D), F32), "near"), (shape(wide, BF), "raw"), (act, "raw")],
        [
            pltpu.VMEM(wide, BF), pltpu.VMEM((length, D), BF),
            pltpu.SemaphoreType.DMA((4 + len(tokens),)), pltpu.SemaphoreType.DMA((2,)),
        ],
        20, 1,
    )


def mix(plan, query, key, value, seg, pad):
    length = query.shape[0]

    def body(io, ins, outs, bias):
        q_ref, k_ref, v_ref, seg_ref, pad_ref = ins
        at_ref, a_ref, l_ref = outs
        io.start()
        fill_bias(plan, bias, seg_ref, pad_ref)
        io.need(0, 1, 2)

        @pl.loop(0, PAIRS, unroll=True)
        def _(p):
            cols = pl.ds(pl.multiple_of(p * 128, 128), 128)
            keys = k_ref[:, cols]
            turned = v_ref[:, cols].T
            for half, query in enumerate(halves_of(q_ref[:, cols])):
                scores = dot(keys, query, 1, 1) + bias[...]
                top = jnp.max(scores, axis=0, keepdims=True)
                lifted = jnp.exp(scores - top)
                total = jnp.sum(lifted, axis=0, keepdims=True)
                soft = (lifted * (1.0 / total)).astype(BF)
                mixed = dot(turned[half * HD : (half + 1) * HD], soft, 1, 0)
                at_ref[pl.ds(pl.multiple_of(p * 128 + half * HD, HD), HD), :] = mixed.astype(BF)
                l_ref[pl.ds(2 * p + half, 1), :] = top + jnp.log(total)
            a_ref[:, cols] = at_ref[pl.ds(pl.multiple_of(p * 128, 128), 128), :].T

    return call(
        "mix", body, [*far(query, key, value), (seg, "near"), (pad, "near")],
        [(shape((D, length), BF), "far"), (shape((length, D), BF), "far"), (shape((H, length), F32), "far")],
        [pltpu.VMEM((length, length), F32)],
        14,
    )


def widen(plan, tokens, mixed, norms, parts):
    length = tokens.shape[0]
    pieces = [(0, HALF, 0), (HALF, 2 * D, D)]

    def body(io, ins, outs, whole, sems, put_sems):
        x_ref, a_ref, n_ref, *part_refs = ins
        m_ref, h_ref, z_ref, s_ref, w_ref = outs
        io.start(1)
        start_parts(plan, part_refs, whole, sems, pieces[:1])
        io.start(0)
        start_parts(plan, part_refs, whole, sems.at[pl.ds(1, 1)], pieces[1:])
        io.need(0, 1)
        wait_part(whole, sems, 0, pieces[0])
        m_ref[...] = x_ref[...].astype(F32) + dot(a_ref[...], flat(whole[:, :, :, 0:D]), 1, 0)
        io.ship(0)
        for rows in row_blocks(length):
            normed, _ = norm_of(m_ref[rows, :])
            h_ref[rows, :] = (normed * n_ref[2:3, :] + n_ref[3:4, :]).astype(BF)
        io.ship(1)
        wait_part(whole, sems, 1, pieces[1])
        put = pltpu.make_async_copy(whole, w_ref, put_sems.at[0])
        put.start()
        for block in range(BLOCKS):
            cols = slice(block * D, (block + 1) * D)
            up = dot(h_ref[...], flat(whole[:, :, :, (block + 1) * D : (block + 2) * D]), 1, 0)
            bell = 0.5 + 0.5 * lax.erf(up * 0.7071067811865476)
            z_ref[:, cols] = (up * bell).astype(BF)
            s_ref[:, cols] = (bell + up * (jnp.exp(-0.5 * up * up) * 0.3989422804014327)).astype(BF)
            io.ship(2, pl.ds(block * D, D))
            io.ship(3, pl.ds(block * D, D))
        put.wait()

    act = shape((length, D), BF)
    wide = plan.wide(D, D + FF)
    hidden = shape((length, FF), BF)
    outs = [shape((length, D), F32), act, hidden, hidden]
    return call(
        "widen", body, [*far(tokens, mixed), (norms, "near"), *[(p, "any") for p in parts]],
        [*[(o, "far") for o in outs], (shape(wide, BF), "raw")],
        [pltpu.VMEM(wide, BF), pltpu.SemaphoreType.DMA((2,)), pltpu.SemaphoreType.DMA((1,))],
        28,
    )


def grad_of_down(plan, hidden, cot):
    length = hidden.shape[0]

    def body(io, ins, outs, g_in, z_in, sems, z_sems, put_sems, g_sem, held):
        z_ref, *bands = ins
        *grads, g_out = outs
        loads = load_bands(plan, bands, g_in, sems)
        z_loads = [
            pltpu.make_async_copy(z_ref.at[:, pl.ds(i * D, D)], z_in.at[:, pl.ds(i * D, D)], z_sems.at[i])
            for i in range(BLOCKS)
        ]
        for load in z_loads:
            load.start()
        for load in loads:
            load.wait()
        puts = [pltpu.make_async_copy(g_in, g_out, g_sem.at[0])]
        puts[0].start()
        for block in range(BLOCKS):
            z_loads[block].wait()
            tile = dot(z_in[:, block * D : (block + 1) * D], g_in[...], 0, 0)
            store_grad(plan, tile, held, FF, block * D, slice(None))
            view = (slice(None), pl.ds(block, 1)) if plan.fast else (pl.ds(block * D, D),)
            puts += put_grad(held, grads, put_sems.at[block], view, view)
        for put in puts:
            put.wait()

    act = shape((length, D), BF)
    grads = plan.grads(FF, D)
    return call(
        "grad_of_down", body, [(hidden, "raw"), *[(c, "any") for c in cot]],
        [*[(g, "raw") for g in grads], (act, "raw")],
        [
            pltpu.VMEM((length, D), BF), pltpu.VMEM((length, FF), BF),
            pltpu.SemaphoreType.DMA((len(cot),)), pltpu.SemaphoreType.DMA((BLOCKS,)),
            pltpu.SemaphoreType.DMA((BLOCKS, len(grads))), pltpu.SemaphoreType.DMA((1,)),
            held_grad(plan, FF, D),
        ],
        28,
    )


def narrow(plan, blocks, mid, below, grads, low, hidden, slope, cot, whole_ou, parts_down):
    length = mid.shape[0]
    count = len(blocks)
    start, final = blocks[0] == 0, blocks[-1] == BLOCKS - 1
    cut = (blocks[0] * D, count * D)
    n_out = plan.outs()

    def body(io, ins, outs, *scratch):
        m_ref, h_ref, z_ref, s_ref, g_ref, up_ref, *rest = ins
        downs = rest[: len(parts_down)]
        b_ref, *grad_refs = outs[: 1 + n_out]
        o_refs = outs[1 + n_out :]
        held, du_ref, acc, whole_up, whole_down, sems, put_sems = scratch
        copies = []
        down = (0, HALF, 0)
        io.start(4)
        start_parts(plan, downs, whole_down, sems.at[pl.ds(0, 1)], [down], blocks)
        io.start(3, 1)
        up = pltpu.make_async_copy(up_ref.at[..., pl.ds(D + cut[0], cut[1])], whole_up, sems.at[1])
        up.start()
        io.start()
        io.need(4)
        wait_part(whole_down, sems, 0, down)
        io.need(3, 1)
        for number, block in enumerate(blocks):
            local = slice(number * D, (number + 1) * D)
            back = dot(g_ref[...], flat(whole_down[number]), 1, 1)
            du_ref[:, local] = (back * s_ref[:, local]).astype(BF)
            tile = dot(h_ref[...], du_ref[:, local], 0, 0)
            store_grad(plan, tile, held, D, 0, local)
            views = [(*[slice(None)] * (plan.grads(D, D)[0].ndim - 1), pl.ds(at * D, D)) for at in (number, block)]
            copies += put_grad(held, grad_refs, put_sems.at[number], *views)
        up.wait()
        lower = dot(du_ref[...], flat(whole_up[...]), 1, 1)
        if start:
            b_ref[...] = lower
        else:
            io.need(6 + len(parts_down))
            b_ref[...] = rest[len(parts_down)][...] + lower
        io.ship(0)
        io.need(0, 2)
        gain = m_ref[...] + dot(z_ref[...], whole_down[...].reshape(count * D, D), 1, 0)
        if final:
            acc[...] = gain
            for number, o_ref in enumerate(o_refs):
                o_ref[...] = acc[band(plan, number, length), :].astype(BF)
        else:
            o_refs[0][...] = gain
        for copy in copies:
            copy.wait()

    deep = plan.wide(FF, D)
    ins = [
        *far(mid, low), (hidden, "far", cut), (slope, "far", cut), *far(cot), (whole_ou, "raw"),
        *[(p, "any") for p in parts_down],
    ]
    aliases = {}
    if not start:
        ins += far(below)
        aliases = {len(ins) + i: 1 + i for i in range(n_out)}
        ins += [(g, "raw") for g in grads]
    return call(
        "narrow" + str(blocks[0]), body, ins,
        [
            (shape((length, D), F32), "far"), *[(g, "raw") for g in plan.grads(D, FF)],
            *[(o, "far") for o in (plan.band_shapes(length) if final else [shape((length, D), F32)])],
        ],
        [
            held_grad(plan, D, count * D),
            pltpu.VMEM((length, count * D), BF),
            pltpu.VMEM((length, D), F32),
            pltpu.VMEM(plan.wide(D, count * D), BF),
            pltpu.VMEM((count, *deep[1:]), BF),
            pltpu.SemaphoreType.DMA((2,)),
            pltpu.SemaphoreType.DMA((count, n_out)),
        ],
        40, aliases=aliases,
    )


def turn(plan, mid, back, cot, norms, whole_ou):
    length = mid.shape[0]

    def body(io, ins, outs, whole, sems):
        m_ref, b_ref, g_ref, n_ref, w_ref = ins
        x_ref, low, d_ref, s_ref = outs
        io.start()
        load = pltpu.make_async_copy(w_ref.at[..., pl.ds(0, D)], whole, sems.at[0])
        load.start()
        s_ref[...] = jnp.zeros_like(s_ref)
        io.need(0, 1, 2)
        for rows in row_blocks(length):
            normed, inverse = norm_of(m_ref[rows, :])
            upstream = b_ref[rows, :]
            total = g_ref[rows, :].astype(F32) + norm_back(upstream, normed, inverse, n_ref[2:3, :])
            x_ref[rows, :] = total
            low[rows, :] = total.astype(BF)
            s_ref[0:1, :] += jnp.sum(upstream * normed, axis=0, keepdims=True)
            s_ref[1:2, :] += jnp.sum(upstream, axis=0, keepdims=True)
        io.ship(0)
        io.ship(1)
        load.wait()
        d_ref[...] = dot(low[...], flat(whole[...]), 1, 1).astype(BF)

    act = shape((length, D), BF)
    return call(
        "turn", body, [*far(mid, back, cot), (norms, "near"), (whole_ou, "raw")],
        [(shape((length, D), F32), "far"), (act, "far"), (act, "far"), (shape((2, D), F32), "near")],
        [pltpu.VMEM(plan.wide(D, D), BF), pltpu.SemaphoreType.DMA((1,))],
        24,
    )


def attend_back(plan, side, low, query, key, value, lse, cot, seg, pad, extra=()):
    length = low.shape[0]
    width = 3 * HALF + (D if extra else 0)
    cut = (side * HALF, HALF)

    def body(io, ins, outs, bias, held, put_sems):
        h_ref, q_ref, k_ref, v_ref, c_ref, l_ref, seg_ref, pad_ref, *more = ins
        d_ref, *grads = outs
        io.start(1, 2, 3, 4, 5)
        io.start()
        fill_bias(plan, bias, seg_ref, pad_ref)
        io.need(1, 2, 3, 4, 5)

        @pl.loop(0, PAIRS // 2)
        def _(local):
            p = local + side * (PAIRS // 2)
            first = pl.multiple_of(local * 128, 128)
            cols = pl.ds(first, 128)
            keys, values = k_ref[:, cols], v_ref[:, cols]
            turned = keys.T
            queries, cots = halves_of(q_ref[:, cols]), halves_of(c_ref[:, cols])
            dv = dk = None
            dqs = []
            for half in range(2):
                scores = dot(keys, queries[half], 1, 1) + bias[...]
                soft = jnp.exp(scores - l_ref[pl.ds(2 * p + half, 1), :])
                gain = dot(soft.astype(BF), cots[half], 1, 0)
                dv = gain if dv is None else dv + gain
                dp = dot(values, cots[half], 1, 1)
                share = jnp.sum(soft * dp, axis=0, keepdims=True)
                ds = (soft * (dp - share)).astype(BF)
                gain = dot(ds, queries[half], 1, 0)
                dk = gain if dk is None else dk + gain
                dqs.append(dot(turned[half * HD : (half + 1) * HD], ds, 1, 0) * 0.125)
            d_ref[:, cols] = jnp.concatenate(dqs, axis=0).T.astype(BF)
            d_ref[:, pl.ds(first + HALF, 128)] = dk.astype(BF)
            d_ref[:, pl.ds(first + 2 * HALF, 128)] = dv.astype(BF)

        io.ship(0)
        io.need(0)
        lead, copies = [slice(None)] * (len(grads[0].shape) - 1), []
        if extra:
            io.need(8, 9)
            tile = dot(more[0][...], more[1][...], 1, 0)
            store_grad(plan, tile, held, D, 0, slice(3 * HALF, width))
            view = (*lead, pl.ds(3 * HALF, D))
            copies += put_grad(held, grads, put_sems.at[3], view, view)
        for m in range(3):
            cols = slice(m * HALF, (m + 1) * HALF)
            store_grad(plan, dot(h_ref[...], d_ref[:, cols], 0, 0), held, D, 0, cols)
            view = (*lead, pl.ds(m * HALF, HALF))
            copies += put_grad(held, grads, put_sems.at[m], view, view)
        for copy in copies:
            copy.wait()

    return call(
        "attend_back" + str(side), body,
        [
            *far(low), *[(a, "far", cut) for a in (query, key, value, cot)], *far(lse),
            (seg, "near"), (pad, "near"), *far(*extra),
        ],
        [(shape((length, 3 * HALF), BF), "far"), *[(g, "raw") for g in plan.grads(D, width)]],
        [
            pltpu.VMEM((length, length), F32), held_grad(plan, D, width),
            pltpu.SemaphoreType.DMA((4, plan.outs())),
        ],
        26,
    )


def finish_tokens(plan, tokens, spreads, mid_cot, norms, whole_qkv):
    length = tokens.shape[0]

    def body(io, ins, outs, back, whole, sems):
        x_ref, d0_ref, d1_ref, c_ref, n_ref, w_ref = ins
        *o_refs, s_ref = outs
        io.start(1, 2)
        load = pltpu.make_async_copy(w_ref.at[..., pl.ds(0, 3 * D)], whole, sems.at[0])
        load.start()
        io.start()
        s_ref[...] = jnp.zeros_like(s_ref)
        io.need(1, 2)
        load.wait()
        back[...] = sum(
            dot(
                jnp.concatenate([d[:, m * HALF : (m + 1) * HALF] for d in (d0_ref, d1_ref)], axis=1),
                flat(whole[:, :, :, m * D : (m + 1) * D]), 1, 1,
            )
            for m in range(3)
        )
        io.need(0, 3)
        for rows in row_blocks(length):
            normed, inverse = norm_of(x_ref[rows, :].astype(F32))
            upstream = back[rows, :]
            c_ref[rows, :] += norm_back(upstream, normed, inverse, n_ref[0:1, :])
            s_ref[0:1, :] += jnp.sum(upstream * normed, axis=0, keepdims=True)
            s_ref[1:2, :] += jnp.sum(upstream, axis=0, keepdims=True)
        for number, o_ref in enumerate(o_refs):
            o_ref[...] = c_ref[band(plan, number, length), :].astype(BF)

    return call(
        "finish_tokens", body, [*far(tokens, *spreads, mid_cot), (norms, "near"), (whole_qkv, "raw")],
        [*[(o, "far") for o in plan.band_shapes(length)], (shape((2, D), F32), "near")],
        [pltpu.VMEM((length, D), F32), pltpu.VMEM(plan.wide(D, 3 * D), BF), pltpu.SemaphoreType.DMA((1,))],
        20, 1,
    )


def sum_up(plan, blocks, others, slices):
    nz, rows, columns = blocks.shape
    wide = 4 * D // plan.count

    def body(io, ins, outs, held, sems):
        blocks_ref, others_ref, slice_ref = ins
        g_ref, card_ref = outs
        loads = [pltpu.make_async_copy(blocks_ref.at[i], held.at[i], sems.at[i]) for i in range(nz)]
        for load in loads:
            load.start()
        for load in loads:
            load.wait()
        value = jnp.sum(held[...].astype(F32), axis=0)
        g_ref[...] = value
        left = jnp.sum(jnp.sum(value * value, axis=0, keepdims=True), axis=1, keepdims=True) + others_ref[0:1, 0:1]
        lane = lax.broadcasted_iota(jnp.int32, slice_ref.shape, 1)
        card = slice_ref[...]
        for i in range(3):
            piece = left.astype(BF).astype(F32)
            card = jnp.where(lane == wide + i, piece, card)
            left = left - piece
        card = card.astype(BF)
        for i in range(plan.count):
            card_ref[i] = card

    return call(
        "sum_up", body, [(blocks, "any"), (others, "near"), (slices, "near")],
        [(shape((rows, columns), F32), "near"), (shape((plan.count, *slices.shape), BF), "near")],
        [pltpu.VMEM(blocks.shape, BF), pltpu.SemaphoreType.DMA((nz,))], 8,
    )


def update(plan, grads, cards, masters, firsts, seconds, passed):
    rates = [D**-0.5] * 3 + [4.0 * D**-0.5, D**-0.5, FF**-0.5, 0.2]
    decays = [0.01] * 6 + [0.0]
    count = len(masters)
    given = len(grads)

    def body(io, ins, outs, total, sems):
        grad_refs, card_ref = ins[:given], ins[given]
        first = given + 1
        io.start(*(first + k * count + i for i in reversed(range(count)) for k in range(3)))
        io.start()
        sources, rows, _ = card_ref.shape
        split = min(2, sources)
        for c in range(split):
            cards_c = [card_ref[i].astype(F32) for i in range(c, sources, split)]
            total[c * rows : (c + 1) * rows, :] = sum(cards_c[1:], cards_c[0])
        wide = 4 * D // plan.count
        all_norms = total[...]
        lane = lax.broadcasted_iota(jnp.int32, all_norms.shape, 1)
        own = jnp.where(lane < wide, all_norms * all_norms, all_norms * (1.0 / rows))
        square = jnp.sum(jnp.sum(own, axis=0, keepdims=True), axis=1, keepdims=True)
        norm = jnp.sqrt(square)
        outs[0][...] = jnp.broadcast_to(norm, outs[0].shape)
        factor = jnp.minimum(1.0, clip_limit / (norm + 1e-06))
        place_of = lax.axis_index("dp") * plan.seq + lax.axis_index("seq")
        if split == 2:
            place_of = (place_of & 1) * rows + (place_of >> 1)
        mine = total[pl.ds(place_of, 1), :]
        each = wide // 4
        grad_norms = jnp.concatenate([mine[:, p * each : (p + 1) * each] for p in range(4)], axis=0)
        for i in reversed(range(count)):
            w_ref, m_ref, s_ref = (ins[first + k * count + i] for k in range(3))
            io.need(*(first + k * count + i for k in range(3)))
            if i < 3:
                cols = [
                    (slice(h * HALF, (h + 1) * HALF), grad_refs[0][:, (5 * h + i) * HALF : (5 * h + i + 1) * HALF])
                    for h in range(2)
                ]
            elif i == 3:
                cols = [(slice(None), grad_refs[0][:, 3 * HALF : 5 * HALF])]
            elif i < 6:
                cols = [(slice(None), grad_refs[i - 3][...])]
            else:
                cols = [(slice(None), grad_norms)]
            for where, grad in cols:
                clipped = factor * grad
                one = 0.5 * m_ref[:, where] + 0.5 * clipped
                two = 0.55 * s_ref[:, where] + 0.45 * clipped * clipped
                root = jnp.sqrt(two * (1.0 / (1.0 - 0.55**STEP))) + 1e-08
                weight = w_ref[:, where]
                step = (one * (1.0 / (1.0 - 0.5**STEP))) / root + decays[i] * weight
                outs[1 + i][:, where] = weight - rates[i] * step
                outs[1 + count + i][:, where] = one
                outs[1 + 2 * count + i][:, where] = two
            for k in range(3):
                io.ship(1 + k * count + i)
        last = first + 3 * count
        copies = []
        for number in range(len(passed)):
            which, place_in = number // plan.bands(), number % plan.bands()
            io.need(last + number)
            target = outs[1 + 3 * count + which]
            if plan.bands() > 1:
                target = target.at[lax.axis_index("seq") ^ place_in]
            copies.append(pltpu.make_async_copy(ins[last + number], target, sems.at[number]))
            copies[-1].start()
        for copy in copies:
            copy.wait()

    like = [(shape(w.shape, F32), "far") for w in masters] * 3
    pieces = [shape((plan.bands(), *p.shape), BF) if plan.bands() > 1 else p for p in passed[:: plan.bands()]]
    return call(
        "update", body, [*[(g, "near") for g in grads], (cards, "near"), *far(*masters, *firsts, *seconds, *passed)],
        [(shape((1, 128), F32), "near"), *like, *[(o, "raw") for o in pieces]],
        [pltpu.VMEM((min(2, cards.shape[0]) * cards.shape[1], 128), F32), pltpu.SemaphoreType.DMA((len(passed),))], 20,
    )


def after(values, *others):
    return lax.optimization_barrier((values, others))[0]


def meet(*values):
    return lax.optimization_barrier(values)


def send(plan, values, perm):
    return lax.ppermute(values, AXES, perm)


def block_of(plan, mine, other):
    core = lax.axis_index("seq") & 1
    got = send(plan, other, plan.core)
    return jnp.where(core == 0, jnp.concatenate([mine, got]), jnp.concatenate([got, mine]))


def copies_of(plan, block):
    return jnp.broadcast_to(block[None], (plan.nz, *block.shape))


def along_z(plan, values):
    return lax.all_to_all(values, "dp", 0, 0, axis_index_groups=plan.groups, tiled=True)


def gather_whole(matrices):
    split = [w.reshape(w.shape[0], 2, -1) for w in matrices]
    halves = jnp.concatenate(split, axis=2).transpose(1, 0, 2).astype(BF)
    full = lax.all_gather(halves, AXES, axis=1, tiled=True)
    return [full.reshape(2, BLOCKS, 1, -1, full.shape[-1])]


def add(one, two):
    return one.astype(F32) + two.astype(F32)


def fold(keep, got):
    if keep.ndim == 4:
        keep, got = (v.reshape(-1, *v.shape[2:]) for v in (keep, got))
    size = keep.shape[0] // 2
    return add(keep[size:], got[size:]).astype(BF), add(keep[:size], got[:size]).astype(BF)


def total(blocks):
    return jnp.sum(blocks.astype(F32), axis=0)


def finish(plan, grads, sums, masters, firsts, seconds, *passed):
    wide = sums.shape[0] * D // plan.count
    slices = sums.reshape(sums.shape[0], plan.count, -1).transpose(1, 0, 2).reshape(plan.count, wide)
    slices = jnp.pad(slices, ((0, 0), (0, 128 - wide)))
    if plan.fast:
        core = lax.axis_index("seq") & 1
        pairs = slices.reshape(-1, 2, 128)
        mine, other = (lax.dynamic_index_in_dim(pairs, c, 1, keepdims=False) for c in (core, 1 - core))
        slices = mine + send(plan, other, plan.core)
        blocks, *others = grads
        left = jnp.broadcast_to(sum(jnp.sum(g * g) for g in others), (1, 128))
        left, slices, blocks, passed = meet(left, slices, blocks, passed)
        last, cards = sum_up(plan, blocks, left, slices)
        grads = [last, *others]
        cards = lax.all_to_all(cards, AXES, 0, 0, tiled=True)
    else:
        left = jnp.broadcast_to(sum(jnp.sum(g * g) for g in grads), (plan.count, 1))
        cards = lax.psum(slices + jnp.pad(left, ((0, 0), (wide, 127 - wide))), AXES)[None]
    norm, *updated, output, input_grad = update(plan, grads, cards, masters, firsts, seconds, passed)
    return (output, input_grad, norm[0, 0], *updated)


def on_device(plan, *args):
    tokens_in, segment_ids, pad_mask, out_grad = args[:4]
    masters, firsts, seconds = args[4:11], args[11:18], args[18:25]
    each, piece, _ = tokens_in.shape
    length = each // plan.seq * plan.seq * piece

    plan.fast = plan.fast and each == plan.seq

    def swap(values, number):
        return lax.ppermute(values, "seq", [(i, i ^ number) for i in range(plan.seq)])

    def to_rows(values, others=None):
        if not plan.fast:
            return [lax.all_to_all(values, "seq", 0, 0, tiled=True).reshape(length, D)]
        return [values, *[swap(other, 1 + n) for n, other in enumerate(others)]]

    def to_pieces(bands):
        if not plan.fast:
            return [lax.all_to_all(bands[0].reshape(each, piece, D), "seq", 0, 0, tiled=True)]
        return [bands[0], *[swap(other, 1 + n) for n, other in enumerate(bands[1:])]]

    seg, pad = segment_ids, pad_mask

    if not plan.fast:
        side = jnp.pad(masters[6].T, ((0, 0), (0, 124)))
        side = jnp.concatenate([side, side], axis=1)
        one, two, three = (gather_whole(m) for m in ([*masters[0:3], side], masters[3:5], masters[5:6]))
        low_one, query, key, value, norms, whole_qkv, tokens = project(plan, to_rows(tokens_in), one)
        mixed_t, mixed, lse = mix(plan, query, key, value, seg, pad)
        mid, low_two, hidden, slope, whole_ou = widen(plan, tokens, mixed, norms, two)
        *g_down, cot = grad_of_down(plan, hidden, to_rows(out_grad))
        back, *g_up, part = narrow(plan, (0, 1), mid, None, None, low_two, hidden, slope, cot, whole_ou, three)
        back, *g_up, result = narrow(plan, (2, 3), part, back, g_up, low_two, hidden, slope, cot, whole_ou, three)
        mid_cot, low_cot, mixed_cot, sums_two = turn(plan, mid, back, cot, norms, whole_ou)
        halves = [
            attend_back(plan, side, low_one, query, key, value, lse, mixed_cot, seg, pad, extra)
            for side, extra in enumerate(((mixed_t, low_cot), ()))
        ]
        stream, sums_one = finish_tokens(plan, tokens, [h[0] for h in halves], mid_cot, norms, whole_qkv)
        grads = [
            lax.psum_scatter(g.astype(F32), AXES, scatter_dimension=0, tiled=True)
            for g in (halves[0][1], halves[1][1], *g_up, *g_down)
        ]
        grads = [jnp.concatenate(grads[:2], axis=1), *grads[2:]]
        sums = jnp.concatenate([sums_one, sums_two], axis=0)
        return finish(plan, grads, sums, masters, firsts, seconds, *to_pieces([result]), *to_pieces([stream]))

    first, second, third = prepare(plan, masters[:6], masters[6])
    block = block_of(plan, *first)
    near_one = along_z(plan, copies_of(plan, block))
    others, others_cot = other_rows(plan, [after(tokens_in, block), out_grad])
    tokens = to_rows(tokens_in, others)
    block_two = block_of(plan, *second)
    spread_two = copies_of(plan, block_two)
    spread_three = copies_of(plan, block_of(plan, *third))
    near_one, tokens, spread_two, spread_three = meet(near_one, tokens, spread_two, spread_three)

    def spread(near):
        return send(plan, near, plan.second), send(plan, near, plan.first)

    def to_core(*parts):
        return [send(plan, part, plan.core) for part in parts]

    beside_one, across_one = spread(near_one)
    near_two = along_z(plan, spread_two)
    beside_one, across_one = meet(beside_one, across_one)
    corner_one = send(plan, beside_one, plan.first)
    one = [near_one, beside_one, across_one]
    one_core = to_core(*one)
    corner_one, one_core = meet(corner_one, one_core)
    one = [*one, corner_one, *one_core, *to_core(corner_one)]
    low_one, query, key, value, norms, whole_qkv, tokens = project(plan, tokens, one)
    cot = to_rows(out_grad, after(others_cot, corner_one))
    near_two, query = meet(near_two, query)
    beside_two, across_two = spread(near_two)
    spread_three, cot = meet(after(spread_three, near_two), cot)
    near_three = along_z(plan, spread_three)
    mixed_t, mixed, lse = mix(plan, query, key, value, seg, pad)
    beside_two, across_two, mixed, lse, mixed_t = meet(beside_two, across_two, mixed, lse, mixed_t)
    corner_two = send(plan, beside_two, plan.first)
    two = [near_two, beside_two, across_two]
    two_core = to_core(*two)
    corner_two, two_core, near_three = meet(corner_two, two_core, near_three)
    beside_three, across_three = spread(near_three)
    two = [*two, corner_two, *two_core, *to_core(corner_two)]
    mid, low_two, hidden, slope, whole_ou = widen(plan, tokens, mixed, norms, two)
    beside_three, across_three, hidden = meet(beside_three, across_three, hidden)
    corner_three = send(plan, beside_three, plan.first)
    three = [near_three, beside_three, across_three]
    three_core = to_core(*three)
    keep_d, go_d, cot = grad_of_down(plan, hidden, cot)
    corner_three, three_core, keep_d, go_d, cot = meet(corner_three, three_core, keep_d, go_d, cot)
    three = [*three, corner_three, *three_core, *to_core(corner_three)]

    got_d = send(plan, go_d, plan.core)
    back, *g_up, part = narrow(plan, (0, 1), mid, None, None, low_two, hidden, slope, cot, whole_ou, three)
    got_d, back, part = meet(got_d, back, part)
    go_d, keep_d = fold(keep_d, got_d)
    got_d = send(plan, go_d, plan.first)
    part = after(part, go_d)
    back, *rest = narrow(plan, (2, 3), part, back, g_up, low_two, hidden, slope, cot, whole_ou, three)
    got_d, back, rest = meet(got_d, back, rest)
    (keep_u, go_u), result = rest[:2], rest[2:]
    got_u = send(plan, go_u, plan.core)
    go_d, keep_d = fold(keep_d, got_d)
    got_d = send(plan, go_d, plan.second)
    back = after(back, go_d)
    mid_cot, low_cot, mixed_cot, sums_two = turn(plan, mid, back, cot, norms, whole_ou)
    got_u, mixed_cot, low_cot, mid_cot, result = meet(got_u, mixed_cot, low_cot, mid_cot, result)
    go_u, keep_u = fold(keep_u, got_u)
    got_d, go_u = meet(got_d, go_u)
    got_u = send(plan, go_u, plan.first)
    mixed_cot = after(mixed_cot, go_u)
    spread_a, keep_a, go_a = attend_back(
        plan, 0, low_one, query, key, value, lse, mixed_cot, seg, pad, (mixed_t, low_cot)
    )
    got_u, keep_a, spread_a = meet(got_u, keep_a, spread_a)
    got_a = send(plan, go_a, plan.core)
    block_d = add(keep_d, got_d).astype(BF)
    blocks_d = along_z(plan, block_d)
    go_u, keep_u = fold(keep_u, got_u)
    got_u = send(plan, go_u, plan.second)
    go_a, keep_a = fold(keep_a, got_a)
    got_a = send(plan, go_a, plan.first)
    mixed_cot = after(mixed_cot, go_u, go_a, block_d)
    spread_b, keep_b, go_b = attend_back(plan, 1, low_one, query, key, value, lse, mixed_cot, seg, pad)
    blocks_d, got_u, got_a, keep_b, spread_b = meet(blocks_d, got_u, got_a, keep_b, spread_b)
    got_b = send(plan, go_b, plan.core)
    block_u = add(keep_u, got_u).astype(BF)
    blocks_u = along_z(plan, block_u)
    output = to_pieces(after(result, spread_b))
    go_b, keep_b = fold(keep_b, after(got_b, block_u, output))
    got_b = send(plan, go_b, plan.first)
    go_a, keep_a = fold(keep_a, after(got_a, go_b))
    got_a = send(plan, go_a, plan.second)
    mid_cot = after(mid_cot, go_a, go_b)
    *stream, sums_one = finish_tokens(plan, tokens, [spread_a, spread_b], mid_cot, norms, whole_qkv)
    got_b, sums_one, stream = meet(got_b, sums_one, stream)
    go_b, keep_b = fold(keep_b, got_b)
    got_b = send(plan, go_b, plan.second)
    got_a = after(got_a, go_b)
    input_grad = to_pieces(after(stream, go_b))
    halves = [add(keep_a, got_a), add(keep_b, got_b)]
    blocks_ab = along_z(plan, jnp.concatenate(halves, axis=2).astype(BF))
    grads = [blocks_ab, total(blocks_u), total(blocks_d)]
    sums = jnp.concatenate([sums_one, sums_two], axis=0)
    return finish(plan, grads, sums, masters, firsts, seconds, *output, *input_grad)


def solution(mesh):
    plan = Plan(mesh, None)
    rows = P(AXES, None)
    weights = (*[rows] * 6, P(None, AXES))
    tokens = P("dp", "seq", None)
    return jax.shard_map(
        partial(on_device, plan),
        mesh=mesh,
        in_specs=(tokens, P("dp", None), P("dp", None), tokens, *weights * 3),
        out_specs=(tokens, tokens, P(), *weights * 3),
        check_vma=False,
    )
```

```python
from functools import partial

import jax
import jax.numpy as jnp
from jax import lax
from jax.experimental import pallas as pl
from jax.experimental.pallas import tpu as pltpu
from jax.sharding import PartitionSpec as P

D = 768
H = 12
HD = 64
FF = 3072
STEP = 7
HALF = D // 2
PAIRS = H // 2
BLOCKS = 4
BF = jnp.bfloat16
F32 = jnp.float32
AXES = ("dp", "seq")
clip_limit = 1.0
MIB = 2**20

VM = pl.BlockSpec(memory_space=pltpu.VMEM)
ANY = pl.BlockSpec(memory_space=pl.ANY)
FAR = pl.BlockSpec(memory_space=pltpu.HBM)


def dot(left, right, left_dim, right_dim):
    return lax.dot_general(
        left, right, (((left_dim,), (right_dim,)), ((), ())), preferred_element_type=F32
    )


def shape(dims, kind):
    return jax.ShapeDtypeStruct(dims, kind)


class Plan:
    def __init__(self, mesh, rows_each):
        self.dp = mesh.shape["dp"]
        self.seq = mesh.shape["seq"]
        self.count = self.dp * self.seq
        self.fast = (
            self.seq == 4
            and self.dp % 2 == 0
            and BLOCKS * 8 == self.count
            and (2 * D // self.count) % 16 == 0
        )
        self.nz = self.dp // 2
        self.rows = D // self.count
        self.far = FF // self.count
        both = range(self.count)
        self.core = [(d, d ^ 1) for d in both]
        self.first = [(d, d ^ (2 if d % 2 == 0 else 4)) for d in both]
        self.second = [(d, d ^ (4 if d % 2 == 0 else 2)) for d in both]
        self.groups = [list(range(low, self.dp, 2)) for low in range(2)]

    def wide(self, rows, columns):
        if self.fast:
            return (self.nz, 4, 2 * rows // self.count, columns)
        return (BLOCKS, 1, rows // BLOCKS, columns)

    def parts(self):
        return 8 if self.fast else 1

    def grads(self, rows, columns):
        if self.fast:
            half = shape((4, self.nz, rows // self.count, columns), BF)
            return [half, half]
        return [shape((rows, columns), BF)]

    def outs(self):
        return 2 if self.fast else 1

    def bands(self):
        return self.seq if self.fast else 1

    def band_shapes(self, length):
        return [shape((length // self.bands(), D), BF)] * self.bands()


def place():
    seq = lax.axis_index("seq")
    return seq & 1, seq >> 1, lax.axis_index("dp") & 1


def start_parts(plan, parts, whole, sems, pieces, blocks=None):
    blocks = slice(None) if blocks is None else pl.ds(blocks[0], len(blocks))
    for index, (first, size, to) in enumerate(pieces):
        columns = pl.ds(first, size)
        if len(parts) == 1:
            for half in range(2):
                pltpu.make_async_copy(
                    parts[0].at[half, blocks, :, :, columns], whole.at[..., pl.ds(to + half * size, size)], sems.at[index]
                ).start()
            continue
        core, mine_x, mine_y = place()
        for number, part in enumerate(parts):
            owner = core if number < 4 else 1 - core
            one, two = (number >> 1) & 1, number & 1
            off_x = jnp.where(owner == 0, one, two)
            off_y = jnp.where(owner == 0, two, one)
            spot = (mine_y ^ off_y) * 2 + (mine_x ^ off_x)
            target = pl.ds(pl.multiple_of(to + owner * size, 128), size)
            pltpu.make_async_copy(part.at[blocks, :, columns], whole.at[:, spot, :, target], sems.at[index]).start()


def wait_part(whole, sems, index, piece):
    view = whole.at[..., pl.ds(piece[2], 2 * piece[1])]
    pltpu.make_async_copy(view, view, sems.at[index]).wait()


def band(plan, number, length):
    if plan.bands() == 1:
        return pl.ds(0, length)
    size = length // plan.bands()
    return pl.ds(pl.multiple_of((lax.axis_index("seq") ^ number) * size, size), size)


def load_bands(plan, refs, whole, sems):
    copies = []
    for number, ref in enumerate(refs):
        source = ref.at[lax.axis_index("seq")] if number == 0 and plan.bands() > 1 else ref
        target = whole.at[band(plan, number, whole.shape[0]), :]
        copies.append(pltpu.make_async_copy(source, target, sems.at[number]))
    for copy in copies:
        copy.start()
    return copies


def flat(value):
    return value.reshape(-1, value.shape[-1])


def held_grad(plan, rows, columns):
    one = plan.grads(rows, columns)
    return pltpu.VMEM((len(one), *one[0].shape), BF)


def put_grad(held, outs, sems, held_view, out_view):
    copies = [
        pltpu.make_async_copy(held.at[(i, *held_view)], out.at[out_view], sems.at[i]) for i, out in enumerate(outs)
    ]
    for copy in copies:
        copy.start()
    return copies


def store_grad(plan, tile, held, rows, first_row, columns):
    if not plan.fast:
        held[0, pl.ds(first_row, tile.shape[0]), columns] = tile.astype(BF)
        return
    core, mine_x, mine_y = place()
    step = rows // plan.count

    def spot(pair, owner):
        off_x = (pair & 1) ^ mine_x
        off_y = ((pair >> 1) & 1) ^ mine_y
        return (off_x * 2 + off_y if owner == 0 else off_y * 2 + off_x), pair >> 2

    for local in range(tile.shape[0] // (2 * step)):
        pair = first_row // (2 * step) + local
        low = tile[2 * step * local : 2 * step * local + step]
        high = tile[2 * step * local + step : 2 * step * (local + 1)]
        held[core, *spot(pair, 0), :, columns] = low.astype(BF)
        held[1 - core, *spot(pair, 1), :, columns] = high.astype(BF)


class Io:
    def __init__(self, ins, outs, held_in, held_out, in_sems, out_sems):
        self.loads, self.running = {}, []
        for number, (index, ref, cut) in enumerate(ins):
            source = ref if cut is None else ref.at[:, pl.ds(*cut)]
            self.loads[index] = pltpu.make_async_copy(source, held_in[number], in_sems.at[number])
        self.outs = {
            index: (held_out[number], ref, out_sems.at[number]) for number, (index, ref) in enumerate(outs)
        }
        self.shipped = []

    def start(self, *indices):
        for index in indices or [i for i in self.loads if i not in self.running]:
            self.loads[index].start()
            self.running.append(index)

    def need(self, *indices):
        for index in indices:
            self.loads.pop(index).wait()

    def ship(self, index, columns=None):
        held, ref, sem = self.outs[index]
        if columns is None:
            pltpu.make_async_copy(held, ref, sem).start()
        else:
            pltpu.make_async_copy(held.at[..., columns], ref.at[..., columns], sem).start()
        if index not in self.shipped:
            self.shipped.append(index)

    def finish(self):
        self.need(*list(self.loads))
        for index in self.outs:
            if index not in self.shipped:
                self.ship(index)
        for held, ref, sem in self.outs.values():
            pltpu.make_async_copy(held, ref, sem).wait()


def call(name, body, ins, outs, scratch, limit, cost=10**11, aliases=None):
    staged_in = [i for i, item in enumerate(ins) if item[1] == "far"]
    staged_out = [i for i, item in enumerate(outs) if item[1] == "far"]
    cuts = {i: (ins[i][2] if len(ins[i]) > 2 else None) for i in staged_in}

    def held_shape(i):
        array = ins[i][0]
        dims = array.shape if cuts[i] is None else (array.shape[0], cuts[i][1])
        return pltpu.VMEM(dims, array.dtype)

    specs = {"near": VM, "far": FAR, "raw": FAR, "any": ANY}
    n_in, n_out, n_scratch = len(ins), len(outs), len(scratch)

    def kernel(*refs):
        in_refs, refs = list(refs[:n_in]), refs[n_in:]
        out_refs, refs = list(refs[:n_out]), refs[n_out:]
        own, refs = refs[:n_scratch], refs[n_scratch:]
        held_in, refs = refs[: len(staged_in)], refs[len(staged_in) :]
        held_out, refs = refs[: len(staged_out)], refs[len(staged_out) :]
        in_sems, out_sems = refs
        io = Io(
            [(i, in_refs[i], cuts[i]) for i in staged_in],
            [(i, out_refs[i]) for i in staged_out],
            held_in, held_out, in_sems, out_sems,
        )
        for number, i in enumerate(staged_in):
            in_refs[i] = held_in[number]
        for number, i in enumerate(staged_out):
            out_refs[i] = held_out[number]
        body(io, in_refs, out_refs, *own)
        io.finish()

    args = [
        pltpu.with_memory_space_constraint(item[0], pltpu.HBM) if item[1] in ("far", "raw") else item[0]
        for item in ins
    ]
    return pl.pallas_call(
        kernel,
        out_shape=[pltpu.HBM(o.shape, o.dtype) if kind in ("far", "raw") else o for o, kind in outs],
        in_specs=[specs[item[1]] for item in ins],
        out_specs=[specs[kind] for _, kind in outs],
        scratch_shapes=[
            *scratch,
            *[held_shape(i) for i in staged_in],
            *[pltpu.VMEM(outs[i][0].shape, outs[i][0].dtype) for i in staged_out],
            pltpu.SemaphoreType.DMA((max(1, len(staged_in)),)),
            pltpu.SemaphoreType.DMA((max(1, len(staged_out)),)),
        ],
        input_output_aliases=aliases or {},
        compiler_params=pltpu.CompilerParams(vmem_limit_bytes=limit * MIB),
        cost_estimate=pl.CostEstimate(flops=cost, bytes_accessed=1, transcendentals=0),
        name=name,
    )(*args)


def far(*arrays):
    return [(array, "far") for array in arrays]


def norm_of(values):
    center = values - jnp.mean(values, axis=-1, keepdims=True)
    inverse = lax.rsqrt(jnp.mean(center * center, axis=-1, keepdims=True) + 1e-05)
    return center * inverse, inverse


def norm_back(upstream, normed, inverse, gain):
    scaled = upstream * gain
    return inverse * (
        scaled
        - jnp.mean(scaled, axis=-1, keepdims=True)
        - normed * jnp.mean(scaled * normed, axis=-1, keepdims=True)
    )


def fill_bias(plan, bias, seg_ref, pad_ref):
    length = bias.shape[0]
    row = pl.ds(lax.axis_index("seq"), 1)
    seg, pad = seg_ref[row, :], pad_ref[row, :]
    code = (2 * seg + pad).astype(F32)
    wanted = (2 * seg + 1).astype(F32)
    coded = jnp.broadcast_to(code, (length, length)).T
    rows = lax.broadcasted_iota(jnp.int32, (length, length), 0)
    cols = lax.broadcasted_iota(jnp.int32, (length, length), 1)
    bias[...] = jnp.where((coded == wanted) | (rows == cols), 0.0, -1e30)


def halves_of(values):
    lane = lax.broadcasted_iota(jnp.int32, values.shape, 1)
    zero = jnp.zeros_like(values)
    return jnp.where(lane < HD, values, zero), jnp.where(lane < HD, zero, values)


def prepare(plan, matrices, norm_params):
    groups = [matrices[0:3], matrices[3:5], matrices[5:6]]

    def body(io, ins, outs):
        io.start()
        core = lax.axis_index("seq") & 1
        first = 0
        rows = norm_params.shape[1]
        same = lax.broadcasted_iota(jnp.int32, (rows, rows), 0) == lax.broadcasted_iota(jnp.int32, (rows, rows), 1)
        lane = lax.broadcasted_iota(jnp.int32, (rows, 128), 1)
        side = jnp.zeros((rows, 128), F32)
        for p in range(norm_params.shape[0]):
            row = jnp.broadcast_to(ins[-1][p : p + 1, :], (rows, rows))
            column = jnp.sum(jnp.where(same, row, 0.0), axis=1, keepdims=True)
            side = jnp.where(lane == p, column, side)
        for out in outs[:2]:
            out[:, 3 * HALF :] = side.astype(BF)
        for number, group in enumerate(groups):
            at = 0
            for index in range(first, first + len(group)):
                io.need(index)
                size = ins[index].shape[1] // 2
                left, right = ins[index][:, :size], ins[index][:, size:]
                mine = jnp.where(core == 0, left, right).astype(BF)
                other = jnp.where(core == 0, right, left).astype(BF)
                outs[2 * number][:, at : at + size] = mine
                outs[2 * number + 1][:, at : at + size] = other
                at += size
            first += len(group)

    outs = []
    for group in groups:
        width = sum(w.shape[1] for w in group) // 2 + (128 if group is groups[0] else 0)
        outs += [(shape((group[0].shape[0], width), BF), "near")] * 2
    flat_outs = call("prepare", body, [*far(*matrices), (norm_params, "near")], outs, [], 8)
    return flat_outs[0:2], flat_outs[2:4], flat_outs[4:6]


def other_rows(plan, arrays):
    others = plan.seq - 1

    def body(io, ins, outs, held, in_sems, out_sems):
        mine = lax.axis_index("seq")
        loads = [
            pltpu.make_async_copy(ins[i // others].at[mine ^ (i % others + 1)], held.at[i], in_sems.at[i])
            for i in range(len(outs))
        ]
        for load in loads:
            load.start()
        puts = [pltpu.make_async_copy(held.at[i], outs[i], out_sems.at[i]) for i in range(len(outs))]
        for load, put in zip(loads, puts):
            load.wait()
            put.start()
        for put in puts:
            put.wait()

    part = arrays[0].shape[1:]
    count = others * len(arrays)
    outs = call(
        "other_rows", body, [(a, "raw") for a in arrays], [(shape(part, BF), "raw")] * count,
        [pltpu.VMEM((count, *part), BF), pltpu.SemaphoreType.DMA((count,)), pltpu.SemaphoreType.DMA((count,))],
        8,
    )
    return [outs[i * others : (i + 1) * others] for i in range(len(arrays))]


def row_blocks(length):
    for i in range(length // 128):
        yield slice(i * 128, (i + 1) * 128)


def project(plan, tokens, parts):
    length = tokens[0].size // D if len(tokens) == 1 else tokens[1].shape[0] * len(tokens)
    width = 3 * D + 256
    pieces = [(3 * HALF, 128, 3 * D), *[(m * HALF, HALF, m * D) for m in range(3)]]

    def body(io, ins, outs, whole, rows_in, sems, put_sems):
        h_ref, q_ref, k_ref, v_ref, n_ref, w_ref, x_ref = outs
        start_parts(plan, ins[len(tokens) :], whole, sems, pieces)
        loads = load_bands(plan, ins[: len(tokens)], rows_in, sems.at[pl.ds(4, len(tokens))])
        wait_part(whole, sems, 0, pieces[0])
        norms = flat(whole[:, :, :, 3 * D : 3 * D + 128]).astype(F32).T[0:8]
        n_ref[...] = norms
        for load in loads:
            load.wait()
        puts = [pltpu.make_async_copy(rows_in, x_ref, put_sems.at[1])]
        puts[0].start()
        for rows in row_blocks(length):
            normed, _ = norm_of(rows_in[rows, :].astype(F32))
            h_ref[rows, :] = (normed * norms[0:1, :] + norms[1:2, :]).astype(BF)
        io.ship(0)
        for m in range(3):
            wait_part(whole, sems, 1 + m, pieces[1 + m])
        puts.append(pltpu.make_async_copy(whole, w_ref, put_sems.at[0]))
        puts[1].start()
        for m, (out, scale) in enumerate(((q_ref, 0.125), (k_ref, 1.0), (v_ref, 1.0))):
            weight = flat(whole[:, :, :, m * D : (m + 1) * D])
            out[...] = (dot(h_ref[...], weight, 1, 0) * scale).astype(BF)
            io.ship(1 + m)
        for put in puts:
            put.wait()

    act = shape((length, D), BF)
    wide = plan.wide(D, width)
    return call(
        "project", body, [*[(t, "any") for t in tokens], *[(p, "any") for p in parts]],
        [*[(act, "far")] * 4, (shape((8, D), F32), "near"), (shape(wide, BF), "raw"), (act, "raw")],
        [
            pltpu.VMEM(wide, BF), pltpu.VMEM((length, D), BF),
            pltpu.SemaphoreType.DMA((4 + len(tokens),)), pltpu.SemaphoreType.DMA((2,)),
        ],
        20, 1,
    )


def mix(plan, query, key, value, seg, pad):
    length = query.shape[0]

    def body(io, ins, outs, bias):
        q_ref, k_ref, v_ref, seg_ref, pad_ref = ins
        at_ref, a_ref, l_ref = outs
        io.start()
        fill_bias(plan, bias, seg_ref, pad_ref)
        io.need(0, 1, 2)

        @pl.loop(0, PAIRS, unroll=True)
        def _(p):
            cols = pl.ds(pl.multiple_of(p * 128, 128), 128)
            keys = k_ref[:, cols]
            turned = v_ref[:, cols].T
            for half, query in enumerate(halves_of(q_ref[:, cols])):
                scores = dot(keys, query, 1, 1) + bias[...]
                top = jnp.max(scores, axis=0, keepdims=True)
                lifted = jnp.exp(scores - top)
                total = jnp.sum(lifted, axis=0, keepdims=True)
                soft = (lifted * (1.0 / total)).astype(BF)
                mixed = dot(turned[half * HD : (half + 1) * HD], soft, 1, 0)
                at_ref[pl.ds(pl.multiple_of(p * 128 + half * HD, HD), HD), :] = mixed.astype(BF)
                l_ref[pl.ds(2 * p + half, 1), :] = top + jnp.log(total)
            a_ref[:, cols] = at_ref[pl.ds(pl.multiple_of(p * 128, 128), 128), :].T

    return call(
        "mix", body, [*far(query, key, value), (seg, "near"), (pad, "near")],
        [(shape((D, length), BF), "far"), (shape((length, D), BF), "far"), (shape((H, length), F32), "far")],
        [pltpu.VMEM((length, length), F32)],
        14,
    )


def widen(plan, tokens, mixed, norms, parts):
    length = tokens.shape[0]
    pieces = [(0, HALF, 0), (HALF, 2 * D, D)]

    def body(io, ins, outs, whole, sems, put_sems):
        x_ref, a_ref, n_ref, *part_refs = ins
        m_ref, h_ref, z_ref, s_ref, w_ref = outs
        io.start(1)
        start_parts(plan, part_refs, whole, sems, pieces[:1])
        io.start(0)
        start_parts(plan, part_refs, whole, sems.at[pl.ds(1, 1)], pieces[1:])
        io.need(0, 1)
        wait_part(whole, sems, 0, pieces[0])
        m_ref[...] = x_ref[...].astype(F32) + dot(a_ref[...], flat(whole[:, :, :, 0:D]), 1, 0)
        io.ship(0)
        for rows in row_blocks(length):
            normed, _ = norm_of(m_ref[rows, :])
            h_ref[rows, :] = (normed * n_ref[2:3, :] + n_ref[3:4, :]).astype(BF)
        io.ship(1)
        wait_part(whole, sems, 1, pieces[1])
        put = pltpu.make_async_copy(whole, w_ref, put_sems.at[0])
        put.start()
        for block in range(BLOCKS):
            cols = slice(block * D, (block + 1) * D)
            up = dot(h_ref[...], flat(whole[:, :, :, (block + 1) * D : (block + 2) * D]), 1, 0)
            bell = 0.5 + 0.5 * lax.erf(up * 0.7071067811865476)
            z_ref[:, cols] = (up * bell).astype(BF)
            s_ref[:, cols] = (bell + up * (jnp.exp(-0.5 * up * up) * 0.3989422804014327)).astype(BF)
            io.ship(2, pl.ds(block * D, D))
            io.ship(3, pl.ds(block * D, D))
        put.wait()

    act = shape((length, D), BF)
    wide = plan.wide(D, D + FF)
    hidden = shape((length, FF), BF)
    outs = [shape((length, D), F32), act, hidden, hidden]
    return call(
        "widen", body, [*far(tokens, mixed), (norms, "near"), *[(p, "any") for p in parts]],
        [*[(o, "far") for o in outs], (shape(wide, BF), "raw")],
        [pltpu.VMEM(wide, BF), pltpu.SemaphoreType.DMA((2,)), pltpu.SemaphoreType.DMA((1,))],
        28,
    )


def grad_of_down(plan, hidden, cot):
    length = hidden.shape[0]

    def body(io, ins, outs, g_in, z_in, sems, z_sems, put_sems, g_sem, held):
        z_ref, *bands = ins
        *grads, g_out = outs
        loads = load_bands(plan, bands, g_in, sems)
        z_loads = [
            pltpu.make_async_copy(z_ref.at[:, pl.ds(i * D, D)], z_in.at[:, pl.ds(i * D, D)], z_sems.at[i])
            for i in range(BLOCKS)
        ]
        for load in z_loads:
            load.start()
        for load in loads:
            load.wait()
        puts = [pltpu.make_async_copy(g_in, g_out, g_sem.at[0])]
        puts[0].start()
        for block in range(BLOCKS):
            z_loads[block].wait()
            tile = dot(z_in[:, block * D : (block + 1) * D], g_in[...], 0, 0)
            store_grad(plan, tile, held, FF, block * D, slice(None))
            view = (slice(None), pl.ds(block, 1)) if plan.fast else (pl.ds(block * D, D),)
            puts += put_grad(held, grads, put_sems.at[block], view, view)
        for put in puts:
            put.wait()

    act = shape((length, D), BF)
    grads = plan.grads(FF, D)
    return call(
        "grad_of_down", body, [(hidden, "raw"), *[(c, "any") for c in cot]],
        [*[(g, "raw") for g in grads], (act, "raw")],
        [
            pltpu.VMEM((length, D), BF), pltpu.VMEM((length, FF), BF),
            pltpu.SemaphoreType.DMA((len(cot),)), pltpu.SemaphoreType.DMA((BLOCKS,)),
            pltpu.SemaphoreType.DMA((BLOCKS, len(grads))), pltpu.SemaphoreType.DMA((1,)),
            held_grad(plan, FF, D),
        ],
        28,
    )


def narrow(plan, blocks, mid, below, grads, low, hidden, slope, cot, whole_ou, parts_down):
    length = mid.shape[0]
    count = len(blocks)
    start, final = blocks[0] == 0, blocks[-1] == BLOCKS - 1
    cut = (blocks[0] * D, count * D)
    n_out = plan.outs()

    def body(io, ins, outs, *scratch):
        m_ref, h_ref, z_ref, s_ref, g_ref, up_ref, *rest = ins
        downs = rest[: len(parts_down)]
        b_ref, *grad_refs = outs[: 1 + n_out]
        o_refs = outs[1 + n_out :]
        held, du_ref, acc, whole_up, whole_down, sems, put_sems = scratch
        copies = []
        down = (0, HALF, 0)
        io.start(4)
        start_parts(plan, downs, whole_down, sems.at[pl.ds(0, 1)], [down], blocks)
        io.start(3, 1)
        up = pltpu.make_async_copy(up_ref.at[..., pl.ds(D + cut[0], cut[1])], whole_up, sems.at[1])
        up.start()
        io.start()
        io.need(4)
        wait_part(whole_down, sems, 0, down)
        io.need(3, 1)
        for number, block in enumerate(blocks):
            local = slice(number * D, (number + 1) * D)
            back = dot(g_ref[...], flat(whole_down[number]), 1, 1)
            du_ref[:, local] = (back * s_ref[:, local]).astype(BF)
            tile = dot(h_ref[...], du_ref[:, local], 0, 0)
            store_grad(plan, tile, held, D, 0, local)
            views = [(*[slice(None)] * (plan.grads(D, D)[0].ndim - 1), pl.ds(at * D, D)) for at in (number, block)]
            copies += put_grad(held, grad_refs, put_sems.at[number], *views)
        up.wait()
        lower = dot(du_ref[...], flat(whole_up[...]), 1, 1)
        if start:
            b_ref[...] = lower
        else:
            io.need(6 + len(parts_down))
            b_ref[...] = rest[len(parts_down)][...] + lower
        io.ship(0)
        io.need(0, 2)
        gain = m_ref[...] + dot(z_ref[...], whole_down[...].reshape(count * D, D), 1, 0)
        if final:
            acc[...] = gain
            for number, o_ref in enumerate(o_refs):
                o_ref[...] = acc[band(plan, number, length), :].astype(BF)
        else:
            o_refs[0][...] = gain
        for copy in copies:
            copy.wait()

    deep = plan.wide(FF, D)
    ins = [
        *far(mid, low), (hidden, "far", cut), (slope, "far", cut), *far(cot), (whole_ou, "raw"),
        *[(p, "any") for p in parts_down],
    ]
    aliases = {}
    if not start:
        ins += far(below)
        aliases = {len(ins) + i: 1 + i for i in range(n_out)}
        ins += [(g, "raw") for g in grads]
    return call(
        "narrow" + str(blocks[0]), body, ins,
        [
            (shape((length, D), F32), "far"), *[(g, "raw") for g in plan.grads(D, FF)],
            *[(o, "far") for o in (plan.band_shapes(length) if final else [shape((length, D), F32)])],
        ],
        [
            held_grad(plan, D, count * D),
            pltpu.VMEM((length, count * D), BF),
            pltpu.VMEM((length, D), F32),
            pltpu.VMEM(plan.wide(D, count * D), BF),
            pltpu.VMEM((count, *deep[1:]), BF),
            pltpu.SemaphoreType.DMA((2,)),
            pltpu.SemaphoreType.DMA((count, n_out)),
        ],
        40, aliases=aliases,
    )


def turn(plan, mid, back, cot, norms, whole_ou):
    length = mid.shape[0]

    def body(io, ins, outs, whole, sems):
        m_ref, b_ref, g_ref, n_ref, w_ref = ins
        x_ref, low, d_ref, s_ref = outs
        io.start()
        load = pltpu.make_async_copy(w_ref.at[..., pl.ds(0, D)], whole, sems.at[0])
        load.start()
        s_ref[...] = jnp.zeros_like(s_ref)
        io.need(0, 1, 2)
        for rows in row_blocks(length):
            normed, inverse = norm_of(m_ref[rows, :])
            upstream = b_ref[rows, :]
            total = g_ref[rows, :].astype(F32) + norm_back(upstream, normed, inverse, n_ref[2:3, :])
            x_ref[rows, :] = total
            low[rows, :] = total.astype(BF)
            s_ref[0:1, :] += jnp.sum(upstream * normed, axis=0, keepdims=True)
            s_ref[1:2, :] += jnp.sum(upstream, axis=0, keepdims=True)
        io.ship(0)
        io.ship(1)
        load.wait()
        d_ref[...] = dot(low[...], flat(whole[...]), 1, 1).astype(BF)

    act = shape((length, D), BF)
    return call(
        "turn", body, [*far(mid, back, cot), (norms, "near"), (whole_ou, "raw")],
        [(shape((length, D), F32), "far"), (act, "far"), (act, "far"), (shape((2, D), F32), "near")],
        [pltpu.VMEM(plan.wide(D, D), BF), pltpu.SemaphoreType.DMA((1,))],
        24,
    )


def attend_back(plan, side, low, query, key, value, lse, cot, seg, pad, extra=()):
    length = low.shape[0]
    width = 3 * HALF + (D if extra else 0)
    cut = (side * HALF, HALF)

    def body(io, ins, outs, bias, held, put_sems):
        h_ref, q_ref, k_ref, v_ref, c_ref, l_ref, seg_ref, pad_ref, *more = ins
        d_ref, *grads = outs
        io.start(1, 2, 3, 4, 5)
        io.start()
        fill_bias(plan, bias, seg_ref, pad_ref)
        io.need(1, 2, 3, 4, 5)

        @pl.loop(0, PAIRS // 2)
        def _(local):
            p = local + side * (PAIRS // 2)
            first = pl.multiple_of(local * 128, 128)
            cols = pl.ds(first, 128)
            keys, values = k_ref[:, cols], v_ref[:, cols]
            turned = keys.T
            queries, cots = halves_of(q_ref[:, cols]), halves_of(c_ref[:, cols])
            dv = dk = None
            dqs = []
            for half in range(2):
                scores = dot(keys, queries[half], 1, 1) + bias[...]
                soft = jnp.exp(scores - l_ref[pl.ds(2 * p + half, 1), :])
                gain = dot(soft.astype(BF), cots[half], 1, 0)
                dv = gain if dv is None else dv + gain
                dp = dot(values, cots[half], 1, 1)
                share = jnp.sum(soft * dp, axis=0, keepdims=True)
                ds = (soft * (dp - share)).astype(BF)
                gain = dot(ds, queries[half], 1, 0)
                dk = gain if dk is None else dk + gain
                dqs.append(dot(turned[half * HD : (half + 1) * HD], ds, 1, 0) * 0.125)
            d_ref[:, cols] = jnp.concatenate(dqs, axis=0).T.astype(BF)
            d_ref[:, pl.ds(first + HALF, 128)] = dk.astype(BF)
            d_ref[:, pl.ds(first + 2 * HALF, 128)] = dv.astype(BF)

        io.ship(0)
        io.need(0)
        lead, copies = [slice(None)] * (len(grads[0].shape) - 1), []
        if extra:
            io.need(8, 9)
            tile = dot(more[0][...], more[1][...], 1, 0)
            store_grad(plan, tile, held, D, 0, slice(3 * HALF, width))
            view = (*lead, pl.ds(3 * HALF, D))
            copies += put_grad(held, grads, put_sems.at[3], view, view)
        cols = slice(0, 3 * HALF)
        store_grad(plan, dot(h_ref[...], d_ref[...], 0, 0), held, D, 0, cols)
        view = (*lead, pl.ds(0, 3 * HALF))
        copies += put_grad(held, grads, put_sems.at[0], view, view)
        for copy in copies:
            copy.wait()

    return call(
        "attend_back" + str(side), body,
        [
            *far(low), *[(a, "far", cut) for a in (query, key, value, cot)], *far(lse),
            (seg, "near"), (pad, "near"), *far(*extra),
        ],
        [(shape((length, 3 * HALF), BF), "far"), *[(g, "raw") for g in plan.grads(D, width)]],
        [
            pltpu.VMEM((length, length), F32), held_grad(plan, D, width),
            pltpu.SemaphoreType.DMA((4, plan.outs())),
        ],
        26,
    )


def finish_tokens(plan, tokens, spreads, mid_cot, norms, whole_qkv):
    length = tokens.shape[0]

    def body(io, ins, outs, back, whole, sems):
        x_ref, d0_ref, d1_ref, c_ref, n_ref, w_ref = ins
        *o_refs, s_ref = outs
        io.start(1, 2)
        load = pltpu.make_async_copy(w_ref.at[..., pl.ds(0, 3 * D)], whole, sems.at[0])
        load.start()
        io.start()
        s_ref[...] = jnp.zeros_like(s_ref)
        io.need(1, 2)
        load.wait()
        back[...] = sum(
            dot(
                jnp.concatenate([d[:, m * HALF : (m + 1) * HALF] for d in (d0_ref, d1_ref)], axis=1),
                flat(whole[:, :, :, m * D : (m + 1) * D]), 1, 1,
            )
            for m in range(3)
        )
        io.need(0, 3)
        for rows in row_blocks(length):
            normed, inverse = norm_of(x_ref[rows, :].astype(F32))
            upstream = back[rows, :]
            c_ref[rows, :] += norm_back(upstream, normed, inverse, n_ref[0:1, :])
            s_ref[0:1, :] += jnp.sum(upstream * normed, axis=0, keepdims=True)
            s_ref[1:2, :] += jnp.sum(upstream, axis=0, keepdims=True)
        for number, o_ref in enumerate(o_refs):
            o_ref[...] = c_ref[band(plan, number, length), :].astype(BF)

    return call(
        "finish_tokens", body, [*far(tokens, *spreads, mid_cot), (norms, "near"), (whole_qkv, "raw")],
        [*[(o, "far") for o in plan.band_shapes(length)], (shape((2, D), F32), "near")],
        [pltpu.VMEM((length, D), F32), pltpu.VMEM(plan.wide(D, 3 * D), BF), pltpu.SemaphoreType.DMA((1,))],
        20, 1,
    )


def sum_up(plan, blocks, others, slices):
    nz, rows, columns = blocks.shape
    wide = 4 * D // plan.count

    def body(io, ins, outs, held, sems):
        blocks_ref, others_ref, slice_ref = ins
        g_ref, card_ref = outs
        loads = [pltpu.make_async_copy(blocks_ref.at[i], held.at[i], sems.at[i]) for i in range(nz)]
        for load in loads:
            load.start()
        for load in loads:
            load.wait()
        value = jnp.sum(held[...].astype(F32), axis=0)
        g_ref[...] = value
        left = jnp.sum(jnp.sum(value * value, axis=0, keepdims=True), axis=1, keepdims=True) + others_ref[0:1, 0:1]
        lane = lax.broadcasted_iota(jnp.int32, slice_ref.shape, 1)
        card = slice_ref[...]
        for i in range(3):
            piece = left.astype(BF).astype(F32)
            card = jnp.where(lane == wide + i, piece, card)
            left = left - piece
        card = card.astype(BF)
        for i in range(plan.count):
            card_ref[i] = card

    return call(
        "sum_up", body, [(blocks, "any"), (others, "near"), (slices, "near")],
        [(shape((rows, columns), F32), "near"), (shape((plan.count, *slices.shape), BF), "near")],
        [pltpu.VMEM(blocks.shape, BF), pltpu.SemaphoreType.DMA((nz,))], 8,
    )


def update(plan, grads, cards, masters, firsts, seconds, passed):
    rates = [D**-0.5] * 3 + [4.0 * D**-0.5, D**-0.5, FF**-0.5, 0.2]
    decays = [0.01] * 6 + [0.0]
    count = len(masters)
    given = len(grads)

    def body(io, ins, outs, total, sems):
        grad_refs, card_ref = ins[:given], ins[given]
        first = given + 1
        io.start(*(first + k * count + i for i in reversed(range(count)) for k in range(3)))
        io.start()
        sources, rows, _ = card_ref.shape
        split = min(2, sources)
        for c in range(split):
            cards_c = [card_ref[i].astype(F32) for i in range(c, sources, split)]
            total[c * rows : (c + 1) * rows, :] = sum(cards_c[1:], cards_c[0])
        wide = 4 * D // plan.count
        all_norms = total[...]
        lane = lax.broadcasted_iota(jnp.int32, all_norms.shape, 1)
        own = jnp.where(lane < wide, all_norms * all_norms, all_norms * (1.0 / rows))
        square = jnp.sum(jnp.sum(own, axis=0, keepdims=True), axis=1, keepdims=True)
        norm = jnp.sqrt(square)
        outs[0][...] = jnp.broadcast_to(norm, outs[0].shape)
        factor = jnp.minimum(1.0, clip_limit / (norm + 1e-06))
        place_of = lax.axis_index("dp") * plan.seq + lax.axis_index("seq")
        if split == 2:
            place_of = (place_of & 1) * rows + (place_of >> 1)
        mine = total[pl.ds(place_of, 1), :]
        each = wide // 4
        grad_norms = jnp.concatenate([mine[:, p * each : (p + 1) * each] for p in range(4)], axis=0)
        for i in reversed(range(count)):
            w_ref, m_ref, s_ref = (ins[first + k * count + i] for k in range(3))
            io.need(*(first + k * count + i for k in range(3)))
            if i < 3:
                cols = [
                    (slice(h * HALF, (h + 1) * HALF), grad_refs[0][:, (5 * h + i) * HALF : (5 * h + i + 1) * HALF])
                    for h in range(2)
                ]
            elif i == 3:
                cols = [(slice(None), grad_refs[0][:, 3 * HALF : 5 * HALF])]
            elif i < 6:
                cols = [(slice(None), grad_refs[i - 3][...])]
            else:
                cols = [(slice(None), grad_norms)]
            for where, grad in cols:
                clipped = factor * grad
                one = 0.5 * m_ref[:, where] + 0.5 * clipped
                two = 0.55 * s_ref[:, where] + 0.45 * clipped * clipped
                root = jnp.sqrt(two * (1.0 / (1.0 - 0.55**STEP))) + 1e-08
                weight = w_ref[:, where]
                step = (one * (1.0 / (1.0 - 0.5**STEP))) / root + decays[i] * weight
                outs[1 + i][:, where] = weight - rates[i] * step
                outs[1 + count + i][:, where] = one
                outs[1 + 2 * count + i][:, where] = two
            for k in range(3):
                io.ship(1 + k * count + i)
        last = first + 3 * count
        copies = []
        for number in range(len(passed)):
            which, place_in = number // plan.bands(), number % plan.bands()
            io.need(last + number)
            target = outs[1 + 3 * count + which]
            if plan.bands() > 1:
                target = target.at[lax.axis_index("seq") ^ place_in]
            copies.append(pltpu.make_async_copy(ins[last + number], target, sems.at[number]))
            copies[-1].start()
        for copy in copies:
            copy.wait()

    like = [(shape(w.shape, F32), "far") for w in masters] * 3
    pieces = [shape((plan.bands(), *p.shape), BF) if plan.bands() > 1 else p for p in passed[:: plan.bands()]]
    return call(
        "update", body, [*[(g, "near") for g in grads], (cards, "near"), *far(*masters, *firsts, *seconds, *passed)],
        [(shape((1, 128), F32), "near"), *like, *[(o, "raw") for o in pieces]],
        [pltpu.VMEM((min(2, cards.shape[0]) * cards.shape[1], 128), F32), pltpu.SemaphoreType.DMA((len(passed),))], 20,
    )


def after(values, *others):
    return lax.optimization_barrier((values, others))[0]


def meet(*values):
    return lax.optimization_barrier(values)


def send(plan, values, perm):
    return lax.ppermute(values, AXES, perm)


def block_of(plan, mine, other):
    core = lax.axis_index("seq") & 1
    got = send(plan, other, plan.core)
    return jnp.where(core == 0, jnp.concatenate([mine, got]), jnp.concatenate([got, mine]))


def copies_of(plan, block):
    return jnp.broadcast_to(block[None], (plan.nz, *block.shape))


def along_z(plan, values):
    return lax.all_to_all(values, "dp", 0, 0, axis_index_groups=plan.groups, tiled=True)


def gather_whole(matrices):
    split = [w.reshape(w.shape[0], 2, -1) for w in matrices]
    halves = jnp.concatenate(split, axis=2).transpose(1, 0, 2).astype(BF)
    full = lax.all_gather(halves, AXES, axis=1, tiled=True)
    return [full.reshape(2, BLOCKS, 1, -1, full.shape[-1])]


def add(one, two):
    return one.astype(F32) + two.astype(F32)


def fold(keep, got):
    if keep.ndim == 4:
        keep, got = (v.reshape(-1, *v.shape[2:]) for v in (keep, got))
    size = keep.shape[0] // 2
    return add(keep[size:], got[size:]).astype(BF), add(keep[:size], got[:size]).astype(BF)


def total(blocks):
    return jnp.sum(blocks.astype(F32), axis=0)


def finish(plan, grads, sums, masters, firsts, seconds, *passed):
    wide = sums.shape[0] * D // plan.count
    slices = sums.reshape(sums.shape[0], plan.count, -1).transpose(1, 0, 2).reshape(plan.count, wide)
    slices = jnp.pad(slices, ((0, 0), (0, 128 - wide)))
    if plan.fast:
        core = lax.axis_index("seq") & 1
        pairs = slices.reshape(-1, 2, 128)
        mine, other = (lax.dynamic_index_in_dim(pairs, c, 1, keepdims=False) for c in (core, 1 - core))
        slices = mine + send(plan, other, plan.core)
        blocks, *others = grads
        left = jnp.broadcast_to(sum(jnp.sum(g * g) for g in others), (1, 128))
        left, slices, blocks, passed = meet(left, slices, blocks, passed)
        last, cards = sum_up(plan, blocks, left, slices)
        grads = [last, *others]
        cards = lax.all_to_all(cards, AXES, 0, 0, tiled=True)
    else:
        left = jnp.broadcast_to(sum(jnp.sum(g * g) for g in grads), (plan.count, 1))
        cards = lax.psum(slices + jnp.pad(left, ((0, 0), (wide, 127 - wide))), AXES)[None]
    norm, *updated, output, input_grad = update(plan, grads, cards, masters, firsts, seconds, passed)
    return (output, input_grad, norm[0, 0], *updated)


def on_device(plan, *args):
    tokens_in, segment_ids, pad_mask, out_grad = args[:4]
    masters, firsts, seconds = args[4:11], args[11:18], args[18:25]
    each, piece, _ = tokens_in.shape
    length = each // plan.seq * plan.seq * piece

    plan.fast = plan.fast and each == plan.seq

    def swap(values, number):
        return lax.ppermute(values, "seq", [(i, i ^ number) for i in range(plan.seq)])

    def to_rows(values, others=None):
        if not plan.fast:
            return [lax.all_to_all(values, "seq", 0, 0, tiled=True).reshape(length, D)]
        return [values, *[swap(other, 1 + n) for n, other in enumerate(others)]]

    def to_pieces(bands):
        if not plan.fast:
            return [lax.all_to_all(bands[0].reshape(each, piece, D), "seq", 0, 0, tiled=True)]
        return [bands[0], *[swap(other, 1 + n) for n, other in enumerate(bands[1:])]]

    seg, pad = segment_ids, pad_mask

    if not plan.fast:
        side = jnp.pad(masters[6].T, ((0, 0), (0, 124)))
        side = jnp.concatenate([side, side], axis=1)
        one, two, three = (gather_whole(m) for m in ([*masters[0:3], side], masters[3:5], masters[5:6]))
        low_one, query, key, value, norms, whole_qkv, tokens = project(plan, to_rows(tokens_in), one)
        mixed_t, mixed, lse = mix(plan, query, key, value, seg, pad)
        mid, low_two, hidden, slope, whole_ou = widen(plan, tokens, mixed, norms, two)
        *g_down, cot = grad_of_down(plan, hidden, to_rows(out_grad))
        back, *g_up, part = narrow(plan, (0, 1), mid, None, None, low_two, hidden, slope, cot, whole_ou, three)
        back, *g_up, result = narrow(plan, (2, 3), part, back, g_up, low_two, hidden, slope, cot, whole_ou, three)
        mid_cot, low_cot, mixed_cot, sums_two = turn(plan, mid, back, cot, norms, whole_ou)
        halves = [
            attend_back(plan, side, low_one, query, key, value, lse, mixed_cot, seg, pad, extra)
            for side, extra in enumerate(((mixed_t, low_cot), ()))
        ]
        stream, sums_one = finish_tokens(plan, tokens, [h[0] for h in halves], mid_cot, norms, whole_qkv)
        grads = [
            lax.psum_scatter(g.astype(F32), AXES, scatter_dimension=0, tiled=True)
            for g in (halves[0][1], halves[1][1], *g_up, *g_down)
        ]
        grads = [jnp.concatenate(grads[:2], axis=1), *grads[2:]]
        sums = jnp.concatenate([sums_one, sums_two], axis=0)
        return finish(plan, grads, sums, masters, firsts, seconds, *to_pieces([result]), *to_pieces([stream]))

    first, second, third = prepare(plan, masters[:6], masters[6])
    block = block_of(plan, *first)
    near_one = along_z(plan, copies_of(plan, block))
    others, others_cot = other_rows(plan, [after(tokens_in, block), out_grad])
    tokens = to_rows(tokens_in, others)
    block_two = block_of(plan, *second)
    spread_two = copies_of(plan, block_two)
    spread_three = copies_of(plan, block_of(plan, *third))
    near_one, tokens, spread_two, spread_three = meet(near_one, tokens, spread_two, spread_three)

    def spread(near):
        return send(plan, near, plan.second), send(plan, near, plan.first)

    def to_core(*parts):
        return [send(plan, part, plan.core) for part in parts]

    beside_one, across_one = spread(near_one)
    near_two = along_z(plan, spread_two)
    beside_one, across_one = meet(beside_one, across_one)
    corner_one = send(plan, beside_one, plan.first)
    one = [near_one, beside_one, across_one]
    one_core = to_core(*one)
    corner_one, one_core = meet(corner_one, one_core)
    one = [*one, corner_one, *one_core, *to_core(corner_one)]
    low_one, query, key, value, norms, whole_qkv, tokens = project(plan, tokens, one)
    cot = to_rows(out_grad, after(others_cot, corner_one))
    near_two, query = meet(near_two, query)
    beside_two, across_two = spread(near_two)
    spread_three, cot = meet(after(spread_three, near_two), cot)
    near_three = along_z(plan, spread_three)
    mixed_t, mixed, lse = mix(plan, query, key, value, seg, pad)
    beside_two, across_two, mixed, lse, mixed_t = meet(beside_two, across_two, mixed, lse, mixed_t)
    corner_two = send(plan, beside_two, plan.first)
    two = [near_two, beside_two, across_two]
    two_core = to_core(*two)
    corner_two, two_core, near_three = meet(corner_two, two_core, near_three)
    beside_three, across_three = spread(near_three)
    two = [*two, corner_two, *two_core, *to_core(corner_two)]
    mid, low_two, hidden, slope, whole_ou = widen(plan, tokens, mixed, norms, two)
    beside_three, across_three, hidden = meet(beside_three, across_three, hidden)
    corner_three = send(plan, beside_three, plan.first)
    three = [near_three, beside_three, across_three]
    three_core = to_core(*three)
    keep_d, go_d, cot = grad_of_down(plan, hidden, cot)
    corner_three, three_core, keep_d, go_d, cot = meet(corner_three, three_core, keep_d, go_d, cot)
    three = [*three, corner_three, *three_core, *to_core(corner_three)]

    got_d = send(plan, go_d, plan.core)
    back, *g_up, part = narrow(plan, (0, 1), mid, None, None, low_two, hidden, slope, cot, whole_ou, three)
    got_d, back, part = meet(got_d, back, part)
    go_d, keep_d = fold(keep_d, got_d)
    got_d = send(plan, go_d, plan.first)
    part = after(part, go_d)
    back, *rest = narrow(plan, (2, 3), part, back, g_up, low_two, hidden, slope, cot, whole_ou, three)
    got_d, back, rest = meet(got_d, back, rest)
    (keep_u, go_u), result = rest[:2], rest[2:]
    got_u = send(plan, go_u, plan.core)
    go_d, keep_d = fold(keep_d, got_d)
    got_d = send(plan, go_d, plan.second)
    back = after(back, go_d)
    mid_cot, low_cot, mixed_cot, sums_two = turn(plan, mid, back, cot, norms, whole_ou)
    got_u, mixed_cot, low_cot, mid_cot, result = meet(got_u, mixed_cot, low_cot, mid_cot, result)
    go_u, keep_u = fold(keep_u, got_u)
    got_d, go_u = meet(got_d, go_u)
    got_u = send(plan, go_u, plan.first)
    mixed_cot = after(mixed_cot, go_u)
    spread_a, keep_a, go_a = attend_back(
        plan, 0, low_one, query, key, value, lse, mixed_cot, seg, pad, (mixed_t, low_cot)
    )
    got_u, keep_a, spread_a = meet(got_u, keep_a, spread_a)
    got_a = send(plan, go_a, plan.core)
    block_d = add(keep_d, got_d).astype(BF)
    blocks_d = along_z(plan, block_d)
    go_u, keep_u = fold(keep_u, got_u)
    got_u = send(plan, go_u, plan.second)
    go_a, keep_a = fold(keep_a, got_a)
    got_a = send(plan, go_a, plan.first)
    mixed_cot = after(mixed_cot, go_u, go_a, block_d)
    spread_b, keep_b, go_b = attend_back(plan, 1, low_one, query, key, value, lse, mixed_cot, seg, pad)
    blocks_d, got_u, got_a, keep_b, spread_b = meet(blocks_d, got_u, got_a, keep_b, spread_b)
    got_b = send(plan, go_b, plan.core)
    block_u = add(keep_u, got_u).astype(BF)
    blocks_u = along_z(plan, block_u)
    output = to_pieces(after(result, spread_b))
    go_b, keep_b = fold(keep_b, after(got_b, block_u, output))
    got_b = send(plan, go_b, plan.first)
    go_a, keep_a = fold(keep_a, after(got_a, go_b))
    got_a = send(plan, go_a, plan.second)
    mid_cot = after(mid_cot, go_a, go_b)
    *stream, sums_one = finish_tokens(plan, tokens, [spread_a, spread_b], mid_cot, norms, whole_qkv)
    got_b, sums_one, stream = meet(got_b, sums_one, stream)
    go_b, keep_b = fold(keep_b, got_b)
    got_b = send(plan, go_b, plan.second)
    got_a = after(got_a, go_b)
    input_grad = to_pieces(after(stream, go_b))
    halves = [add(keep_a, got_a), add(keep_b, got_b)]
    blocks_ab = along_z(plan, jnp.concatenate(halves, axis=2).astype(BF))
    grads = [blocks_ab, total(blocks_u), total(blocks_d)]
    sums = jnp.concatenate([sums_one, sums_two], axis=0)
    return finish(plan, grads, sums, masters, firsts, seconds, *output, *input_grad)


def solution(mesh):
    plan = Plan(mesh, None)
    rows = P(AXES, None)
    weights = (*[rows] * 6, P(None, AXES))
    tokens = P("dp", "seq", None)
    return jax.shard_map(
        partial(on_device, plan),
        mesh=mesh,
        in_specs=(tokens, P("dp", None), P("dp", None), tokens, *weights * 3),
        out_specs=(tokens, tokens, P(), *weights * 3),
        check_vma=False,
    )
```
